128 devices in a mesh: queue: 32 (over y_lo, x, z), tensor: 4 (over y_hi, core).
Axes of the slice: x: 4, y: 4 (y_hi: 2, y_lo: 2; y = y_hi * 2 + y_lo), z: 4, core: 2. Of those that a mesh axis runs over, the one named last changes fastest.
Arguments:
- queue_latents: bfloat16 [64, 384, 3072], P('queue')
- fresh_noise: bfloat16 [2, 384, 3072], replicated, may hold values from -6 to 6
- levels: int32 [64], P('queue'), may hold values from 0 to 49, as said below
- window_start: int32 [64], P('queue'), may hold values from 0 to 61, as said below
- modulation: float32 [50, 3, 3072], replicated, may hold values from -3 to 3
- w_qkv: bfloat16 [3072, 3, 1536], P(None, None, 'tensor')
- qk_gain: float32 [2, 1536], P(None, 'tensor')
- w_out: bfloat16 [1536, 3072], P('tensor'), may hold values from -0.15625 to 0.15625
- sampler: float32 [50, 2], replicated, may hold values from 0.3 to 1
Outputs:
- advanced_queue: bfloat16 [64, 384, 3072], P('queue')
The draws below stay inside these ranges and needn't reach their ends.
Inputs may be any that keep to these rules, and one draw needn't show every extreme that they name: `levels`: level indices grow along the queue: slot f has f * 50 // 64 or one more, at most 49. The window of slot f, window_start[f] to window_start[f] + 2, contains f; for even f it starts at f - 2 or f - 1, for odd f at f - 1 or f, in each case clipped to 0 to 61.
All inputs are finite; a program needn't handle non-finite values.
Results may differ from the reference program's by a relative error of at most 0.014.
Values may be sent and summed in bfloat16 or wider, within the bound.
A program may use at most 192 MiB of HBM per device.

```python
import jax
import jax.numpy as jnp
from jax import lax

D = 3072
HEADS = 24
HDIM = 64
FT = 384
LEVELS = 50
WIN = 3
STEPS = 2
FRAMES = 64
N_TENSOR = 4


def draw_queue_latents(key, part):
    key = jax.random.fold_in(key, 1)
    base = jax.random.normal(key, (FRAMES, FT, D), jnp.float32)
    return base.astype(jnp.bfloat16)


def draw_w_qkv(key, part):
    key = jax.random.fold_in(key, 3)
    weight = jax.random.normal(key, (D, 3, HEADS * HDIM), jnp.float32) * D ** (-0.5)
    return weight.astype(jnp.bfloat16)


def gains_between(key, low, high):
    head_key, entry_key = jax.random.split(key)
    unit = jax.random.uniform(head_key, (2, HEADS, 1), jnp.float32)
    head_gain = jnp.exp(jnp.log(low) + unit * (jnp.log(high) - jnp.log(low)))
    ripple = 1.0 + 0.2 * jax.random.uniform(entry_key, (2, HEADS, HDIM), jnp.float32)
    return (head_gain * ripple).reshape(2, HEADS * HDIM)


def draw_qk_gain(key, part):
    key = jax.random.fold_in(key, 4)
    return gains_between(key, 1.0, 2.2)


def draw_levels(key, part):
    key = jax.random.fold_in(key, 5)
    slots = jnp.arange(FRAMES, dtype=jnp.int32)
    extra = jax.random.randint(key, (FRAMES,), 0, 2, jnp.int32)
    return jnp.minimum(slots * LEVELS // FRAMES + extra, LEVELS - 1).astype(jnp.int32)


def draw_window_start(key, part):
    key = jax.random.fold_in(key, 6)
    slots = jnp.arange(FRAMES, dtype=jnp.int32)
    parity = slots % 2
    back = jax.random.randint(key, (FRAMES,), 0, 2, jnp.int32)
    start = slots - 2 + parity + back
    return jnp.clip(start, 0, FRAMES - WIN).astype(jnp.int32)


def steps_of(rng, dims, cuts, low, top_value):
    def one(position, parts):
        draws = jax.random.uniform(jax.random.fold_in(jax.random.fold_in(rng, 6), position), (parts,), jnp.float32, low / len(cuts), top_value / len(cuts))
        return jnp.repeat(jnp.exp(draws), dims[position] // parts).reshape((-1,) + (1,) * (len(dims) - position - 1))

    factor_of = one(*cuts[0])
    for cut in cuts[1:]:
        factor_of = factor_of * one(*cut)
    return factor_of


def noise(key, dims, width, bound, cuts=(), kind=jnp.bfloat16):
    result = jax.random.normal(key, dims, jnp.float32) * width
    if len(cuts) > 0:
        result = steps_of(key, dims, cuts, -0.22, 0.18) * result
    return jnp.clip(result, min=-bound, max=bound).astype(kind)


def setup_inputs(seed: int = 0) -> dict:
    streams_of = jax.random.split(jax.random.key(seed), 10)
    queue_latents = draw_queue_latents(jax.random.fold_in(streams_of[9], 71), 0)
    fresh_noise = noise(streams_of[1], (STEPS, FT, D), 1.0, 6.0)
    levels = draw_levels(jax.random.fold_in(streams_of[9], 71), 0)
    window_start = draw_window_start(jax.random.fold_in(streams_of[9], 71), 0)
    modulation = noise(streams_of[4], (LEVELS, 3, D), 0.5, 3.0, (), jnp.float32)
    w_qkv = draw_w_qkv(jax.random.fold_in(streams_of[9], 71), 0)
    qk_gain = draw_qk_gain(jax.random.fold_in(streams_of[9], 71), 0)
    w_out = noise(streams_of[7], (HEADS * HDIM, D), (HEADS * HDIM) ** -0.5, 0.15625, ((0, 4),))
    sampler = jnp.clip(jax.random.uniform(streams_of[8], (LEVELS, 2), jnp.float32, 0.3, 1.0), 0.3, 1.0)
    return {"queue_latents": queue_latents, "fresh_noise": fresh_noise, "levels": levels, "window_start": window_start, "modulation": modulation, "w_qkv": w_qkv, "qk_gain": qk_gain, "w_out": w_out, "sampler": sampler}


def layer_norm(values, eps_value):
    mean = lax.optimization_barrier(jnp.mean(values, axis=-1, keepdims=True))
    centered = values - mean
    var = lax.optimization_barrier(jnp.mean(centered * centered, axis=-1, keepdims=True))
    return centered * lax.rsqrt(var + eps_value)

def reference(queue_latents, fresh_noise, levels, window_start, modulation, w_qkv, qk_gain, w_out, sampler):
    x = queue_latents
    mods = modulation[levels]
    coefs = sampler[levels]
    shift = mods[:, 0][:, None, :]
    scale = mods[:, 1][:, None, :]
    gate = mods[:, 2][:, None, :]
    coef_a = coefs[:, 0][:, None, None]
    coef_b = coefs[:, 1][:, None, None]
    group = HEADS * HDIM // N_TENSOR
    for step in range(STEPS):
        xf = x.astype(jnp.float32)
        hidden = (layer_norm(xf, 1e-06) * (1.0 + scale) + shift).astype(jnp.bfloat16)
        qkv = jnp.dot(hidden.reshape(FRAMES * FT, D), w_qkv.reshape(D, 3 * HEADS * HDIM), preferred_element_type=jnp.float32)
        qkv = qkv.reshape(FRAMES, FT, 3, HEADS, HDIM)
        query = (layer_norm(qkv[:, :, 0], 1e-06) * qk_gain[0].reshape(HEADS, HDIM)).astype(jnp.bfloat16)
        keys = (layer_norm(qkv[:, :, 1], 1e-06) * qk_gain[1].reshape(HEADS, HDIM)).astype(jnp.bfloat16)
        values = qkv[:, :, 2].astype(jnp.bfloat16)

        def one_frame(index):
            start = window_start[index].astype(jnp.int32)
            kwin = lax.dynamic_slice_in_dim(keys, start, WIN, 0).reshape(WIN * FT, HEADS, HDIM)
            vwin = lax.dynamic_slice_in_dim(values, start, WIN, 0).reshape(WIN * FT, HEADS, HDIM)
            scores = jnp.einsum('qhd,khd->hqk', query[index].astype(jnp.float32), kwin.astype(jnp.float32)) / jnp.sqrt(jnp.float32(HDIM))
            top = lax.optimization_barrier(jnp.max(scores, axis=-1, keepdims=True))
            expo = jnp.exp(scores - top)
            weights = (expo / lax.optimization_barrier(jnp.sum(expo, axis=-1, keepdims=True))).astype(jnp.bfloat16)
            out = jnp.einsum('hqk,khd->qhd', weights.astype(jnp.float32), vwin.astype(jnp.float32))
            return out.astype(jnp.bfloat16).reshape(FT, HEADS * HDIM)
        attn = lax.map(one_frame, jnp.arange(FRAMES, dtype=jnp.int32)).reshape(FRAMES * FT, HEADS * HDIM)
        branch = jnp.zeros((FRAMES * FT, D), jnp.float32)
        for member in range(N_TENSOR):
            part = jnp.dot(attn[:, member * group:(member + 1) * group], w_out[member * group:(member + 1) * group], preferred_element_type=jnp.float32).astype(jnp.bfloat16)
            part = lax.optimization_barrier(part)
            branch = branch + part.astype(jnp.float32)
        branch = branch.reshape(FRAMES, FT, D)
        noise_pred = xf + gate * branch
        new = (coef_a * xf + coef_b * noise_pred).astype(jnp.bfloat16)
        x = jnp.concatenate([new[1:], fresh_noise[step][None]], axis=0)
    return x
```

```python
import functools

import jax
import jax.numpy as jnp
from jax import lax
from jax.experimental import pallas as pl
from jax.experimental.pallas import tpu as pltpu
from jax.sharding import PartitionSpec as P

MESH = pl.DeviceIdType.MESH
BF16 = jnp.bfloat16
F32 = jnp.float32
STEPS = 2
WIN = 3
EPS = 1e-6

SEM = {}


def slots(name, count):
    SEM[name] = sum(n for _, n in SEM.values()), count


slots("halo_up", 6)
slots("halo_down", 6)
slots("halo_wrap", 3)
slots("attn_core", 6)
slots("attn_y", 6)
slots("attn_fwd", 6)
slots("wout_core", 1)
slots("wout_y", 4)
slots("wout_x", 4)
slots("gather", 6)
slots("shift", 4)
slots("out_y", 4)
slots("out_core", 4)
slots("out_fwd", 4)
slots("meta", 1)
N_SEM = sum(n for _, n in SEM.values())


def kernel(
    frame, width, heads_width,
    x_in, fresh, levels, window_start, mod_in, w_in, gain, wout_in, sampler,
    out,
    x0, x1, h, wkv, wq, wfull, q, attn0, attn1, kv00, kv01, kv02, kv10, kv11, kv12,
    chosen, xs, mod, slot0, slot1, lsem, ssem, rsem,
):
    rows = 2 * frame
    half = width // 2
    quarter = width // 4
    pairs = heads_width // 128
    qi = lax.axis_index("queue")
    ti = lax.axis_index("tensor")
    n_queue = lax.axis_size("queue")
    core = lax.rem(ti, 2)
    chip = lax.div(ti, 2)
    t_core = chip * 2 + (1 - core)
    t_y = lax.rem(ti + 2, 4)
    t_far = 3 - ti
    up = lax.rem(qi + 1, n_queue)
    down = lax.rem(qi + n_queue - 1, n_queue)
    across = lax.rem(qi + n_queue // 2, n_queue)
    plane = lax.div(qi, 16) * 16
    x_up = plane + lax.rem(qi + 4, 16)
    x_down = plane + lax.rem(qi + 12, 16)
    x_pos = lax.div(lax.rem(qi, 16), 4)
    first = qi == 0
    final = qi == n_queue - 1

    def rcopy(name, index, src, dst, device):
        slot = SEM[name][0] + index
        return pltpu.make_async_remote_copy(
            src_ref=src, dst_ref=dst, send_sem=ssem.at[slot], recv_sem=rsem.at[slot],
            device_id=device, device_id_type=MESH,
        )

    def landed(name, index, ref):
        rcopy(name, index, ref, ref, (qi, t_core)).wait_recv()

    def local(index, src, dst):
        return pltpu.make_async_copy(src, dst, lsem.at[index])

    def at_lane(start, size):
        return pl.ds(pl.multiple_of(start, 128), size)

    def at_row(start, size):
        return pl.ds(pl.multiple_of(start, 16), size)

    load_x = local(0, x_in, x0)
    load_mod = local(1, mod_in, mod)
    load_x.start()
    load_mod.start()
    load_w = []
    for p in range(pairs):
        for j in (1, 2):
            load_w.append(
                local(1 + 2 * p + j, w_in.at[j, :, p * 128 : (p + 1) * 128],
                      wkv.at[p, :, (j - 1) * 128 : j * 128])
            )
    load_w.append(local(8, w_in.at[0], wq))
    for load in load_w:
        load.start()
    my_half = at_lane(core * half, half)
    other_half = at_lane((1 - core) * half, half)
    load_wout = local(9, wout_in.at[:, my_half], wfull.at[at_row(ti * heads_width, heads_width)])
    load_wout.start()

    barrier = pltpu.get_barrier_semaphore()
    partners = [
        (up, ti), (down, ti), (qi, t_core), (qi, t_y),
        (across, t_y), (across, t_far), (x_up, ti), (x_down, ti),
    ]
    for device in partners:
        pl.semaphore_signal(barrier, inc=1, device_id=device, device_id_type=MESH)
    pl.semaphore_wait(barrier, len(partners))

    sends = []

    def send(name, index, src, dst, device):
        copy = rcopy(name, index, src, dst, device)
        copy.start()
        sends.append((None, copy))
        return copy

    def send_if(cond, name, index, src, dst, device):
        copy = rcopy(name, index, src, dst, device)

        @pl.when(cond)
        def _():
            copy.start()

        sends.append((cond, copy))

    piece = heads_width // 4

    def my_piece(k):
        return lax.rem(x_pos + k, 4) * piece

    def wout_rows(t, k):
        return wfull.at[at_row(t * heads_width + my_piece(k), piece)]

    def wout_src(k, columns):
        return wout_in.at[at_row(my_piece(k), piece), columns]

    send("wout_y", 0, wout_src(0, my_half), wout_rows(ti, 0), (across, t_y))
    send("wout_y", 1, wout_src(0, other_half), wout_rows(ti, 0), (across, t_far))
    send("wout_core", 0, wout_in.at[:, other_half],
         wfull.at[at_row(ti * heads_width, heads_width)], (qi, t_core))
    send("wout_y", 2, wout_src(2, my_half), wout_rows(ti, 2), (across, t_y))
    send("wout_y", 3, wout_src(2, other_half), wout_rows(ti, 2), (across, t_far))

    def forward_wout():
        for i, t in enumerate((t_y, t_far)):
            landed("wout_y", i, wout_rows(t, 0))
            send("wout_x", i, wout_rows(t, 0), wout_rows(t, 0), (x_up, ti))
            send("wout_x", 2 + i, wout_rows(t, 0), wout_rows(t, 0), (x_down, ti))

    def finish_wout():
        load_wout.wait()
        landed("wout_core", 0, wfull.at[at_row(t_core * heads_width, heads_width)])
        for i, t in enumerate((t_y, t_far)):
            landed("wout_y", 2 + i, wout_rows(t, 2))
            landed("wout_x", i, wout_rows(t, 3))
            landed("wout_x", 2 + i, wout_rows(t, 1))

    row_head = lax.broadcasted_iota(jnp.int32, (128, 128), 0) >> 6
    col_head = lax.broadcasted_iota(jnp.int32, (128, 128), 1) >> 6
    head_mean = jnp.where(row_head == col_head, 1.0 / 64.0, 0.0).astype(BF16)

    def head_norm(values, gain_row):
        high = values.astype(BF16)
        low = (values - high.astype(F32)).astype(BF16)
        mean = jnp.dot(high, head_mean, preferred_element_type=F32)
        mean = mean + jnp.dot(low, head_mean, preferred_element_type=F32)
        centered = values - mean
        var = jnp.dot((centered * centered).astype(BF16), head_mean, preferred_element_type=F32)
        return (centered * lax.rsqrt(var + EPS) * gain_row).astype(BF16)

    for f in range(2):
        slot0[f, 3:4, :] = jnp.full((1, width), sampler[0, levels[f]], F32)
        slot0[f, 4:5, :] = jnp.full((1, width), sampler[1, levels[f]], F32)
        slot0[f, 5:8, :] = jnp.full((3, width), window_start[f].astype(F32), F32)
    load_mod.wait()
    for f in range(2):
        for j in range(3):
            slot0[f, j : j + 1, :] = mod[j, pl.ds(levels[f], 1), :]
    send("meta", 0, slot0.at[1], slot1, (up, ti))

    def norm_rows(src, params):
        chunk = 16
        for f in range(2):
            param = params[f]

            @pl.loop(0, frame // chunk)
            def _(i):
                at = pl.ds(pl.multiple_of(f * frame + i * chunk, chunk), chunk)
                values = src[at, :].astype(F32)
                mean = jnp.mean(values, axis=-1, keepdims=True)
                centered = values - mean
                var = jnp.mean(centered * centered, axis=-1, keepdims=True)
                normed = centered * lax.rsqrt(var + EPS)
                h[at, :] = (
                    normed * (1.0 + param[1:2, :]) + param[0:1, :]
                ).astype(BF16)

    def project_kv(kv, p):
        @pl.loop(0, 2)
        def _(f):
            at = pl.ds(pl.multiple_of(f * frame, frame), frame)
            acc = jnp.dot(h[at, :], wkv[p], preferred_element_type=F32)
            kv[f + 2, :, 0:128] = head_norm(acc[:, :128], gain[1:2, p * 128 : (p + 1) * 128])
            kv[f + 2, :, 128:256] = acc[:, 128:].astype(BF16)

    def project_q():
        @pl.loop(0, 2)
        def _(f):
            at = pl.ds(pl.multiple_of(f * frame, frame), frame)
            acc = jnp.dot(h[at, :], wq[...], preferred_element_type=F32)
            for p in range(pairs):
                cols = slice(p * 128, (p + 1) * 128)
                q[at, cols] = head_norm(acc[:, cols], gain[0:1, cols]) * jnp.asarray(0.125, BF16)

    q_chunk = frame // 2
    first_head = lax.broadcasted_iota(jnp.int32, (q_chunk, 128), 1) < 64
    zeros = jnp.zeros((q_chunk, 128), BF16)
    ones = jnp.ones((WIN * frame, 128), BF16)

    def attend(kv, p, f, window, flag, attn):
        fixed, second, if_set, if_clear = window
        chosen[...] = jnp.where(
            flag, kv[if_set].astype(F32), kv[if_clear].astype(F32)
        ).astype(BF16)

        @pl.loop(0, 2)
        def _(i):
            at = pl.ds(pl.multiple_of(f * frame + i * q_chunk, 16), q_chunk)
            keys = jnp.concatenate(
                [kv[fixed, :, 0:128], kv[second, :, 0:128], chosen[:, 0:128]], axis=0
            )
            values = jnp.concatenate(
                [kv[fixed, :, 128:256], kv[second, :, 128:256], chosen[:, 128:256]], axis=0
            )
            values = jnp.concatenate([values, ones], axis=1)
            rows_q = q[at, p * 128 : (p + 1) * 128]
            both = jnp.concatenate(
                [jnp.where(first_head, rows_q, zeros), jnp.where(first_head, zeros, rows_q)], axis=0
            )
            scores = lax.dot_general(
                both, keys, (((1,), (1,)), ((), ())), preferred_element_type=F32
            )
            top = jnp.max(scores, axis=-1, keepdims=True)
            expo = jnp.exp(scores - top).astype(BF16)
            total = jnp.dot(expo, values, preferred_element_type=F32)
            mixed = total[:, :128] / total[:, 128:]
            attn[at, at_lane(ti * heads_width + p * 128, 128)] = jnp.where(
                first_head, mixed[:q_chunk], mixed[q_chunk:]
            ).astype(BF16)

    def attn_block(attn, t, p):
        return attn.at[:, at_lane(t * heads_width + p * 128, 128)]

    def share_attn(step, attn, p):
        mine = attn_block(attn, ti, p)
        send("attn_core", step * 3 + p, mine, mine, (qi, t_core))
        send("attn_y", step * 3 + p, mine, mine, (qi, t_y))

    def forward_attn(step, attn, p):
        block = attn_block(attn, t_y, p)
        landed("attn_y", step * 3 + p, block)
        send("attn_fwd", step * 3 + p, block, block, (qi, t_core))

    def finish_attn(step, attn):
        for p in range(pairs):
            landed("attn_core", step * 3 + p, attn_block(attn, t_core, p))
        for p in range(pairs):
            landed("attn_fwd", step * 3 + p, attn_block(attn, t_far, p))

    def update(values, branch, param, columns):
        values = values.astype(F32)
        noise_pred = values + param[2:3, columns] * branch
        return (param[3:4, columns] * values + param[4:5, columns] * noise_pred).astype(BF16)

    kv0 = (kv00, kv01, kv02)
    kv1 = (kv10, kv11, kv12)
    param0 = (slot0.at[0], slot0.at[1])
    param1 = (slot1, slot0.at[0])
    window0 = (
        (2, jnp.where(first, 4, 1), 3, 0),
        (3, jnp.where(final, 1, 4), 5, 2),
    )
    window1 = (
        (2, jnp.where(first, 0, 3), jnp.where(first, 1, 4), 1),
        (3, 2, 4, 1),
    )

    def starts_from(param, slot):
        start = jnp.concatenate([param[5:6, 0:128]] * 2, axis=1)
        return start >= slot.astype(F32)

    load_x.wait()
    norm_rows(x0, param0)
    for p in range(pairs):
        load_w[2 * p].wait()
        load_w[2 * p + 1].wait()
        project_kv(kv0[p], p)
        own = kv0[p].at[2:4]
        send_if(jnp.logical_not(final), "halo_up", p, own, kv0[p].at[0:2], (up, ti))
        send_if(jnp.logical_not(first), "halo_down", p, own, kv0[p].at[4:6], (down, ti))
    load_w[6].wait()
    project_q()
    for p in range(pairs):
        if p == 1:
            forward_wout()

        @pl.when(jnp.logical_not(first))
        def _():
            landed("halo_up", p, kv0[p].at[0:2])

        @pl.when(jnp.logical_not(final))
        def _():
            landed("halo_down", p, kv0[p].at[4:6])

        for f in range(2):
            attend(kv0[p], p, f, window0[f], starts_from(param0[f], 2 * qi - 1 + 2 * f), attn0)
        share_attn(0, attn0, p)
        if p > 0:
            forward_attn(0, attn0, p - 1)
    forward_attn(0, attn0, pairs - 1)
    finish_wout()
    finish_attn(0, attn0)

    n_cols = 256

    @pl.loop(0, half // n_cols)
    def _(n):
        columns = at_lane(core * half + n * n_cols, n_cols)
        weight = wfull[:, at_lane(n * n_cols, n_cols)]
        for f in range(2):
            at = slice(f * frame, (f + 1) * frame)
            branch = jnp.dot(attn0[at, :], weight, preferred_element_type=F32)
            x1[at, columns] = update(x0[at, columns], branch, param0[f], columns)
        rcopy("gather", n, x1.at[:, columns], x1.at[:, columns], (qi, t_core)).start()

    @pl.loop(0, half // n_cols)
    def _(n):
        theirs = at_lane((1 - core) * half + n * n_cols, n_cols)
        columns = at_lane(core * half + n * n_cols, n_cols)
        rcopy("gather", n, x1.at[:, columns], x1.at[:, theirs], (qi, t_core)).wait_send()
        landed("gather", n, x1.at[:, theirs])

    @pl.when(first)
    def _():
        entered = local(0, fresh.at[0], x1.at[0:frame])
        entered.start()
        entered.wait()

    landed("meta", 0, slot1)
    norm_rows(x1, param1)
    for p in range(pairs):
        project_kv(kv1[p], p)
        send("halo_up", 3 + p, kv1[p].at[3], kv1[p].at[1], (up, ti))
        send("halo_down", 3 + p, kv1[p].at[2], kv1[p].at[4], (down, ti))
        send_if(final, "halo_wrap", p, kv1[p].at[2], kv1[p].at[0], (up, ti))
    project_q()
    for p in range(pairs):
        landed("halo_up", 3 + p, kv1[p].at[1])
        landed("halo_down", 3 + p, kv1[p].at[4])

        @pl.when(first)
        def _():
            landed("halo_wrap", p, kv1[p].at[0])

        for f in range(2):
            attend(kv1[p], p, f, window1[f], starts_from(param1[f], 2 * qi - 1), attn1)
        share_attn(1, attn1, p)
        if p > 0:
            forward_attn(1, attn1, p - 1)
    forward_attn(1, attn1, pairs - 1)
    finish_attn(1, attn1)

    chunks = 4
    n_rows = rows // chunks
    my_quarter = core * half + chip * quarter
    y_quarter = core * half + (1 - chip) * quarter

    def out_part(j, start):
        return out.at[at_row(j * n_rows, n_rows), at_lane(start, quarter)]

    for j in range(chunks):
        f = j // 2
        at = slice(j * n_rows, (j + 1) * n_rows)

        @pl.loop(0, quarter // n_cols)
        def _(n):
            columns = at_lane(my_quarter + n * n_cols, n_cols)
            inner = at_lane(n * n_cols, n_cols)
            weight = wfull[:, at_lane(chip * quarter + n * n_cols, n_cols)]
            branch = jnp.dot(attn1[at, :], weight, preferred_element_type=F32)
            xs[at, inner] = update(x1[at, columns], branch, param1[f], columns)

        part = (xs.at[at], out_part(j, my_quarter), (down, ti))
        if f == 0:
            send("shift", j, *part)
        else:
            send_if(jnp.logical_not(first), "shift", j, *part)

    @pl.when(final)
    def _():
        last = local(0, fresh.at[1], out.at[frame:rows])
        last.start()
        last.wait()

    def guarded(f, action):
        if f == 0:
            action()
        else:
            pl.when(jnp.logical_not(final))(action)

    def spread(j):
        def action():
            part = out_part(j, my_quarter)
            landed("shift", j, part)
            rcopy("out_y", j, part, part, (qi, t_y)).start()
            rcopy("out_core", j, part, part, (qi, t_core)).start()

        guarded(j // 2, action)

    def pass_on(j):
        def action():
            part = out_part(j, y_quarter)
            landed("out_y", j, part)
            rcopy("out_fwd", j, part, part, (qi, t_core)).start()

        guarded(j // 2, action)

    for j in range(chunks):
        spread(j)
        if j > 0:
            pass_on(j - 1)
    pass_on(chunks - 1)

    core_quarter = (1 - core) * half + chip * quarter
    far_quarter = (1 - core) * half + (1 - chip) * quarter
    for j in range(chunks):

        def action():
            landed("out_core", j, out_part(j, core_quarter))
            landed("out_fwd", j, out_part(j, far_quarter))
            mine = out_part(j, my_quarter)
            rcopy("out_y", j, mine, mine, (qi, t_y)).wait_send()
            rcopy("out_core", j, mine, mine, (qi, t_core)).wait_send()
            passed = out_part(j, y_quarter)
            rcopy("out_fwd", j, passed, passed, (qi, t_core)).wait_send()

        guarded(j // 2, action)

    for cond, copy in sends:
        if cond is None:
            copy.wait_send()
        else:
            pl.when(cond)(copy.wait_send)


def body(
    queue_latents, fresh_noise, levels, window_start, modulation, w_qkv, qk_gain, w_out, sampler
):
    frames, frame, width = queue_latents.shape
    rows = frames * frame
    heads_width = w_out.shape[0]
    level_count = modulation.shape[0]
    any_space = pl.BlockSpec(memory_space=pl.ANY)
    smem = pl.BlockSpec(memory_space=pltpu.SMEM)
    vmem = pl.BlockSpec(memory_space=pltpu.VMEM)
    kv = pltpu.VMEM((6, frame, 256), BF16)
    result = pl.pallas_call(
        functools.partial(kernel, frame, width, heads_width),
        name="diagonal_steps",
        out_shape=jax.ShapeDtypeStruct((rows, width), BF16),
        in_specs=[any_space, any_space, smem, smem, any_space, any_space, vmem, any_space, smem],
        out_specs=any_space,
        scratch_shapes=[
            pltpu.VMEM((rows, width), BF16),
            pltpu.VMEM((rows, width), BF16),
            pltpu.VMEM((rows, width), BF16),
            pltpu.VMEM((heads_width // 128, width, 256), BF16),
            pltpu.VMEM((width, heads_width), BF16),
            pltpu.VMEM((4 * heads_width, width // 2), BF16),
            pltpu.VMEM((rows, heads_width), BF16),
            pltpu.VMEM((rows, 4 * heads_width), BF16),
            pltpu.VMEM((rows, 4 * heads_width), BF16),
            kv, kv, kv, kv, kv, kv,
            pltpu.VMEM((frame, 256), BF16),
            pltpu.VMEM((rows, width // 4), BF16),
            pltpu.VMEM((3, level_count, width), F32),
            pltpu.VMEM((2, 8, width), F32),
            pltpu.VMEM((8, width), F32),
            pltpu.SemaphoreType.DMA((10,)),
            pltpu.SemaphoreType.DMA((N_SEM,)),
            pltpu.SemaphoreType.DMA((N_SEM,)),
        ],
        compiler_params=pltpu.CompilerParams(
            collective_id=0, has_side_effects=True, vmem_limit_bytes=60 * 1024 * 1024
        ),
        cost_estimate=pl.CostEstimate(
            flops=4 * rows * width * 1536 * 2, bytes_accessed=40 * 2**20, transcendentals=10**7
        ),
    )(
        queue_latents.reshape(rows, width),
        fresh_noise,
        levels,
        window_start,
        jnp.transpose(modulation, (1, 0, 2)),
        jnp.transpose(w_qkv, (1, 0, 2)),
        qk_gain,
        w_out,
        jnp.transpose(sampler, (1, 0)),
    )
    return result.reshape(frames, frame, width)


def solution(mesh):
    in_specs = (
        P("queue", None, None),
        P(),
        P("queue"),
        P("queue"),
        P(),
        P(None, None, "tensor"),
        P(None, "tensor"),
        P("tensor", None),
        P(),
    )
    out_specs = P("queue", None, None)
    return jax.shard_map(body, mesh=mesh, in_specs=in_specs, out_specs=out_specs, check_vma=False)
```

```python
import functools

import jax
import jax.numpy as jnp
from jax import lax
from jax.experimental import pallas as pl
from jax.experimental.pallas import tpu as pltpu
from jax.sharding import PartitionSpec as P

MESH = pl.DeviceIdType.MESH
BF16 = jnp.bfloat16
F32 = jnp.float32
STEPS = 2
WIN = 3
EPS = 1e-6

SEM = {}


def slots(name, count):
    SEM[name] = sum(n for _, n in SEM.values()), count


slots("halo_up", 6)
slots("halo_down", 6)
slots("halo_wrap", 3)
slots("attn_core", 12)
slots("attn_y", 12)
slots("attn_fwd", 12)
slots("wout_core", 1)
slots("wout_y", 4)
slots("wout_x", 4)
slots("gather", 6)
slots("shift", 8)
slots("out_y", 8)
slots("out_core", 8)
slots("out_fwd", 8)
slots("meta", 1)
N_SEM = sum(n for _, n in SEM.values())


def kernel(
    frame, width, heads_width,
    x_in, fresh, levels, window_start, mod_in, w_in, gain, wout_in, sampler,
    out,
    x0, x1, h, wkv, wq, wfull, q, attn0, attn1, kv00, kv01, kv02, kv10, kv11, kv12,
    xs, mod, slot0, slot1, lsem, ssem, rsem,
):
    rows = 2 * frame
    half = width // 2
    quarter = width // 4
    pairs = heads_width // 128
    qi = lax.axis_index("queue")
    ti = lax.axis_index("tensor")
    n_queue = lax.axis_size("queue")
    core = lax.rem(ti, 2)
    chip = lax.div(ti, 2)
    t_core = chip * 2 + (1 - core)
    t_y = lax.rem(ti + 2, 4)
    t_far = 3 - ti
    up = lax.rem(qi + 1, n_queue)
    down = lax.rem(qi + n_queue - 1, n_queue)
    across = lax.rem(qi + n_queue // 2, n_queue)
    plane = lax.div(qi, 16) * 16
    x_up = plane + lax.rem(qi + 4, 16)
    x_down = plane + lax.rem(qi + 12, 16)
    x_pos = lax.div(lax.rem(qi, 16), 4)
    first = qi == 0
    final = qi == n_queue - 1

    def rcopy(name, index, src, dst, device):
        slot = SEM[name][0] + index
        return pltpu.make_async_remote_copy(
            src_ref=src, dst_ref=dst, send_sem=ssem.at[slot], recv_sem=rsem.at[slot],
            device_id=device, device_id_type=MESH,
        )

    def landed(name, index, ref):
        rcopy(name, index, ref, ref, (qi, t_core)).wait_recv()

    def local(index, src, dst):
        return pltpu.make_async_copy(src, dst, lsem.at[index])

    def at_lane(start, size):
        return pl.ds(pl.multiple_of(start, 128), size)

    def at_row(start, size):
        return pl.ds(pl.multiple_of(start, 16), size)

    load_mod = local(1, mod_in, mod)
    load_mod.start()
    load_x = []
    for f, index in ((0, 0), (1, 11)):
        at = slice(f * frame, (f + 1) * frame)
        load_x.append(local(index, x_in.at[at], x0.at[at]))
        load_x[f].start()
    load_w = []
    for p in range(pairs):
        for j in (1, 2):
            load_w.append(
                local(1 + 2 * p + j, w_in.at[j, :, p * 128 : (p + 1) * 128],
                      wkv.at[p, :, (j - 1) * 128 : j * 128])
            )
    load_w.append(local(8, w_in.at[0], wq))
    my_half = at_lane(core * half, half)
    other_half = at_lane((1 - core) * half, half)
    load_wout = local(9, wout_in.at[:, my_half], wfull.at[at_row(ti * heads_width, heads_width)])

    last = local(10, fresh.at[1], out.at[frame:rows])

    @pl.when(final)
    def _():
        last.start()

    barrier = pltpu.get_barrier_semaphore()
    partners = [
        (up, ti), (down, ti), (qi, t_core), (qi, t_y),
        (across, t_y), (across, t_far), (x_up, ti), (x_down, ti),
    ]
    for device in partners:
        pl.semaphore_signal(barrier, inc=1, device_id=device, device_id_type=MESH)
    pl.semaphore_wait(barrier, len(partners))

    sends = []

    def send(name, index, src, dst, device):
        copy = rcopy(name, index, src, dst, device)
        copy.start()
        sends.append((None, copy))
        return copy

    def send_if(cond, name, index, src, dst, device):
        copy = rcopy(name, index, src, dst, device)

        @pl.when(cond)
        def _():
            copy.start()

        sends.append((cond, copy))

    piece = heads_width // 4

    def my_piece(k):
        return lax.rem(x_pos + k, 4) * piece

    def wout_rows(t, k):
        return wfull.at[at_row(t * heads_width + my_piece(k), piece)]

    def wout_src(k, columns):
        return wout_in.at[at_row(my_piece(k), piece), columns]

    send("wout_y", 0, wout_src(0, my_half), wout_rows(ti, 0), (across, t_y))
    send("wout_y", 1, wout_src(0, other_half), wout_rows(ti, 0), (across, t_far))
    send("wout_core", 0, wout_in.at[:, other_half],
         wfull.at[at_row(ti * heads_width, heads_width)], (qi, t_core))
    send("wout_y", 2, wout_src(2, my_half), wout_rows(ti, 2), (across, t_y))
    send("wout_y", 3, wout_src(2, other_half), wout_rows(ti, 2), (across, t_far))

    def forward_wout():
        for i, t in enumerate((t_y, t_far)):
            landed("wout_y", i, wout_rows(t, 0))
            send("wout_x", i, wout_rows(t, 0), wout_rows(t, 0), (x_up, ti))
            send("wout_x", 2 + i, wout_rows(t, 0), wout_rows(t, 0), (x_down, ti))

    def finish_wout():
        load_wout.wait()
        landed("wout_core", 0, wfull.at[at_row(t_core * heads_width, heads_width)])
        for i, t in enumerate((t_y, t_far)):
            landed("wout_y", 2 + i, wout_rows(t, 2))
            landed("wout_x", i, wout_rows(t, 3))
            landed("wout_x", 2 + i, wout_rows(t, 1))

    row_head = lax.broadcasted_iota(jnp.int32, (128, 128), 0) >> 6
    col_head = lax.broadcasted_iota(jnp.int32, (128, 128), 1) >> 6
    head_mean = jnp.where(row_head == col_head, 1.0 / 64.0, 0.0).astype(BF16)

    def head_norm(values, gain_row):
        high = values.astype(BF16)
        low = (values - high.astype(F32)).astype(BF16)
        mean = jnp.dot(high, head_mean, preferred_element_type=F32)
        mean = mean + jnp.dot(low, head_mean, preferred_element_type=F32)
        centered = values - mean
        var = jnp.dot((centered * centered).astype(BF16), head_mean, preferred_element_type=F32)
        return (centered * lax.rsqrt(var + EPS) * gain_row).astype(BF16)

    for f in range(2):
        slot0[f, 3:4, :] = jnp.full((1, width), sampler[0, levels[f]], F32)
        slot0[f, 4:5, :] = jnp.full((1, width), sampler[1, levels[f]], F32)
        slot0[f, 5:8, :] = jnp.full((3, width), window_start[f].astype(F32), F32)
    load_mod.wait()
    for f in range(2):
        for j in range(3):
            slot0[f, j : j + 1, :] = mod[j, pl.ds(levels[f], 1), :]
    send("meta", 0, slot0.at[1], slot1, (up, ti))

    def norm_rows(src, params, f):
        param = params[f]
        chunk = 64

        @pl.loop(0, frame // chunk)
        def _(i):
            at = pl.ds(pl.multiple_of(f * frame + i * chunk, chunk), chunk)
            mean = jnp.mean(src[at, :].astype(F32), axis=-1, keepdims=True)
            centered = src[at, :].astype(F32) - mean
            var = jnp.mean(centered * centered, axis=-1, keepdims=True)
            normed = (src[at, :].astype(F32) - mean) * lax.rsqrt(var + EPS)
            h[at, :] = (normed * (1.0 + param[1:2, :]) + param[0:1, :]).astype(BF16)

    def project_kv(kv, p):
        acc = jnp.dot(h[...], wkv[p], preferred_element_type=F32)
        for f in range(2):
            part = acc[f * frame : (f + 1) * frame]
            kv[f + 2, :, 0:128] = head_norm(part[:, :128], gain[1:2, p * 128 : (p + 1) * 128])
            kv[f + 2, :, 128:256] = part[:, 128:].astype(BF16)

    def project_q():
        acc = jnp.dot(h[...], wq[...], preferred_element_type=F32)
        for p in range(pairs):
            cols = slice(p * 128, (p + 1) * 128)
            q[:, cols] = head_norm(acc[:, cols], gain[0:1, cols]) * jnp.asarray(0.125, BF16)

    q_chunk = 128
    first_head = lax.broadcasted_iota(jnp.int32, (q_chunk, 128), 1) < 64
    zeros = jnp.zeros((q_chunk, 128), BF16)
    ones = jnp.ones((WIN * frame, 128), BF16)

    def attend(kv, p, f, window, flag, attn):
        fixed, second, if_set, if_clear = window
        chosen = jnp.where(flag, kv[if_set].astype(F32), kv[if_clear].astype(F32)).astype(BF16)
        keys = jnp.concatenate([kv[fixed, :, 0:128], kv[second, :, 0:128], chosen[:, 0:128]], axis=0)
        values = jnp.concatenate(
            [kv[fixed, :, 128:256], kv[second, :, 128:256], chosen[:, 128:256]], axis=0
        )
        values = jnp.concatenate([values, ones], axis=1)

        def scores_of(i):
            start = f * frame + i * q_chunk
            rows_q = q[start : start + q_chunk, p * 128 : (p + 1) * 128]
            both = jnp.concatenate(
                [jnp.where(first_head, rows_q, zeros), jnp.where(first_head, zeros, rows_q)], axis=0
            )
            return lax.dot_general(
                both, keys, (((1,), (1,)), ((), ())), preferred_element_type=F32
            )

        n = frame // q_chunk
        ahead = scores_of(0)
        for i in range(n):
            scores = ahead
            if i + 1 < n:
                ahead = scores_of(i + 1)
            top = jnp.max(scores, axis=-1, keepdims=True)
            expo = jnp.exp(scores - top).astype(BF16)
            total = jnp.dot(expo, values, preferred_element_type=F32)
            picked = jnp.where(
                jnp.concatenate([first_head, first_head], axis=1), total[:q_chunk], total[q_chunk:]
            )
            start = f * frame + i * q_chunk
            attn[start : start + q_chunk, at_lane(ti * heads_width + p * 128, 128)] = (
                picked[:, :128] / picked[:, 128:]
            ).astype(BF16)

    def attn_block(attn, t, p, f):
        return attn.at[f * frame : (f + 1) * frame, at_lane(t * heads_width + p * 128, 128)]

    def attn_slot(step, p, f):
        return step * 6 + p * 2 + f

    def share_attn(step, attn, p, f):
        mine = attn_block(attn, ti, p, f)
        send("attn_y", attn_slot(step, p, f), mine, mine, (qi, t_y))
        send("attn_core", attn_slot(step, p, f), mine, mine, (qi, t_core))

    def forward_attn(step, attn, p, f):
        block = attn_block(attn, t_y, p, f)
        landed("attn_y", attn_slot(step, p, f), block)
        send("attn_fwd", attn_slot(step, p, f), block, block, (qi, t_core))

    def finish_attn(step, attn, f):
        for p in range(pairs):
            landed("attn_core", attn_slot(step, p, f), attn_block(attn, t_core, p, f))
            landed("attn_fwd", attn_slot(step, p, f), attn_block(attn, t_far, p, f))

    def update(values, branch, param, columns):
        values = values.astype(F32)
        noise_pred = values + param[2:3, columns] * branch
        return (param[3:4, columns] * values + param[4:5, columns] * noise_pred).astype(BF16)

    kv0 = (kv00, kv01, kv02)
    kv1 = (kv10, kv11, kv12)
    param0 = (slot0.at[0], slot0.at[1])
    param1 = (slot1, slot0.at[0])
    window0 = (
        (2, jnp.where(first, 4, 1), 3, 0),
        (3, jnp.where(final, 1, 4), 5, 2),
    )
    window1 = (
        (2, jnp.where(first, 0, 3), jnp.where(first, 1, 4), 1),
        (3, 2, 4, 1),
    )

    def starts_from(param, slot):
        start = jnp.concatenate([param[5:6, 0:128]] * 2, axis=1)
        return start >= slot.astype(F32)

    for f in range(2):
        load_x[f].wait()
        if f == 1:
            for load in load_w + [load_wout]:
                load.start()
        norm_rows(x0, param0, f)
    for p in range(pairs):
        load_w[2 * p].wait()
        load_w[2 * p + 1].wait()
        project_kv(kv0[p], p)
        own = kv0[p].at[2:4]
        send_if(jnp.logical_not(final), "halo_up", p, own, kv0[p].at[0:2], (up, ti))
        send_if(jnp.logical_not(first), "halo_down", p, own, kv0[p].at[4:6], (down, ti))
    load_w[6].wait()
    project_q()
    for p in range(pairs):
        if p == 1:
            forward_wout()

        @pl.when(jnp.logical_not(first))
        def _():
            landed("halo_up", p, kv0[p].at[0:2])

        @pl.when(jnp.logical_not(final))
        def _():
            landed("halo_down", p, kv0[p].at[4:6])

        for f in range(2):
            attend(kv0[p], p, f, window0[f], starts_from(param0[f], 2 * qi - 1 + 2 * f), attn0)
            share_attn(0, attn0, p, f)
            if p > 0:
                forward_attn(0, attn0, p - 1, f)
    finish_wout()
    for f in range(2):
        forward_attn(0, attn0, pairs - 1, f)
    for f in range(2):
        finish_attn(0, attn0, f)

    n_cols = 256

    @pl.loop(0, half // n_cols)
    def _(n):
        columns = at_lane(core * half + n * n_cols, n_cols)
        weight = wfull[:, at_lane(n * n_cols, n_cols)]
        for f in range(2):
            at = slice(f * frame, (f + 1) * frame)
            branch = jnp.dot(attn0[at, :], weight, preferred_element_type=F32)
            x1[at, columns] = update(x0[at, columns], branch, param0[f], columns)
        rcopy("gather", n, x1.at[:, columns], x1.at[:, columns], (qi, t_core)).start()

    @pl.loop(0, half // n_cols)
    def _(n):
        theirs = at_lane((1 - core) * half + n * n_cols, n_cols)
        columns = at_lane(core * half + n * n_cols, n_cols)
        rcopy("gather", n, x1.at[:, columns], x1.at[:, theirs], (qi, t_core)).wait_send()
        landed("gather", n, x1.at[:, theirs])

    @pl.when(first)
    def _():
        entered = local(0, fresh.at[0], x1.at[0:frame])
        entered.start()
        entered.wait()

    landed("meta", 0, slot1)
    for f in range(2):
        norm_rows(x1, param1, f)
    for p in range(pairs):
        project_kv(kv1[p], p)
        send("halo_up", 3 + p, kv1[p].at[3], kv1[p].at[1], (up, ti))
        send("halo_down", 3 + p, kv1[p].at[2], kv1[p].at[4], (down, ti))
        send_if(final, "halo_wrap", p, kv1[p].at[2], kv1[p].at[0], (up, ti))
    project_q()
    for p in range(pairs):
        landed("halo_up", 3 + p, kv1[p].at[1])
        landed("halo_down", 3 + p, kv1[p].at[4])

        @pl.when(first)
        def _():
            landed("halo_wrap", p, kv1[p].at[0])

        for f in range(2):
            attend(kv1[p], p, f, window1[f], starts_from(param1[f], 2 * qi - 1), attn1)
            share_attn(1, attn1, p, f)
            if p > 0:
                forward_attn(1, attn1, p - 1, f)

    chunks = 8
    n_rows = rows // chunks
    my_quarter = core * half + chip * quarter
    y_quarter = core * half + (1 - chip) * quarter

    def out_part(j, start):
        return out.at[at_row(j * n_rows, n_rows), at_lane(start, quarter)]

    for f in range(2):
        forward_attn(1, attn1, pairs - 1, f)
        finish_attn(1, attn1, f)
        at = slice(f * frame, (f + 1) * frame)

        @pl.loop(0, quarter // n_cols)
        def _(n):
            columns = at_lane(my_quarter + n * n_cols, n_cols)
            inner = at_lane(n * n_cols, n_cols)
            weight = wfull[:, at_lane(chip * quarter + n * n_cols, n_cols)]
            branch = jnp.dot(attn1[at, :], weight, preferred_element_type=F32)
            xs[at, inner] = update(x1[at, columns], branch, param1[f], columns)

        for j in range(f * chunks // 2, (f + 1) * chunks // 2):
            part = (xs.at[j * n_rows : (j + 1) * n_rows], out_part(j, my_quarter), (down, ti))
            if f == 0:
                send("shift", j, *part)
            else:
                send_if(jnp.logical_not(first), "shift", j, *part)

    def guarded(f, action):
        if f == 0:
            action()
        else:
            pl.when(jnp.logical_not(final))(action)

    def spread(j):
        def action():
            part = out_part(j, my_quarter)
            landed("shift", j, part)
            rcopy("out_y", j, part, part, (qi, t_y)).start()
            rcopy("out_core", j, part, part, (qi, t_core)).start()

        guarded(j // (chunks // 2), action)

    def pass_on(j):
        def action():
            part = out_part(j, y_quarter)
            landed("out_y", j, part)
            rcopy("out_fwd", j, part, part, (qi, t_core)).start()

        guarded(j // (chunks // 2), action)

    for j in range(chunks):
        spread(j)
        if j > 0:
            pass_on(j - 1)
    pass_on(chunks - 1)

    core_quarter = (1 - core) * half + chip * quarter
    far_quarter = (1 - core) * half + (1 - chip) * quarter
    for j in range(chunks):

        def action():
            landed("out_core", j, out_part(j, core_quarter))
            landed("out_fwd", j, out_part(j, far_quarter))
            mine = out_part(j, my_quarter)
            rcopy("out_y", j, mine, mine, (qi, t_y)).wait_send()
            rcopy("out_core", j, mine, mine, (qi, t_core)).wait_send()
            passed = out_part(j, y_quarter)
            rcopy("out_fwd", j, passed, passed, (qi, t_core)).wait_send()

        guarded(j // (chunks // 2), action)

    @pl.when(final)
    def _():
        last.wait()

    for cond, copy in sends:
        if cond is None:
            copy.wait_send()
        else:
            pl.when(cond)(copy.wait_send)


def body(
    queue_latents, fresh_noise, levels, window_start, modulation, w_qkv, qk_gain, w_out, sampler
):
    frames, frame, width = queue_latents.shape
    rows = frames * frame
    heads_width = w_out.shape[0]
    level_count = modulation.shape[0]
    any_space = pl.BlockSpec(memory_space=pl.ANY)
    smem = pl.BlockSpec(memory_space=pltpu.SMEM)
    vmem = pl.BlockSpec(memory_space=pltpu.VMEM)
    kv = pltpu.VMEM((6, frame, 256), BF16)
    result = pl.pallas_call(
        functools.partial(kernel, frame, width, heads_width),
        name="diagonal_steps",
        out_shape=jax.ShapeDtypeStruct((rows, width), BF16),
        in_specs=[any_space, any_space, smem, smem, any_space, any_space, vmem, any_space, smem],
        out_specs=any_space,
        scratch_shapes=[
            pltpu.VMEM((rows, width), BF16),
            pltpu.VMEM((rows, width), BF16),
            pltpu.VMEM((rows, width), BF16),
            pltpu.VMEM((heads_width // 128, width, 256), BF16),
            pltpu.VMEM((width, heads_width), BF16),
            pltpu.VMEM((4 * heads_width, width // 2), BF16),
            pltpu.VMEM((rows, heads_width), BF16),
            pltpu.VMEM((rows, 4 * heads_width), BF16),
            pltpu.VMEM((rows, 4 * heads_width), BF16),
            kv, kv, kv, kv, kv, kv,
            pltpu.VMEM((rows, width // 4), BF16),
            pltpu.VMEM((3, level_count, width), F32),
            pltpu.VMEM((2, 8, width), F32),
            pltpu.VMEM((8, width), F32),
            pltpu.SemaphoreType.DMA((12,)),
            pltpu.SemaphoreType.DMA((N_SEM,)),
            pltpu.SemaphoreType.DMA((N_SEM,)),
        ],
        compiler_params=pltpu.CompilerParams(
            collective_id=0, has_side_effects=True, vmem_limit_bytes=60 * 1024 * 1024
        ),
        cost_estimate=pl.CostEstimate(
            flops=4 * rows * width * 1536 * 2, bytes_accessed=40 * 2**20, transcendentals=10**7
        ),
    )(
        queue_latents.reshape(rows, width),
        fresh_noise,
        levels,
        window_start,
        jnp.transpose(modulation, (1, 0, 2)),
        jnp.transpose(w_qkv, (1, 0, 2)),
        qk_gain,
        w_out,
        jnp.transpose(sampler, (1, 0)),
    )
    return result.reshape(frames, frame, width)


def solution(mesh):
    in_specs = (
        P("queue", None, None),
        P(),
        P("queue"),
        P("queue"),
        P(),
        P(None, None, "tensor"),
        P(None, "tensor"),
        P("tensor", None),
        P(),
    )
    out_specs = P("queue", None, None)
    return jax.shard_map(body, mesh=mesh, in_specs=in_specs, out_specs=out_specs, check_vma=False)
```

```python
import functools

import jax
import jax.numpy as jnp
from jax import lax
from jax.experimental import pallas as pl
from jax.experimental.pallas import tpu as pltpu
from jax.sharding import PartitionSpec as P

MESH = pl.DeviceIdType.MESH
BF16 = jnp.bfloat16
F32 = jnp.float32
STEPS = 2
WIN = 3
EPS = 1e-6

SEM = {}


def slots(name, count):
    SEM[name] = sum(n for _, n in SEM.values()), count


slots("halo_up", 6)
slots("halo_down", 6)
slots("attn_core", 15)
slots("attn_y", 15)
slots("attn_fwd", 15)
slots("wout_core", 1)
slots("wout_y", 4)
slots("wout_x", 4)
slots("gather", 6)
slots("shift", 8)
slots("out_y", 8)
slots("out_core", 8)
slots("out_fwd", 8)
slots("relay", 8)
slots("relayed", 8)
slots("meta", 1)
N_SEM = sum(n for _, n in SEM.values())


def kernel(
    frame, width, heads_width,
    x_in, fresh, levels, window_start, mod_in, w_in, gain, wout_in, sampler,
    out,
    x0, x1, h, wkv, wq, wfull, q, attn0, attn1, kv00, kv01, kv02, kv10, kv11, kv12,
    xs, xf, qf, attnf, xsf, relay, mod, slot0, slot1, lsem, ssem, rsem,
):
    rows = 2 * frame
    half = width // 2
    quarter = width // 4
    pairs = heads_width // 128
    qi = lax.axis_index("queue")
    ti = lax.axis_index("tensor")
    n_queue = lax.axis_size("queue")
    core = lax.rem(ti, 2)
    chip = lax.div(ti, 2)
    t_core = chip * 2 + (1 - core)
    t_y = lax.rem(ti + 2, 4)
    t_far = 3 - ti
    up = lax.rem(qi + 1, n_queue)
    down = lax.rem(qi + n_queue - 1, n_queue)
    across = lax.rem(qi + n_queue // 2, n_queue)
    plane = lax.div(qi, 16) * 16
    x_up = plane + lax.rem(qi + 4, 16)
    x_down = plane + lax.rem(qi + 12, 16)
    x_pos = lax.div(lax.rem(qi, 16), 4)
    first = qi == 0
    final = qi == n_queue - 1
    mirror = plane + 15 - lax.rem(qi, 16)
    middle = qi == n_queue // 2
    not_first = jnp.logical_not(first)
    not_final = jnp.logical_not(final)

    def rcopy(name, index, src, dst, device, lands_as=None):
        slot = SEM[name][0] + index
        lands = SEM[lands_as or name][0] + index
        return pltpu.make_async_remote_copy(
            src_ref=src, dst_ref=dst, send_sem=ssem.at[slot], recv_sem=rsem.at[lands],
            device_id=device, device_id_type=MESH,
        )

    def landed(name, index, ref):
        rcopy(name, index, ref, ref, (qi, t_core)).wait_recv()

    def local(index, src, dst):
        return pltpu.make_async_copy(src, dst, lsem.at[index])

    def at_lane(start, size):
        return pl.ds(pl.multiple_of(start, 128), size)

    def at_row(start, size):
        return pl.ds(pl.multiple_of(start, 16), size)

    load_mod = local(1, mod_in, mod)
    load_mod.start()
    load_x = []
    for f, index in ((0, 0), (1, 11)):
        at = slice(f * frame, (f + 1) * frame)
        load_x.append(local(index, x_in.at[at], x0.at[at]))
        load_x[f].start()
    load_w = []
    for p in range(pairs):
        for j in (1, 2):
            load_w.append(
                local(1 + 2 * p + j, w_in.at[j, :, p * 128 : (p + 1) * 128],
                      wkv.at[p, :, (j - 1) * 128 : j * 128])
            )
    load_w.append(local(8, w_in.at[0], wq))
    my_half = at_lane(core * half, half)
    other_half = at_lane((1 - core) * half, half)
    load_wout = local(9, wout_in.at[:, my_half], wfull.at[at_row(ti * heads_width, heads_width)])

    last = local(10, fresh.at[1], out.at[frame:rows])
    load_f = local(12, fresh.at[0], xf)

    @pl.when(final)
    def _():
        load_f.start()
        last.start()

    barrier = pltpu.get_barrier_semaphore()
    partners = [
        (up, ti), (down, ti), (qi, t_core), (qi, t_y),
        (across, t_y), (across, t_far), (x_up, ti), (x_down, ti), (mirror, ti), (across, ti),
    ]
    for device in partners:
        pl.semaphore_signal(barrier, inc=1, device_id=device, device_id_type=MESH)
    pl.semaphore_wait(barrier, len(partners))

    sends = []

    def send(name, index, src, dst, device):
        copy = rcopy(name, index, src, dst, device)
        copy.start()
        sends.append((None, copy))
        return copy

    def send_if(cond, name, index, src, dst, device):
        copy = rcopy(name, index, src, dst, device)

        @pl.when(cond)
        def _():
            copy.start()

        sends.append((cond, copy))

    piece = heads_width // 4

    def my_piece(k):
        return lax.rem(x_pos + k, 4) * piece

    def wout_rows(t, k):
        return wfull.at[at_row(t * heads_width + my_piece(k), piece)]

    def wout_src(k, columns):
        return wout_in.at[at_row(my_piece(k), piece), columns]

    send("wout_y", 0, wout_src(0, my_half), wout_rows(ti, 0), (across, t_y))
    send("wout_y", 1, wout_src(0, other_half), wout_rows(ti, 0), (across, t_far))
    send("wout_core", 0, wout_in.at[:, other_half],
         wfull.at[at_row(ti * heads_width, heads_width)], (qi, t_core))
    send("wout_y", 2, wout_src(2, my_half), wout_rows(ti, 2), (across, t_y))
    send("wout_y", 3, wout_src(2, other_half), wout_rows(ti, 2), (across, t_far))

    def forward_wout():
        for i, t in enumerate((t_y, t_far)):
            landed("wout_y", i, wout_rows(t, 0))
            send("wout_x", i, wout_rows(t, 0), wout_rows(t, 0), (x_up, ti))
            send("wout_x", 2 + i, wout_rows(t, 0), wout_rows(t, 0), (x_down, ti))

    def finish_wout():
        load_wout.wait()
        landed("wout_core", 0, wfull.at[at_row(t_core * heads_width, heads_width)])
        for i, t in enumerate((t_y, t_far)):
            landed("wout_y", 2 + i, wout_rows(t, 2))
            landed("wout_x", i, wout_rows(t, 3))
            landed("wout_x", 2 + i, wout_rows(t, 1))

    row_head = lax.broadcasted_iota(jnp.int32, (128, 128), 0) >> 6
    col_head = lax.broadcasted_iota(jnp.int32, (128, 128), 1) >> 6
    head_mean = jnp.where(row_head == col_head, 1.0 / 64.0, 0.0).astype(BF16)

    def head_norm(values, gain_row):
        high = values.astype(BF16)
        low = (values - high.astype(F32)).astype(BF16)
        mean = jnp.dot(high, head_mean, preferred_element_type=F32)
        mean = mean + jnp.dot(low, head_mean, preferred_element_type=F32)
        centered = values - mean
        var = jnp.dot((centered * centered).astype(BF16), head_mean, preferred_element_type=F32)
        return (centered * lax.rsqrt(var + EPS) * gain_row).astype(BF16)

    for f in range(2):
        slot0[f, 3:4, :] = jnp.full((1, width), sampler[0, levels[f]], F32)
        slot0[f, 4:5, :] = jnp.full((1, width), sampler[1, levels[f]], F32)
        slot0[f, 5:8, :] = jnp.full((3, width), window_start[f].astype(F32), F32)
    load_mod.wait()
    for f in range(2):
        for j in range(3):
            slot0[f, j : j + 1, :] = mod[j, pl.ds(levels[f], 1), :]
    send_if(not_final, "meta", 0, slot0.at[1], slot1, (up, ti))

    @pl.when(first)
    def _():
        slot1[...] = slot0[0]

    def norm_rows(src, param, f):
        chunk = 64

        @pl.loop(0, frame // chunk)
        def _(i):
            at = pl.ds(pl.multiple_of(f * frame + i * chunk, chunk), chunk)
            mean = jnp.mean(src[at, :].astype(F32), axis=-1, keepdims=True)
            centered = src[at, :].astype(F32) - mean
            var = jnp.mean(centered * centered, axis=-1, keepdims=True)
            normed = (src[at, :].astype(F32) - mean) * lax.rsqrt(var + EPS)
            h[at, :] = (normed * (1.0 + param[1:2, :]) + param[0:1, :]).astype(BF16)

    def store_kv(kv, p, f, acc):
        kv[f + 2, :, 0:128] = head_norm(acc[:, :128], gain[1:2, p * 128 : (p + 1) * 128])
        kv[f + 2, :, 128:256] = acc[:, 128:].astype(BF16)

    def store_q(to, acc):
        for p in range(pairs):
            cols = slice(p * 128, (p + 1) * 128)
            to[:, cols] = head_norm(acc[:, cols], gain[0:1, cols]) * jnp.asarray(0.125, BF16)

    def project(kvs, send_halo, wait_weights):
        def product(p):
            wait_weights(p)
            weight = wq[...] if p == pairs else wkv[p]
            return jnp.dot(h[...], weight, preferred_element_type=F32)

        ahead = product(0)
        for p in range(pairs):
            acc = ahead
            if p > 0:
                ahead = product(p + 1)
            for f in range(2):
                store_kv(kvs[p], p, f, acc[f * frame : (f + 1) * frame])
            send_halo(p)
            if p == 0:
                ahead = product(1)
        store_q(q, ahead)

    q_chunk = 128
    first_head = lax.broadcasted_iota(jnp.int32, (q_chunk, 128), 1) < 64
    zeros = jnp.zeros((q_chunk, 128), BF16)
    ones = jnp.ones((WIN * frame, 128), BF16)

    def attend(kv, p, f, window, flag, queries, attn):
        fixed, second, if_set, if_clear = window
        chosen = jnp.where(flag, kv[if_set].astype(F32), kv[if_clear].astype(F32)).astype(BF16)
        keys = jnp.concatenate([kv[fixed, :, 0:128], kv[second, :, 0:128], chosen[:, 0:128]], axis=0)
        values = jnp.concatenate(
            [kv[fixed, :, 128:256], kv[second, :, 128:256], chosen[:, 128:256]], axis=0
        )
        values = jnp.concatenate([values, ones], axis=1)

        def scores_of(i):
            start = f * frame + i * q_chunk
            rows_q = queries[start : start + q_chunk, p * 128 : (p + 1) * 128]
            both = jnp.concatenate(
                [jnp.where(first_head, rows_q, zeros), jnp.where(first_head, zeros, rows_q)], axis=0
            )
            return lax.dot_general(
                both, keys, (((1,), (1,)), ((), ())), preferred_element_type=F32
            )

        n = frame // q_chunk
        ahead = scores_of(0)
        for i in range(n):
            scores = ahead
            if i + 1 < n:
                ahead = scores_of(i + 1)
            top = jnp.max(scores, axis=-1, keepdims=True)
            expo = jnp.exp(scores - top).astype(BF16)
            total = jnp.dot(expo, values, preferred_element_type=F32)
            picked = jnp.where(
                jnp.concatenate([first_head, first_head], axis=1), total[:q_chunk], total[q_chunk:]
            )
            start = f * frame + i * q_chunk
            attn[start : start + q_chunk, at_lane(ti * heads_width + p * 128, 128)] = (
                picked[:, :128] / picked[:, 128:]
            ).astype(BF16)

    def attn_block(attn, t, p, f):
        return attn.at[f * frame : (f + 1) * frame, at_lane(t * heads_width + p * 128, 128)]

    def attn_slot(step, p, f):
        return step * 6 + p * 2 + f

    def share_attn(step, attn, p, f):
        mine = attn_block(attn, ti, p, f)
        send("attn_y", attn_slot(step, p, f), mine, mine, (qi, t_y))
        send("attn_core", attn_slot(step, p, f), mine, mine, (qi, t_core))

    def forward_attn(step, attn, p, f):
        block = attn_block(attn, t_y, p, f)
        landed("attn_y", attn_slot(step, p, f), block)
        send("attn_fwd", attn_slot(step, p, f), block, block, (qi, t_core))

    def finish_attn(step, attn, f):
        for p in range(pairs):
            landed("attn_core", attn_slot(step, p, f), attn_block(attn, t_core, p, f))
            landed("attn_fwd", attn_slot(step, p, f), attn_block(attn, t_far, p, f))

    def update(values, branch, param, columns):
        values = values.astype(F32)
        noise_pred = values + param[2:3, columns] * branch
        return (param[3:4, columns] * values + param[4:5, columns] * noise_pred).astype(BF16)

    kv0 = (kv00, kv01, kv02)
    kv1 = (kv10, kv11, kv12)
    param0 = (slot0.at[0], slot0.at[1])
    param1 = (slot1, slot0.at[0])
    window0 = (
        (2, jnp.where(first, 4, 1), 3, 0),
        (3, jnp.where(final, 1, 4), 5, 2),
    )
    window1 = ((2, 3, 4, 1), (3, 2, 4, 1))

    def starts_from(param, slot):
        start = jnp.concatenate([param[5:6, 0:128]] * 2, axis=1)
        return start >= slot.astype(F32)

    for f in range(2):
        load_x[f].wait()
        if f == 1:
            for load in load_w + [load_wout]:
                load.start()
        norm_rows(x0, param0[f], f)

    def send_halo0(p):
        own = kv0[p].at[2:4]
        send_if(not_final, "halo_up", p, own, kv0[p].at[0:2], (up, ti))
        send_if(not_first, "halo_down", p, own, kv0[p].at[4:6], (down, ti))

    def wait_weights(p):
        if p == pairs:
            load_w[2 * pairs].wait()
        else:
            load_w[2 * p].wait()
            load_w[2 * p + 1].wait()

    project(kv0, send_halo0, wait_weights)

    @pl.when(final)
    def _():
        load_f.wait()
        norm_rows(xf, slot0.at[1], 0)
        for p in range(pairs):
            store_kv(kv1[p], p, 2, jnp.dot(h[0:frame], wkv[p], preferred_element_type=F32))
        store_q(qf, jnp.dot(h[0:frame], wq[...], preferred_element_type=F32))

    for p in range(pairs):
        if p == 1:
            forward_wout()

        @pl.when(not_first)
        def _():
            landed("halo_up", p, kv0[p].at[0:2])

        @pl.when(not_final)
        def _():
            landed("halo_down", p, kv0[p].at[4:6])

        for f in range(2):
            attend(kv0[p], p, f, window0[f], starts_from(param0[f], 2 * qi - 1 + 2 * f), q, attn0)
            share_attn(0, attn0, p, f)
            if p > 0:
                forward_attn(0, attn0, p - 1, f)
    finish_wout()
    for f in range(2):
        forward_attn(0, attn0, pairs - 1, f)
    for f in range(2):
        finish_attn(0, attn0, f)

    n_cols = 256

    @pl.loop(0, half // n_cols)
    def _(n):
        columns = at_lane(core * half + n * n_cols, n_cols)
        weight = wfull[:, at_lane(n * n_cols, n_cols)]
        for f in range(2):
            at = slice(f * frame, (f + 1) * frame)
            branch = jnp.dot(attn0[at, :], weight, preferred_element_type=F32)
            x1[at, columns] = update(x0[at, columns], branch, param0[f], columns)
        rcopy("gather", n, x1.at[:, columns], x1.at[:, columns], (qi, t_core)).start()

    @pl.loop(0, half // n_cols)
    def _(n):
        theirs = at_lane((1 - core) * half + n * n_cols, n_cols)
        columns = at_lane(core * half + n * n_cols, n_cols)
        rcopy("gather", n, x1.at[:, columns], x1.at[:, theirs], (qi, t_core)).wait_send()
        landed("gather", n, x1.at[:, theirs])

    @pl.when(not_first)
    def _():
        landed("meta", 0, slot1)

    for f in range(2):
        norm_rows(x1, param1[f], f)

    def send_halo1(p):
        send_if(not_final, "halo_up", 3 + p, kv1[p].at[3], kv1[p].at[1], (up, ti))
        send_if(not_first, "halo_down", 3 + p, kv1[p].at[2], kv1[p].at[4], (down, ti))

    project(kv1, send_halo1, lambda p: None)
    for p in range(pairs):
        @pl.when(not_first)
        def _():
            landed("halo_up", 3 + p, kv1[p].at[1])

        @pl.when(not_final)
        def _():
            landed("halo_down", 3 + p, kv1[p].at[4])

        for f in range(2):
            attend(kv1[p], p, f, window1[f], starts_from(param1[f], 2 * qi - 1), q, attn1)
            share_attn(1, attn1, p, f)
            if p > 0:
                forward_attn(1, attn1, p - 1, f)

    chunks = 8
    n_rows = rows // chunks
    my_quarter = core * half + chip * quarter
    y_quarter = core * half + (1 - chip) * quarter

    def out_part(j, start):
        return out.at[at_row(j * n_rows, n_rows), at_lane(start, quarter)]

    def piece_of(ref, j):
        return ref.at[j * n_rows : (j + 1) * n_rows]

    def project_out(attn, values, param, f, to):
        at = slice(f * frame, (f + 1) * frame)

        @pl.loop(0, quarter // n_cols)
        def _(n):
            columns = at_lane(my_quarter + n * n_cols, n_cols)
            inner = at_lane(n * n_cols, n_cols)
            weight = wfull[:, at_lane(chip * quarter + n * n_cols, n_cols)]
            branch = jnp.dot(attn[at, :], weight, preferred_element_type=F32)
            to[at, inner] = update(values[at, columns], branch, param, columns)

    def by_relay(j):
        return j % 4 != 0

    for f in range(2):
        forward_attn(1, attn1, pairs - 1, f)
        finish_attn(1, attn1, f)
        project_out(attn1, x1, param1[f], f, xs)
        for j in range(f * chunks // 2, (f + 1) * chunks // 2):
            direct = not_first
            if by_relay(j):
                direct = jnp.logical_and(not_first, jnp.logical_not(middle))
                send_if(middle, "relay", j, piece_of(xs, j), piece_of(relay, j), (mirror, ti))
            send_if(direct, "shift", j, piece_of(xs, j), out_part(j, my_quarter), (down, ti))

    def relayed(j):
        return rcopy("relayed", j, piece_of(relay, j), out_part(j, my_quarter), (across, ti), "shift")

    def pass_relay(j):
        landed("relay", j, piece_of(relay, j))
        relayed(j).start()

    early = [j for j in range(chunks // 2) if by_relay(j)]

    @pl.when(final)
    def _():
        blocks = []
        for p in range(pairs):
            attend(kv1[p], p, 0, (2, 3, 4, 4), starts_from(slot0.at[1], 2 * qi), qf, attnf)
            mine = attn_block(attnf, ti, p, 0)
            theirs = attn_block(attnf, t_y, p, 0)
            blocks.append((
                rcopy("attn_y", 12 + p, mine, mine, (qi, t_y)),
                rcopy("attn_core", 12 + p, mine, mine, (qi, t_core)),
                rcopy("attn_fwd", 12 + p, theirs, theirs, (qi, t_core)),
            ))
            blocks[p][0].start()
            blocks[p][1].start()
            if p < len(early):
                pass_relay(early[p])
        for p in range(pairs):
            landed("attn_y", 12 + p, attn_block(attnf, t_y, p, 0))
            blocks[p][2].start()
        for p in range(pairs):
            landed("attn_core", 12 + p, attn_block(attnf, t_core, p, 0))
            landed("attn_fwd", 12 + p, attn_block(attnf, t_far, p, 0))
        project_out(attnf, xf, slot0.at[1], 0, xsf)
        stays = local(0, xsf, out.at[0:frame, at_lane(my_quarter, quarter)])
        stays.start()
        for block in blocks:
            for copy in block:
                copy.wait_send()
        stays.wait()

    def guarded(f, action):
        if f == 0:
            action()
        else:
            pl.when(not_final)(action)

    def spread(j):
        def action():
            part = out_part(j, my_quarter)
            pl.when(not_final)(lambda: landed("shift", j, part))
            rcopy("out_y", j, part, part, (qi, t_y)).start()
            rcopy("out_core", j, part, part, (qi, t_core)).start()

        guarded(j // (chunks // 2), action)

    def pass_on(j):
        def action():
            part = out_part(j, y_quarter)
            landed("out_y", j, part)
            rcopy("out_fwd", j, part, part, (qi, t_core)).start()

        guarded(j // (chunks // 2), action)

    for j in range(chunks):
        if by_relay(j) and j not in early[:pairs]:
            pl.when(final)(functools.partial(pass_relay, j))
        spread(j)
        if j > 0:
            pass_on(j - 1)
    pass_on(chunks - 1)

    core_quarter = (1 - core) * half + chip * quarter
    far_quarter = (1 - core) * half + (1 - chip) * quarter
    for j in range(chunks):

        def action():
            landed("out_core", j, out_part(j, core_quarter))
            landed("out_fwd", j, out_part(j, far_quarter))
            mine = out_part(j, my_quarter)
            rcopy("out_y", j, mine, mine, (qi, t_y)).wait_send()
            rcopy("out_core", j, mine, mine, (qi, t_core)).wait_send()
            passed = out_part(j, y_quarter)
            rcopy("out_fwd", j, passed, passed, (qi, t_core)).wait_send()

        guarded(j // (chunks // 2), action)

    @pl.when(final)
    def _():
        last.wait()
        for j in range(chunks):
            if by_relay(j):
                relayed(j).wait_send()

    for cond, copy in sends:
        if cond is None:
            copy.wait_send()
        else:
            pl.when(cond)(copy.wait_send)


def body(
    queue_latents, fresh_noise, levels, window_start, modulation, w_qkv, qk_gain, w_out, sampler
):
    frames, frame, width = queue_latents.shape
    rows = frames * frame
    heads_width = w_out.shape[0]
    level_count = modulation.shape[0]
    any_space = pl.BlockSpec(memory_space=pl.ANY)
    smem = pl.BlockSpec(memory_space=pltpu.SMEM)
    vmem = pl.BlockSpec(memory_space=pltpu.VMEM)
    kv = pltpu.VMEM((6, frame, 256), BF16)
    result = pl.pallas_call(
        functools.partial(kernel, frame, width, heads_width),
        name="diagonal_steps",
        out_shape=jax.ShapeDtypeStruct((rows, width), BF16),
        in_specs=[any_space, any_space, smem, smem, any_space, any_space, vmem, any_space, smem],
        out_specs=any_space,
        scratch_shapes=[
            pltpu.VMEM((rows, width), BF16),
            pltpu.VMEM((rows, width), BF16),
            pltpu.VMEM((rows, width), BF16),
            pltpu.VMEM((heads_width // 128, width, 256), BF16),
            pltpu.VMEM((width, heads_width), BF16),
            pltpu.VMEM((4 * heads_width, width // 2), BF16),
            pltpu.VMEM((rows, heads_width), BF16),
            pltpu.VMEM((rows, 4 * heads_width), BF16),
            pltpu.VMEM((rows, 4 * heads_width), BF16),
            kv, kv, kv, kv, kv, kv,
            pltpu.VMEM((rows, width // 4), BF16),
            pltpu.VMEM((frame, width), BF16),
            pltpu.VMEM((frame, heads_width), BF16),
            pltpu.VMEM((frame, 4 * heads_width), BF16),
            pltpu.VMEM((frame, width // 4), BF16),
            pltpu.VMEM((rows, width // 4), BF16),
            pltpu.VMEM((3, level_count, width), F32),
            pltpu.VMEM((2, 8, width), F32),
            pltpu.VMEM((8, width), F32),
            pltpu.SemaphoreType.DMA((13,)),
            pltpu.SemaphoreType.DMA((N_SEM,)),
            pltpu.SemaphoreType.DMA((N_SEM,)),
        ],
        compiler_params=pltpu.CompilerParams(
            collective_id=0, has_side_effects=True, vmem_limit_bytes=60 * 1024 * 1024
        ),
        cost_estimate=pl.CostEstimate(
            flops=4 * rows * width * 1536 * 2, bytes_accessed=40 * 2**20, transcendentals=10**7
        ),
    )(
        queue_latents.reshape(rows, width),
        fresh_noise,
        levels,
        window_start,
        jnp.transpose(modulation, (1, 0, 2)),
        jnp.transpose(w_qkv, (1, 0, 2)),
        qk_gain,
        w_out,
        jnp.transpose(sampler, (1, 0)),
    )
    return result.reshape(frames, frame, width)


def solution(mesh):
    in_specs = (
        P("queue", None, None),
        P(),
        P("queue"),
        P("queue"),
        P(),
        P(None, None, "tensor"),
        P(None, "tensor"),
        P("tensor", None),
        P(),
    )
    out_specs = P("queue", None, None)
    return jax.shard_map(body, mesh=mesh, in_specs=in_specs, out_specs=out_specs, check_vma=False)
```

```python
import functools

import jax
import jax.numpy as jnp
from jax import lax
from jax.experimental import pallas as pl
from jax.experimental.pallas import tpu as pltpu
from jax.sharding import PartitionSpec as P

MESH = pl.DeviceIdType.MESH
BF16 = jnp.bfloat16
F32 = jnp.float32
STEPS = 2
WIN = 3
EPS = 1e-6

SEM = {}


def slots(name, count):
    SEM[name] = sum(n for _, n in SEM.values()), count


slots("halo_up", 12)
slots("halo_down", 12)
slots("attn_core", 15)
slots("attn_y", 15)
slots("attn_fwd", 15)
slots("wout_core", 1)
slots("wout_y", 4)
slots("wout_x", 4)
slots("wout_extra", 4)
slots("gather", 6)
slots("shift", 8)
slots("out_y", 8)
slots("out_core", 8)
slots("out_fwd", 8)
slots("relay", 8)
slots("relayed", 8)
slots("meta", 1)
N_SEM = sum(n for _, n in SEM.values())


def kernel(
    frame, width, heads_width,
    x_in, fresh, levels, window_start, mod_in, w_in, gain, wout_in, sampler,
    out,
    x0, x1, h, wkv, wq, wfull, q, attn0, attn1, kv0, kv1,
    xs, xf, qf, attnf, xsf, relay, mod, slot0, slot1, lsem, ssem, rsem,
):
    rows = 2 * frame
    half = width // 2
    quarter = width // 4
    pairs = heads_width // 128
    qi = lax.axis_index("queue")
    ti = lax.axis_index("tensor")
    n_queue = lax.axis_size("queue")
    core = lax.rem(ti, 2)
    chip = lax.div(ti, 2)
    t_core = chip * 2 + (1 - core)
    t_y = lax.rem(ti + 2, 4)
    t_far = 3 - ti
    up = lax.rem(qi + 1, n_queue)
    down = lax.rem(qi + n_queue - 1, n_queue)
    across = lax.rem(qi + n_queue // 2, n_queue)
    plane = lax.div(qi, 16) * 16
    x_up = plane + lax.rem(qi + 4, 16)
    x_down = plane + lax.rem(qi + 12, 16)
    x_pos = lax.div(lax.rem(qi, 16), 4)
    z_pos = lax.rem(qi, 4)
    first = qi == 0
    final = qi == n_queue - 1
    mirror = plane + 15 - lax.rem(qi, 16)
    middle = qi == n_queue // 2
    not_first = jnp.logical_not(first)
    not_final = jnp.logical_not(final)

    def rcopy(name, index, src, dst, device, lands_as=None):
        slot = SEM[name][0] + index
        lands = SEM[lands_as or name][0] + index
        return pltpu.make_async_remote_copy(
            src_ref=src, dst_ref=dst, send_sem=ssem.at[slot], recv_sem=rsem.at[lands],
            device_id=device, device_id_type=MESH,
        )

    def landed(name, index, ref):
        rcopy(name, index, ref, ref, (qi, t_core)).wait_recv()

    def local(index, src, dst):
        return pltpu.make_async_copy(src, dst, lsem.at[index])

    def at_lane(start, size):
        return pl.ds(pl.multiple_of(start, 128), size)

    def at_row(start, size):
        return pl.ds(pl.multiple_of(start, 16), size)

    load_mod = local(1, mod_in, mod)
    load_mod.start()
    load_x = []
    for c in range(4):
        at = slice(c * frame // 2, (c + 1) * frame // 2)
        load_x.append(local((0, 11, 13, 14)[c], x_in.at[at], x0.at[at]))
        load_x[c].start()
    load_w = []
    for p in range(pairs):
        for j in (1, 2):
            load_w.append(
                local(1 + 2 * p + j, w_in.at[j, :, p * 128 : (p + 1) * 128],
                      wkv.at[:, p * 256 + (j - 1) * 128 : p * 256 + j * 128])
            )
    load_w.append(local(8, w_in.at[0], wq))
    for load in load_w:
        load.start()
    my_half = at_lane(core * half, half)
    other_half = at_lane((1 - core) * half, half)
    load_wout = local(9, wout_in.at[:, my_half], wfull.at[at_row(ti * heads_width, heads_width)])

    last = local(10, fresh.at[1], out.at[frame:rows])
    load_f = local(12, fresh.at[0], xf)

    @pl.when(final)
    def _():
        load_f.start()
        last.start()

    load_wout.start()
    barrier = pltpu.get_barrier_semaphore()
    partners = [
        (up, ti), (down, ti), (qi, t_core), (qi, t_y),
        (across, t_y), (across, t_far), (x_up, ti), (x_down, ti), (mirror, ti), (across, ti),
    ]
    for device in partners:
        pl.semaphore_signal(barrier, inc=1, device_id=device, device_id_type=MESH)
    pl.semaphore_wait(barrier, len(partners))

    sends = []

    def send(name, index, src, dst, device):
        copy = rcopy(name, index, src, dst, device)
        copy.start()
        sends.append((None, copy))
        return copy

    def send_if(cond, name, index, src, dst, device, lands_as=None):
        copy = rcopy(name, index, src, dst, device, lands_as)

        @pl.when(cond)
        def _():
            copy.start()

        sends.append((cond, copy))

    piece = heads_width // 4

    def my_piece(k):
        return lax.rem(x_pos + k, 4) * piece

    def wout_rows(t, k):
        return wfull.at[at_row(t * heads_width + my_piece(k), piece)]

    def wout_src(k, columns):
        return wout_in.at[at_row(my_piece(k), piece), columns]

    send("wout_y", 0, wout_src(0, my_half), wout_rows(ti, 0), (across, t_y))
    send("wout_y", 1, wout_src(0, other_half), wout_rows(ti, 0), (across, t_far))
    send("wout_core", 0, wout_in.at[:, other_half],
         wfull.at[at_row(ti * heads_width, heads_width)], (qi, t_core))
    send("wout_y", 2, wout_src(2, my_half), wout_rows(ti, 2), (across, t_y))
    send("wout_y", 3, wout_src(2, other_half), wout_rows(ti, 2), (across, t_far))

    at_bottom = z_pos == 0
    at_top = z_pos == 3
    for cond, k, index in ((at_top, 3, 0), (at_bottom, 1, 2)):
        for i, (columns, t) in enumerate(((my_half, t_y), (other_half, t_far))):
            send_if(cond, "wout_extra", index + i, wout_src(k, columns), wout_rows(ti, k),
                    (across, t), "wout_x")

    def forward_wout():
        for i, t in enumerate((t_y, t_far)):
            landed("wout_y", i, wout_rows(t, 0))
            mine = wout_rows(t, 0)
            send_if(jnp.logical_not(at_top), "wout_x", i, mine, mine, (x_up, ti))
            send_if(jnp.logical_not(at_bottom), "wout_x", 2 + i, mine, mine, (x_down, ti))

    def finish_wout():
        load_wout.wait()
        landed("wout_core", 0, wfull.at[at_row(t_core * heads_width, heads_width)])
        for i, t in enumerate((t_y, t_far)):
            landed("wout_y", 2 + i, wout_rows(t, 2))
            landed("wout_x", i, wout_rows(t, 3))
            landed("wout_x", 2 + i, wout_rows(t, 1))

    row_head = lax.broadcasted_iota(jnp.int32, (128, 128), 0) >> 6
    col_head = lax.broadcasted_iota(jnp.int32, (128, 128), 1) >> 6
    head_mean = jnp.where(row_head == col_head, 1.0 / 64.0, 0.0).astype(BF16)

    def head_norm(values, gain_row):
        high = values.astype(BF16)
        low = (values - high.astype(F32)).astype(BF16)
        mean = jnp.dot(high, head_mean, preferred_element_type=F32)
        mean = mean + jnp.dot(low, head_mean, preferred_element_type=F32)
        centered = values - mean
        var = jnp.dot((centered * centered).astype(BF16), head_mean, preferred_element_type=F32)
        return (centered * lax.rsqrt(var + EPS) * gain_row).astype(BF16)

    for f in range(2):
        slot0[f, 3:4, :] = jnp.full((1, width), sampler[0, levels[f]], F32)
        slot0[f, 4:5, :] = jnp.full((1, width), sampler[1, levels[f]], F32)
        slot0[f, 5:8, :] = jnp.full((3, width), window_start[f].astype(F32), F32)
    load_mod.wait()
    for f in range(2):
        for j in range(3):
            slot0[f, j : j + 1, :] = mod[j, pl.ds(levels[f], 1), :]
    send_if(not_final, "meta", 0, slot0.at[1], slot1, (up, ti))

    @pl.when(first)
    def _():
        slot1[...] = slot0[0]

    def norm_rows(src, param, start, count):
        chunk = 64
        for i in range(count // chunk):
            at = slice(start + i * chunk, start + (i + 1) * chunk)
            mean = jnp.mean(src[at, :].astype(F32), axis=-1, keepdims=True)
            centered = src[at, :].astype(F32) - mean
            var = jnp.mean(centered * centered, axis=-1, keepdims=True)
            normed = (src[at, :].astype(F32) - mean) * lax.rsqrt(var + EPS)
            h[at, :] = (normed * (1.0 + param[1:2, :]) + param[0:1, :]).astype(BF16)

    def store_kv(kv, p, slot, at, acc):
        kv[slot, at, p * 256 : p * 256 + 128] = head_norm(
            acc[:, :128], gain[1:2, p * 128 : (p + 1) * 128]
        )
        kv[slot, at, p * 256 + 128 : (p + 1) * 256] = acc[:, 128:].astype(BF16)

    def store_q(to, acc):
        for p in range(pairs):
            cols = slice(p * 128, (p + 1) * 128)
            to[:, cols] = head_norm(acc[:, cols], gain[0:1, cols]) * jnp.asarray(0.125, BF16)

    part = frame // 2

    def project(src, params, order, kv, send_halo):
        if load_w:
            load_x[order[0]].wait()
        norm_rows(src, params[order[0] // 2], order[0] * part, part)
        if load_w:
            for load in load_w[: 2 * pairs]:
                load.wait()
        for i, c in enumerate(order):
            if i + 1 < len(order):
                after = order[i + 1]
                if load_w:
                    load_x[after].wait()
                norm_rows(src, params[after // 2], after * part, part)
            f = c // 2
            at = slice((c % 2) * part, (c % 2 + 1) * part)
            acc = jnp.dot(
                h[c * part : (c + 1) * part, :], wkv[...], preferred_element_type=F32
            )
            for p in range(pairs):
                store_kv(kv, p, f + 2, at, acc[:, p * 256 : (p + 1) * 256])
            send_halo(i, f, at)
        if load_w:
            load_w[2 * pairs].wait()
            load_w.clear()
        store_q(q, jnp.dot(h[...], wq[...], preferred_element_type=F32))

    q_chunk = 128
    first_head = lax.broadcasted_iota(jnp.int32, (q_chunk, 128), 1) < 64
    zeros = jnp.zeros((q_chunk, 128), BF16)
    ones = jnp.ones((WIN * frame, 128), BF16)

    def attend(kv, p, f, window, flag, queries, attn):
        fixed, second, if_set, if_clear = window
        lanes = slice(p * 256, (p + 1) * 256)
        k_lanes = slice(p * 256, p * 256 + 128)
        v_lanes = slice(p * 256 + 128, (p + 1) * 256)
        chosen = jnp.where(
            flag, kv[if_set, :, lanes].astype(F32), kv[if_clear, :, lanes].astype(F32)
        ).astype(BF16)
        keys = jnp.concatenate(
            [kv[fixed, :, k_lanes], kv[second, :, k_lanes], chosen[:, :128]], axis=0
        )
        values = jnp.concatenate(
            [kv[fixed, :, v_lanes], kv[second, :, v_lanes], chosen[:, 128:]], axis=0
        )
        values = jnp.concatenate([values, ones], axis=1)

        def scores_of(i):
            start = f * frame + i * q_chunk
            rows_q = queries[start : start + q_chunk, p * 128 : (p + 1) * 128]
            both = jnp.concatenate(
                [jnp.where(first_head, rows_q, zeros), jnp.where(first_head, zeros, rows_q)], axis=0
            )
            return lax.dot_general(
                both, keys, (((1,), (1,)), ((), ())), preferred_element_type=F32
            )

        n = frame // q_chunk
        ahead = scores_of(0)
        for i in range(n):
            scores = ahead
            if i + 1 < n:
                ahead = scores_of(i + 1)
            top = jnp.max(scores, axis=-1, keepdims=True)
            expo = jnp.exp(scores - top).astype(BF16)
            total = jnp.dot(expo, values, preferred_element_type=F32)
            picked = jnp.where(
                jnp.concatenate([first_head, first_head], axis=1), total[:q_chunk], total[q_chunk:]
            )
            start = f * frame + i * q_chunk
            attn[start : start + q_chunk, at_lane(ti * heads_width + p * 128, 128)] = (
                picked[:, :128] / picked[:, 128:]
            ).astype(BF16)

    def attn_block(attn, t, p, f):
        return attn.at[f * frame : (f + 1) * frame, at_lane(t * heads_width + p * 128, 128)]

    def attn_slot(step, p, f):
        return step * 6 + p * 2 + f

    def share_attn(step, attn, p, f):
        mine = attn_block(attn, ti, p, f)
        send("attn_y", attn_slot(step, p, f), mine, mine, (qi, t_y))
        send("attn_core", attn_slot(step, p, f), mine, mine, (qi, t_core))

    def forward_attn(step, attn, p, f):
        block = attn_block(attn, t_y, p, f)
        landed("attn_y", attn_slot(step, p, f), block)
        send("attn_fwd", attn_slot(step, p, f), block, block, (qi, t_core))

    def finish_attn(step, attn, f):
        for p in range(pairs):
            landed("attn_core", attn_slot(step, p, f), attn_block(attn, t_core, p, f))
            landed("attn_fwd", attn_slot(step, p, f), attn_block(attn, t_far, p, f))

    def update(values, branch, param, columns):
        values = values.astype(F32)
        noise_pred = values + param[2:3, columns] * branch
        return (param[3:4, columns] * values + param[4:5, columns] * noise_pred).astype(BF16)

    param0 = (slot0.at[0], slot0.at[1])
    param1 = (slot1, slot0.at[0])
    window0 = (
        (2, jnp.where(first, 4, 1), 3, 0),
        (3, jnp.where(final, 1, 4), 5, 2),
    )
    window1 = ((2, 3, 4, 1), (3, 2, 4, 1))

    def starts_from(param, slot):
        start = jnp.concatenate([param[5:6, 0:128]] * 2, axis=1)
        return start >= slot.astype(F32)

    def cut(kv, slots_of, at, p):
        lanes = slice(0, 2 * heads_width) if p is None else slice(p * 256, (p + 1) * 256)
        return kv.at[slots_of, at, lanes]

    def send_halo0(i, f, at):
        full = slice(0, frame)
        jobs = [(0, f, at, None)] if i == 0 else [(i, f, at, 0)]
        if i == 3:
            for p in range(1, pairs):
                jobs += [(2 * p + 2, 0, half_of(1), p), (2 * p + 3, 1, full, p)]
        for index, g, rows_at, p in jobs:
            own = cut(kv0, g + 2, rows_at, p)
            send_if(not_final, "halo_up", index, own, cut(kv0, g, rows_at, p), (up, ti))
            send_if(not_first, "halo_down", index, own, cut(kv0, g + 4, rows_at, p), (down, ti))

    def half_of(c):
        return slice((c % 2) * part, (c % 2 + 1) * part)

    def land_halo0(p):
        def land(name, base):
            if p == 0:
                landed(name, 0, cut(kv0, base, half_of(0), None))
                for c in (1, 2, 3):
                    landed(name, c, cut(kv0, base + c // 2, half_of(c), 0))
            else:
                landed(name, 2 * p + 2, cut(kv0, base, half_of(1), p))
                landed(name, 2 * p + 3, cut(kv0, base + 1, slice(0, frame), p))

        pl.when(not_first)(lambda: land("halo_up", 0))
        pl.when(not_final)(lambda: land("halo_down", 4))

    project(x0, param0, (0, 1, 2, 3), kv0, send_halo0)

    @pl.when(final)
    def _():
        load_f.wait()
        norm_rows(xf, slot0.at[1], 0, frame)
        entering = jnp.dot(h[0:frame, :], wkv[...], preferred_element_type=F32)
        for p in range(pairs):
            store_kv(kv1, p, 4, slice(0, frame), entering[:, p * 256 : (p + 1) * 256])
        store_q(qf, jnp.dot(h[0:frame, :], wq[...], preferred_element_type=F32))

    lag = 2
    done = []
    for p in range(pairs):
        if p == 1:
            forward_wout()
        land_halo0(p)
        for f in range(2):
            attend(kv0, p, f, window0[f], starts_from(param0[f], 2 * qi - 1 + 2 * f), q, attn0)
            share_attn(0, attn0, p, f)
            done.append((p, f))
            if len(done) > lag:
                forward_attn(0, attn0, *done[-1 - lag])
    finish_wout()
    for piece in done[-lag:]:
        forward_attn(0, attn0, *piece)
    for f in range(2):
        finish_attn(0, attn0, f)

    n_cols = 256

    @pl.loop(0, half // n_cols)
    def _(n):
        columns = at_lane(core * half + n * n_cols, n_cols)
        weight = wfull[:, at_lane(n * n_cols, n_cols)]
        for f in range(2):
            at = slice(f * frame, (f + 1) * frame)
            branch = jnp.dot(attn0[at, :], weight, preferred_element_type=F32)
            x1[at, columns] = update(x0[at, columns], branch, param0[f], columns)
        rcopy("gather", n, x1.at[:, columns], x1.at[:, columns], (qi, t_core)).start()

    @pl.loop(0, half // n_cols)
    def _(n):
        theirs = at_lane((1 - core) * half + n * n_cols, n_cols)
        columns = at_lane(core * half + n * n_cols, n_cols)
        rcopy("gather", n, x1.at[:, columns], x1.at[:, theirs], (qi, t_core)).wait_send()
        landed("gather", n, x1.at[:, theirs])

    @pl.when(not_first)
    def _():
        landed("meta", 0, slot1)


    def send_halo1(i, f, at):
        last_one = i >= 2
        for p in range(pairs) if last_one else [None]:
            index = 8 + (0 if p is None else p + 1)
            own = cut(kv1, f + 2, at, p)
            if f == 1:
                send_if(not_final, "halo_up", index, own, cut(kv1, 1, at, p), (up, ti))
            else:
                send_if(not_first, "halo_down", index, own, cut(kv1, 4, at, p), (down, ti))

    def land_halo1(p):
        def land(name, slot):
            if p == 0:
                landed(name, 8, cut(kv1, slot, half_of(0), None))
            landed(name, 9 + p, cut(kv1, slot, half_of(1), p))

        pl.when(not_first)(lambda: land("halo_up", 1))
        pl.when(not_final)(lambda: land("halo_down", 4))

    project(x1, param1, (0, 2, 1, 3), kv1, send_halo1)
    done = []
    for f in range(2):
        for p in range(pairs):
            if f == 0:
                land_halo1(p)
            attend(kv1, p, f, window1[f], starts_from(param1[f], 2 * qi - 1), q, attn1)
            share_attn(1, attn1, p, f)
            done.append((p, f))
            if len(done) > lag:
                forward_attn(1, attn1, *done[-1 - lag])

    chunks = 8
    n_rows = rows // chunks
    my_quarter = core * half + chip * quarter
    y_quarter = core * half + (1 - chip) * quarter

    def out_part(j, start):
        return out.at[at_row(j * n_rows, n_rows), at_lane(start, quarter)]

    def piece_of(ref, j):
        return ref.at[j * n_rows : (j + 1) * n_rows]

    def project_out(attn, values, param, f, to):
        at = slice(f * frame, (f + 1) * frame)

        @pl.loop(0, quarter // n_cols)
        def _(n):
            columns = at_lane(my_quarter + n * n_cols, n_cols)
            inner = at_lane(n * n_cols, n_cols)
            weight = wfull[:, at_lane(chip * quarter + n * n_cols, n_cols)]
            branch = jnp.dot(attn[at, :], weight, preferred_element_type=F32)
            to[at, inner] = update(values[at, columns], branch, param, columns)

    by_last = (3, 6, 7)
    by_first = (2, 5)

    for f in range(2):
        if f == 1:
            for piece in done[-lag:]:
                forward_attn(1, attn1, *piece)
        finish_attn(1, attn1, f)
        project_out(attn1, x1, param1[f], f, xs)
        for j in range(f * chunks // 2, (f + 1) * chunks // 2):
            direct = not_first
            if j in by_last + by_first:
                direct = jnp.logical_and(not_first, jnp.logical_not(middle))
                by = mirror if j in by_last else across
                send_if(middle, "relay", j, piece_of(xs, j), piece_of(relay, j), (by, ti))
            send_if(direct, "shift", j, piece_of(xs, j), out_part(j, my_quarter), (down, ti))

    def relayed(j):
        to = across if j in by_last else mirror
        return rcopy("relayed", j, piece_of(relay, j), out_part(j, my_quarter), (to, ti), "shift")

    def pass_relay(j):
        landed("relay", j, piece_of(relay, j))
        relayed(j).start()

    @pl.when(final)
    def _():
        blocks = []
        for p in range(pairs):
            attend(kv1, p, 0, (2, 3, 4, 4), starts_from(slot0.at[1], 2 * qi), qf, attnf)
            mine = attn_block(attnf, ti, p, 0)
            theirs = attn_block(attnf, t_y, p, 0)
            blocks.append((
                rcopy("attn_y", 12 + p, mine, mine, (qi, t_y)),
                rcopy("attn_core", 12 + p, mine, mine, (qi, t_core)),
                rcopy("attn_fwd", 12 + p, theirs, theirs, (qi, t_core)),
            ))
            blocks[p][0].start()
            blocks[p][1].start()
            if p == pairs - 1:
                pass_relay(by_last[0])
        for p in range(pairs):
            landed("attn_y", 12 + p, attn_block(attnf, t_y, p, 0))
            blocks[p][2].start()
        for p in range(pairs):
            landed("attn_core", 12 + p, attn_block(attnf, t_core, p, 0))
            landed("attn_fwd", 12 + p, attn_block(attnf, t_far, p, 0))
        project_out(attnf, xf, slot0.at[1], 0, xsf)
        stays = local(0, xsf, out.at[0:frame, at_lane(my_quarter, quarter)])
        stays.start()
        for block in blocks:
            for copy in block:
                copy.wait_send()
        stays.wait()

    def guarded(f, action):
        if f == 0:
            action()
        else:
            pl.when(not_final)(action)

    def spread(j):
        part = out_part(j, my_quarter)
        rcopy("out_y", j, part, part, (qi, t_y)).start()
        rcopy("out_core", j, part, part, (qi, t_core)).start()

    def pass_on(j):
        part = out_part(j, y_quarter)
        landed("out_y", j, part)
        rcopy("out_fwd", j, part, part, (qi, t_core)).start()

    @pl.when(final)
    def _():
        for j in range(chunks // 2):
            spread(j)
        for j in by_last[1:]:
            pass_relay(j)
        for j in range(chunks // 2):
            pass_on(j)

    @pl.when(not_final)
    def _():
        for j in range(chunks):
            if j in (0, 4):
                pl.when(first)(functools.partial(pass_relay, by_first[j // 4]))
            landed("shift", j, out_part(j, my_quarter))
            spread(j)
            if j > 0:
                pass_on(j - 1)
        pass_on(chunks - 1)

    core_quarter = (1 - core) * half + chip * quarter
    far_quarter = (1 - core) * half + (1 - chip) * quarter
    for j in range(chunks):

        def action():
            landed("out_core", j, out_part(j, core_quarter))
            landed("out_fwd", j, out_part(j, far_quarter))
            mine = out_part(j, my_quarter)
            rcopy("out_y", j, mine, mine, (qi, t_y)).wait_send()
            rcopy("out_core", j, mine, mine, (qi, t_core)).wait_send()
            passed = out_part(j, y_quarter)
            rcopy("out_fwd", j, passed, passed, (qi, t_core)).wait_send()

        guarded(j // (chunks // 2), action)

    @pl.when(final)
    def _():
        last.wait()
        for j in by_last:
            relayed(j).wait_send()

    @pl.when(first)
    def _():
        for j in by_first:
            relayed(j).wait_send()

    for cond, copy in sends:
        if cond is None:
            copy.wait_send()
        else:
            pl.when(cond)(copy.wait_send)


def body(
    queue_latents, fresh_noise, levels, window_start, modulation, w_qkv, qk_gain, w_out, sampler
):
    frames, frame, width = queue_latents.shape
    rows = frames * frame
    heads_width = w_out.shape[0]
    level_count = modulation.shape[0]
    any_space = pl.BlockSpec(memory_space=pl.ANY)
    smem = pl.BlockSpec(memory_space=pltpu.SMEM)
    vmem = pl.BlockSpec(memory_space=pltpu.VMEM)
    kv = pltpu.VMEM((6, frame, 2 * heads_width), BF16)
    result = pl.pallas_call(
        functools.partial(kernel, frame, width, heads_width),
        name="diagonal_steps",
        out_shape=jax.ShapeDtypeStruct((rows, width), BF16),
        in_specs=[any_space, any_space, smem, smem, any_space, any_space, vmem, any_space, smem],
        out_specs=any_space,
        scratch_shapes=[
            pltpu.VMEM((rows, width), BF16),
            pltpu.VMEM((rows, width), BF16),
            pltpu.VMEM((rows, width), BF16),
            pltpu.VMEM((width, 2 * heads_width), BF16),
            pltpu.VMEM((width, heads_width), BF16),
            pltpu.VMEM((4 * heads_width, width // 2), BF16),
            pltpu.VMEM((rows, heads_width), BF16),
            pltpu.VMEM((rows, 4 * heads_width), BF16),
            pltpu.VMEM((rows, 4 * heads_width), BF16),
            kv, kv,
            pltpu.VMEM((rows, width // 4), BF16),
            pltpu.VMEM((frame, width), BF16),
            pltpu.VMEM((frame, heads_width), BF16),
            pltpu.VMEM((frame, 4 * heads_width), BF16),
            pltpu.VMEM((frame, width // 4), BF16),
            pltpu.VMEM((rows, width // 4), BF16),
            pltpu.VMEM((3, level_count, width), F32),
            pltpu.VMEM((2, 8, width), F32),
            pltpu.VMEM((8, width), F32),
            pltpu.SemaphoreType.DMA((15,)),
            pltpu.SemaphoreType.DMA((N_SEM,)),
            pltpu.SemaphoreType.DMA((N_SEM,)),
        ],
        compiler_params=pltpu.CompilerParams(
            collective_id=0, has_side_effects=True, vmem_limit_bytes=60 * 1024 * 1024
        ),
        cost_estimate=pl.CostEstimate(
            flops=4 * rows * width * 1536 * 2, bytes_accessed=40 * 2**20, transcendentals=10**7
        ),
    )(
        queue_latents.reshape(rows, width),
        fresh_noise,
        levels,
        window_start,
        jnp.transpose(modulation, (1, 0, 2)),
        jnp.transpose(w_qkv, (1, 0, 2)),
        qk_gain,
        w_out,
        jnp.transpose(sampler, (1, 0)),
    )
    return result.reshape(frames, frame, width)


def solution(mesh):
    in_specs = (
        P("queue", None, None),
        P(),
        P("queue"),
        P("queue"),
        P(),
        P(None, None, "tensor"),
        P(None, "tensor"),
        P("tensor", None),
        P(),
    )
    out_specs = P("queue", None, None)
    return jax.shard_map(body, mesh=mesh, in_specs=in_specs, out_specs=out_specs, check_vma=False)
```

```python
import functools

import jax
import jax.numpy as jnp
from jax import lax
from jax.experimental import pallas as pl
from jax.experimental.pallas import tpu as pltpu
from jax.sharding import PartitionSpec as P

MESH = pl.DeviceIdType.MESH
BF16 = jnp.bfloat16
F32 = jnp.float32
STEPS = 2
WIN = 3
EPS = 1e-6

SEM = {}


def slots(name, count):
    SEM[name] = sum(n for _, n in SEM.values()), count


slots("halo_up", 12)
slots("halo_down", 12)
slots("attn_core", 15)
slots("attn_y", 15)
slots("attn_fwd", 15)
slots("wout_core", 1)
slots("wout_y", 4)
slots("wout_x", 4)
slots("wout_extra", 4)
slots("gather", 6)
slots("shift", 12)
slots("out_y", 12)
slots("out_core", 12)
slots("out_fwd", 12)
slots("relay", 12)
slots("relayed", 12)
slots("meta", 1)
N_SEM = sum(n for _, n in SEM.values())


def kernel(
    frame, width, heads_width,
    x_in, fresh, levels, window_start, mod_in, w_in, gain, wout_in, sampler,
    out,
    x0, x1, h, wkv, wq, wfull, q, attn0, attn1, kv0, kv1,
    xs, xf, qf, attnf, xsf, relay, mod, slot0, slot1, lsem, ssem, rsem,
):
    rows = 2 * frame
    half = width // 2
    quarter = width // 4
    pairs = heads_width // 128
    qi = lax.axis_index("queue")
    ti = lax.axis_index("tensor")
    n_queue = lax.axis_size("queue")
    core = lax.rem(ti, 2)
    chip = lax.div(ti, 2)
    t_core = chip * 2 + (1 - core)
    t_y = lax.rem(ti + 2, 4)
    t_far = 3 - ti
    up = lax.rem(qi + 1, n_queue)
    down = lax.rem(qi + n_queue - 1, n_queue)
    across = lax.rem(qi + n_queue // 2, n_queue)
    plane = lax.div(qi, 16) * 16
    x_up = plane + lax.rem(qi + 4, 16)
    x_down = plane + lax.rem(qi + 12, 16)
    x_pos = lax.div(lax.rem(qi, 16), 4)
    z_pos = lax.rem(qi, 4)
    first = qi == 0
    final = qi == n_queue - 1
    mirror = plane + 15 - lax.rem(qi, 16)
    middle = qi == n_queue // 2
    not_first = jnp.logical_not(first)
    not_final = jnp.logical_not(final)

    def rcopy(name, index, src, dst, device, lands_as=None):
        slot = SEM[name][0] + index
        lands = SEM[lands_as or name][0] + index
        return pltpu.make_async_remote_copy(
            src_ref=src, dst_ref=dst, send_sem=ssem.at[slot], recv_sem=rsem.at[lands],
            device_id=device, device_id_type=MESH,
        )

    def landed(name, index, ref):
        rcopy(name, index, ref, ref, (qi, t_core)).wait_recv()

    def local(index, src, dst):
        return pltpu.make_async_copy(src, dst, lsem.at[index])

    def at_lane(start, size):
        return pl.ds(pl.multiple_of(start, 128), size)

    def at_row(start, size):
        return pl.ds(pl.multiple_of(start, 16), size)

    load_mod = local(1, mod_in, mod)
    load_mod.start()
    load_x = []
    for c in range(4):
        at = slice(c * frame // 2, (c + 1) * frame // 2)
        load_x.append(local((0, 11, 13, 14)[c], x_in.at[at], x0.at[at]))
        load_x[c].start()
    load_w = []
    for p in range(pairs):
        for j in (1, 2):
            load_w.append(
                local(1 + 2 * p + j, w_in.at[j, :, p * 128 : (p + 1) * 128],
                      wkv.at[:, p * 256 + (j - 1) * 128 : p * 256 + j * 128])
            )
    load_w.append(local(8, w_in.at[0], wq))
    for load in load_w:
        load.start()
    my_half = at_lane(core * half, half)
    other_half = at_lane((1 - core) * half, half)
    load_wout = local(9, wout_in.at[:, my_half], wfull.at[at_row(ti * heads_width, heads_width)])

    last = local(10, fresh.at[1], out.at[frame:rows])
    load_f = local(12, fresh.at[0], xf)

    @pl.when(final)
    def _():
        load_f.start()
        last.start()

    load_wout.start()
    barrier = pltpu.get_barrier_semaphore()
    partners = [
        (up, ti), (down, ti), (qi, t_core), (qi, t_y),
        (across, t_y), (across, t_far), (x_up, ti), (x_down, ti), (mirror, ti), (across, ti),
    ]
    for device in partners:
        pl.semaphore_signal(barrier, inc=1, device_id=device, device_id_type=MESH)
    pl.semaphore_wait(barrier, len(partners))

    sends = []

    def send(name, index, src, dst, device):
        copy = rcopy(name, index, src, dst, device)
        copy.start()
        sends.append((None, copy))
        return copy

    def send_if(cond, name, index, src, dst, device, lands_as=None):
        copy = rcopy(name, index, src, dst, device, lands_as)

        @pl.when(cond)
        def _():
            copy.start()

        sends.append((cond, copy))

    piece = heads_width // 4

    def my_piece(k):
        return lax.rem(x_pos + k, 4) * piece

    def wout_rows(t, k):
        return wfull.at[at_row(t * heads_width + my_piece(k), piece)]

    def wout_src(k, columns):
        return wout_in.at[at_row(my_piece(k), piece), columns]

    send("wout_y", 0, wout_src(0, my_half), wout_rows(ti, 0), (across, t_y))
    send("wout_y", 1, wout_src(0, other_half), wout_rows(ti, 0), (across, t_far))
    send("wout_core", 0, wout_in.at[:, other_half],
         wfull.at[at_row(ti * heads_width, heads_width)], (qi, t_core))
    send("wout_y", 2, wout_src(2, my_half), wout_rows(ti, 2), (across, t_y))
    send("wout_y", 3, wout_src(2, other_half), wout_rows(ti, 2), (across, t_far))

    at_bottom = z_pos == 0
    at_top = z_pos == 3
    early_rows = piece // 3

    def wout_cut(t, k, start, count):
        return wfull.at[at_row(t * heads_width + my_piece(k) + start, count)]

    for cond, k, index in ((at_top, 3, 0), (at_bottom, 1, 2)):
        for i, (columns, t) in enumerate(((my_half, t_y), (other_half, t_far))):
            send_if(cond, "wout_extra", index + i,
                    wout_in.at[at_row(my_piece(k), early_rows), columns],
                    wout_cut(ti, k, 0, early_rows), (across, t))

    def forward_wout_late():
        for i, t in enumerate((t_y, t_far)):
            rest = wout_cut(t, 0, early_rows, piece - early_rows)
            send_if(at_top, "wout_x", i, rest, rest, (x_up, ti))
            send_if(at_bottom, "wout_x", 2 + i, rest, rest, (x_down, ti))

    def forward_wout():
        for i, t in enumerate((t_y, t_far)):
            landed("wout_y", i, wout_rows(t, 0))
            mine = wout_rows(t, 0)
            send_if(jnp.logical_not(at_top), "wout_x", i, mine, mine, (x_up, ti))
            send_if(jnp.logical_not(at_bottom), "wout_x", 2 + i, mine, mine, (x_down, ti))

    def finish_piece(cond, t, k, index):
        @pl.when(cond)
        def _():
            landed("wout_extra", index, wout_cut(t, k, 0, early_rows))
            landed("wout_x", index, wout_cut(t, k, early_rows, piece - early_rows))

        @pl.when(jnp.logical_not(cond))
        def _():
            landed("wout_x", index, wout_rows(t, k))

    def finish_wout():
        load_wout.wait()
        landed("wout_core", 0, wfull.at[at_row(t_core * heads_width, heads_width)])
        for i, t in enumerate((t_y, t_far)):
            landed("wout_y", 2 + i, wout_rows(t, 2))
            for cond, k, index in ((at_top, 3, i), (at_bottom, 1, 2 + i)):
                finish_piece(cond, t, k, index)

    row_head = lax.broadcasted_iota(jnp.int32, (128, 128), 0) >> 6
    col_head = lax.broadcasted_iota(jnp.int32, (128, 128), 1) >> 6
    head_mean = jnp.where(row_head == col_head, 1.0 / 64.0, 0.0).astype(BF16)

    def head_norm(values, gain_row):
        high = values.astype(BF16)
        low = (values - high.astype(F32)).astype(BF16)
        mean = jnp.dot(high, head_mean, preferred_element_type=F32)
        mean = mean + jnp.dot(low, head_mean, preferred_element_type=F32)
        centered = values - mean
        var = jnp.dot((centered * centered).astype(BF16), head_mean, preferred_element_type=F32)
        return (centered * lax.rsqrt(var + EPS) * gain_row).astype(BF16)

    for f in range(2):
        slot0[f, 3:4, :] = jnp.full((1, width), sampler[0, levels[f]], F32)
        slot0[f, 4:5, :] = jnp.full((1, width), sampler[1, levels[f]], F32)
        slot0[f, 5:8, :] = jnp.full((3, width), window_start[f].astype(F32), F32)
    load_mod.wait()
    for f in range(2):
        for j in range(3):
            slot0[f, j : j + 1, :] = mod[j, pl.ds(levels[f], 1), :]
    send_if(not_final, "meta", 0, slot0.at[1], slot1, (up, ti))

    @pl.when(first)
    def _():
        slot1[...] = slot0[0]

    def norm_rows(src, param, start, count):
        chunk = 64
        for i in range(count // chunk):
            at = slice(start + i * chunk, start + (i + 1) * chunk)
            mean = jnp.mean(src[at, :].astype(F32), axis=-1, keepdims=True)
            centered = src[at, :].astype(F32) - mean
            var = jnp.mean(centered * centered, axis=-1, keepdims=True)
            normed = (src[at, :].astype(F32) - mean) * lax.rsqrt(var + EPS)
            h[at, :] = (normed * (1.0 + param[1:2, :]) + param[0:1, :]).astype(BF16)

    def store_kv(kv, p, slot, at, acc):
        kv[slot, at, p * 256 : p * 256 + 128] = head_norm(
            acc[:, :128], gain[1:2, p * 128 : (p + 1) * 128]
        )
        kv[slot, at, p * 256 + 128 : (p + 1) * 256] = acc[:, 128:].astype(BF16)

    def store_q(to, acc):
        for p in range(pairs):
            cols = slice(p * 128, (p + 1) * 128)
            to[:, cols] = head_norm(acc[:, cols], gain[0:1, cols]) * jnp.asarray(0.125, BF16)

    part = frame // 2

    def project(src, params, order, kv, send_halo, ready):
        ready(order[0])
        norm_rows(src, params[order[0] // 2], order[0] * part, part)
        if load_w:
            for load in load_w[: 2 * pairs]:
                load.wait()
        for i, c in enumerate(order):
            if i + 1 < len(order):
                after = order[i + 1]
                ready(after)
                norm_rows(src, params[after // 2], after * part, part)
            f = c // 2
            at = slice((c % 2) * part, (c % 2 + 1) * part)
            acc = jnp.dot(
                h[c * part : (c + 1) * part, :], wkv[...], preferred_element_type=F32
            )
            for p in range(pairs):
                store_kv(kv, p, f + 2, at, acc[:, p * 256 : (p + 1) * 256])
            send_halo(i, f, at)
        if load_w:
            load_w[2 * pairs].wait()
            load_w.clear()
        store_q(q, jnp.dot(h[...], wq[...], preferred_element_type=F32))

    q_chunk = 128
    first_head = lax.broadcasted_iota(jnp.int32, (q_chunk, 128), 1) < 64
    zeros = jnp.zeros((q_chunk, 128), BF16)
    ones = jnp.ones((WIN * frame, 128), BF16)

    def attend(kv, p, f, window, flag, queries, attn):
        fixed, second, if_set, if_clear = window
        lanes = slice(p * 256, (p + 1) * 256)
        k_lanes = slice(p * 256, p * 256 + 128)
        v_lanes = slice(p * 256 + 128, (p + 1) * 256)
        chosen = jnp.where(
            flag, kv[if_set, :, lanes].astype(F32), kv[if_clear, :, lanes].astype(F32)
        ).astype(BF16)
        keys = jnp.concatenate(
            [kv[fixed, :, k_lanes], kv[second, :, k_lanes], chosen[:, :128]], axis=0
        )
        values = jnp.concatenate(
            [kv[fixed, :, v_lanes], kv[second, :, v_lanes], chosen[:, 128:]], axis=0
        )
        values = jnp.concatenate([values, ones], axis=1)

        def scores_of(i):
            start = f * frame + i * q_chunk
            rows_q = queries[start : start + q_chunk, p * 128 : (p + 1) * 128]
            both = jnp.concatenate(
                [jnp.where(first_head, rows_q, zeros), jnp.where(first_head, zeros, rows_q)], axis=0
            )
            return lax.dot_general(
                both, keys, (((1,), (1,)), ((), ())), preferred_element_type=F32
            )

        n = frame // q_chunk
        ahead = scores_of(0)
        for i in range(n):
            scores = ahead
            if i + 1 < n:
                ahead = scores_of(i + 1)
            top = jnp.max(scores, axis=-1, keepdims=True)
            expo = jnp.exp(scores - top).astype(BF16)
            total = jnp.dot(expo, values, preferred_element_type=F32)
            picked = jnp.where(
                jnp.concatenate([first_head, first_head], axis=1), total[:q_chunk], total[q_chunk:]
            )
            start = f * frame + i * q_chunk
            attn[start : start + q_chunk, at_lane(ti * heads_width + p * 128, 128)] = (
                picked[:, :128] / picked[:, 128:]
            ).astype(BF16)

    def attn_block(attn, t, p, f):
        return attn.at[f * frame : (f + 1) * frame, at_lane(t * heads_width + p * 128, 128)]

    def attn_slot(step, p, f):
        return step * 6 + p * 2 + f

    def share_attn(step, attn, p, f):
        mine = attn_block(attn, ti, p, f)
        send("attn_y", attn_slot(step, p, f), mine, mine, (qi, t_y))
        send("attn_core", attn_slot(step, p, f), mine, mine, (qi, t_core))

    def forward_attn(step, attn, p, f):
        block = attn_block(attn, t_y, p, f)
        landed("attn_y", attn_slot(step, p, f), block)
        send("attn_fwd", attn_slot(step, p, f), block, block, (qi, t_core))

    def finish_attn(step, attn, f):
        for p in range(pairs):
            landed("attn_core", attn_slot(step, p, f), attn_block(attn, t_core, p, f))
            landed("attn_fwd", attn_slot(step, p, f), attn_block(attn, t_far, p, f))

    def update(values, branch, param, columns):
        values = values.astype(F32)
        noise_pred = values + param[2:3, columns] * branch
        return (param[3:4, columns] * values + param[4:5, columns] * noise_pred).astype(BF16)

    param0 = (slot0.at[0], slot0.at[1])
    param1 = (slot1, slot0.at[0])
    window0 = (
        (2, jnp.where(first, 4, 1), 3, 0),
        (3, jnp.where(final, 1, 4), 5, 2),
    )
    window1 = ((2, 3, 4, 1), (3, 2, 4, 1))

    def starts_from(param, slot):
        start = jnp.concatenate([param[5:6, 0:128]] * 2, axis=1)
        return start >= slot.astype(F32)

    def cut(kv, slots_of, at, p):
        lanes = slice(0, 2 * heads_width) if p is None else slice(p * 256, (p + 1) * 256)
        return kv.at[slots_of, at, lanes]

    def send_halo0(i, f, at):
        full = slice(0, frame)
        jobs = [(0, f, at, None)] if i == 0 else [(i, f, at, 0)]
        if i == 3:
            for p in range(1, pairs):
                jobs += [(2 * p + 2, 0, half_of(1), p), (2 * p + 3, 1, full, p)]
        for index, g, rows_at, p in jobs:
            own = cut(kv0, g + 2, rows_at, p)
            send_if(not_final, "halo_up", index, own, cut(kv0, g, rows_at, p), (up, ti))
            send_if(not_first, "halo_down", index, own, cut(kv0, g + 4, rows_at, p), (down, ti))

    def half_of(c):
        return slice((c % 2) * part, (c % 2 + 1) * part)

    def land_halo0(p):
        def land(name, base):
            if p == 0:
                landed(name, 0, cut(kv0, base, half_of(0), None))
                for c in (1, 2, 3):
                    landed(name, c, cut(kv0, base + c // 2, half_of(c), 0))
            else:
                landed(name, 2 * p + 2, cut(kv0, base, half_of(1), p))
                landed(name, 2 * p + 3, cut(kv0, base + 1, slice(0, frame), p))

        pl.when(not_first)(lambda: land("halo_up", 0))
        pl.when(not_final)(lambda: land("halo_down", 4))

    project(x0, param0, (0, 1, 2, 3), kv0, send_halo0, lambda c: load_x[c].wait())

    @pl.when(final)
    def _():
        load_f.wait()
        norm_rows(xf, slot0.at[1], 0, frame)
        entering = jnp.dot(h[0:frame, :], wkv[...], preferred_element_type=F32)
        for p in range(pairs):
            store_kv(kv1, p, 4, slice(0, frame), entering[:, p * 256 : (p + 1) * 256])
        store_q(qf, jnp.dot(h[0:frame, :], wq[...], preferred_element_type=F32))

    lag = 2
    done = []
    for p in range(pairs):
        if p == 1:
            forward_wout()
        land_halo0(p)
        if p == pairs - 1:
            forward_wout_late()
        for f in range(2):
            attend(kv0, p, f, window0[f], starts_from(param0[f], 2 * qi - 1 + 2 * f), q, attn0)
            share_attn(0, attn0, p, f)
            done.append((p, f))
            if len(done) > lag:
                forward_attn(0, attn0, *done[-1 - lag])
    finish_wout()
    for piece in done[-lag:]:
        forward_attn(0, attn0, *piece)
    for f in range(2):
        finish_attn(0, attn0, f)

    n_cols = 256

    def x1_rows(c, columns):
        return x1.at[c * part : (c + 1) * part, columns]

    order1 = (0, 2, 1, 3)
    for c in order1:
        at = slice(c * part, (c + 1) * part)
        branch = jnp.dot(attn0[at, :], wfull[...], preferred_element_type=F32)
        x1[at, my_half] = update(x0[at, my_half], branch, param0[c // 2], my_half)
        send("gather", c, x1_rows(c, my_half), x1_rows(c, my_half), (qi, t_core))
    @pl.when(not_first)
    def _():
        landed("meta", 0, slot1)


    def send_halo1(i, f, at):
        last_one = i >= 2
        for p in range(pairs) if last_one else [None]:
            index = 8 + (0 if p is None else p + 1)
            own = cut(kv1, f + 2, at, p)
            if f == 1:
                send_if(not_final, "halo_up", index, own, cut(kv1, 1, at, p), (up, ti))
            else:
                send_if(not_first, "halo_down", index, own, cut(kv1, 4, at, p), (down, ti))

    def land_halo1(p):
        def land(name, slot):
            if p == 0:
                landed(name, 8, cut(kv1, slot, half_of(0), None))
            landed(name, 9 + p, cut(kv1, slot, half_of(1), p))

        pl.when(not_first)(lambda: land("halo_up", 1))
        pl.when(not_final)(lambda: land("halo_down", 4))

    project(
        x1, param1, order1, kv1, send_halo1,
        lambda c: landed("gather", c, x1_rows(c, other_half)),
    )
    done = []
    for f in range(2):
        for p in range(pairs):
            if f == 0:
                land_halo1(p)
            attend(kv1, p, f, window1[f], starts_from(param1[f], 2 * qi - 1), q, attn1)
            share_attn(1, attn1, p, f)
            done.append((p, f))
            if len(done) > lag:
                forward_attn(1, attn1, *done[-1 - lag])

    chunks = 12
    n_rows = rows // chunks
    my_quarter = core * half + chip * quarter
    y_quarter = core * half + (1 - chip) * quarter

    def out_part(j, start):
        return out.at[at_row(j * n_rows, n_rows), at_lane(start, quarter)]

    def piece_of(ref, j):
        return ref.at[j * n_rows : (j + 1) * n_rows]

    def project_out(attn, values, param, f, to):
        at = slice(f * frame, (f + 1) * frame)

        @pl.loop(0, quarter // n_cols)
        def _(n):
            columns = at_lane(my_quarter + n * n_cols, n_cols)
            inner = at_lane(n * n_cols, n_cols)
            weight = wfull[:, at_lane(chip * quarter + n * n_cols, n_cols)]
            branch = jnp.dot(attn[at, :], weight, preferred_element_type=F32)
            to[at, inner] = update(values[at, columns], branch, param, columns)

    by_last = (3, 4, 5, 9, 10, 11)
    by_first = (2, 7, 8)

    for f in range(2):
        if f == 1:
            for piece in done[-lag:]:
                forward_attn(1, attn1, *piece)
        finish_attn(1, attn1, f)
        project_out(attn1, x1, param1[f], f, xs)
        for j in range(f * chunks // 2, (f + 1) * chunks // 2):
            direct = not_first
            if j in by_last + by_first:
                direct = jnp.logical_and(not_first, jnp.logical_not(middle))
                by = mirror if j in by_last else across
                send_if(middle, "relay", j, piece_of(xs, j), piece_of(relay, j), (by, ti))
            send_if(direct, "shift", j, piece_of(xs, j), out_part(j, my_quarter), (down, ti))

    def relayed(j):
        to = across if j in by_last else mirror
        return rcopy("relayed", j, piece_of(relay, j), out_part(j, my_quarter), (to, ti), "shift")

    def pass_relay(j):
        landed("relay", j, piece_of(relay, j))
        relayed(j).start()

    @pl.when(final)
    def _():
        blocks = []
        for p in range(pairs):
            attend(kv1, p, 0, (2, 3, 4, 4), starts_from(slot0.at[1], 2 * qi), qf, attnf)
            mine = attn_block(attnf, ti, p, 0)
            theirs = attn_block(attnf, t_y, p, 0)
            blocks.append((
                rcopy("attn_y", 12 + p, mine, mine, (qi, t_y)),
                rcopy("attn_core", 12 + p, mine, mine, (qi, t_core)),
                rcopy("attn_fwd", 12 + p, theirs, theirs, (qi, t_core)),
            ))
            blocks[p][0].start()
            blocks[p][1].start()
            if p == pairs - 1:
                for j in by_last[:3]:
                    pass_relay(j)
        for p in range(pairs):
            landed("attn_y", 12 + p, attn_block(attnf, t_y, p, 0))
            blocks[p][2].start()
        for p in range(pairs):
            landed("attn_core", 12 + p, attn_block(attnf, t_core, p, 0))
            landed("attn_fwd", 12 + p, attn_block(attnf, t_far, p, 0))
        project_out(attnf, xf, slot0.at[1], 0, xsf)
        stays = local(0, xsf, out.at[0:frame, at_lane(my_quarter, quarter)])
        stays.start()
        for block in blocks:
            for copy in block:
                copy.wait_send()
        stays.wait()

    def guarded(f, action):
        if f == 0:
            action()
        else:
            pl.when(not_final)(action)

    def spread(j):
        part = out_part(j, my_quarter)
        rcopy("out_y", j, part, part, (qi, t_y)).start()
        rcopy("out_core", j, part, part, (qi, t_core)).start()

    def pass_on(j):
        part = out_part(j, y_quarter)
        landed("out_y", j, part)
        rcopy("out_fwd", j, part, part, (qi, t_core)).start()

    @pl.when(final)
    def _():
        for j in range(chunks // 2):
            spread(j)
        for j in by_last[3:]:
            pass_relay(j)
        for j in range(chunks // 2):
            pass_on(j)

    @pl.when(not_final)
    def _():
        for j in range(chunks):
            for k in {0: by_first[:1], 4: by_first[1:]}.get(j, ()):
                pl.when(first)(functools.partial(pass_relay, k))
            landed("shift", j, out_part(j, my_quarter))
            spread(j)
            if j > 0:
                pass_on(j - 1)
        pass_on(chunks - 1)

    core_quarter = (1 - core) * half + chip * quarter
    far_quarter = (1 - core) * half + (1 - chip) * quarter
    for j in range(chunks):

        def action():
            landed("out_core", j, out_part(j, core_quarter))
            landed("out_fwd", j, out_part(j, far_quarter))
            mine = out_part(j, my_quarter)
            rcopy("out_y", j, mine, mine, (qi, t_y)).wait_send()
            rcopy("out_core", j, mine, mine, (qi, t_core)).wait_send()
            passed = out_part(j, y_quarter)
            rcopy("out_fwd", j, passed, passed, (qi, t_core)).wait_send()

        guarded(j // (chunks // 2), action)

    @pl.when(final)
    def _():
        last.wait()
        for j in by_last:
            relayed(j).wait_send()

    @pl.when(first)
    def _():
        for j in by_first:
            relayed(j).wait_send()

    for cond, copy in sends:
        if cond is None:
            copy.wait_send()
        else:
            pl.when(cond)(copy.wait_send)


def body(
    queue_latents, fresh_noise, levels, window_start, modulation, w_qkv, qk_gain, w_out, sampler
):
    frames, frame, width = queue_latents.shape
    rows = frames * frame
    heads_width = w_out.shape[0]
    level_count = modulation.shape[0]
    any_space = pl.BlockSpec(memory_space=pl.ANY)
    smem = pl.BlockSpec(memory_space=pltpu.SMEM)
    vmem = pl.BlockSpec(memory_space=pltpu.VMEM)
    kv = pltpu.VMEM((6, frame, 2 * heads_width), BF16)
    result = pl.pallas_call(
        functools.partial(kernel, frame, width, heads_width),
        name="diagonal_steps",
        out_shape=jax.ShapeDtypeStruct((rows, width), BF16),
        in_specs=[any_space, any_space, smem, smem, any_space, any_space, vmem, any_space, smem],
        out_specs=any_space,
        scratch_shapes=[
            pltpu.VMEM((rows, width), BF16),
            pltpu.VMEM((rows, width), BF16),
            pltpu.VMEM((rows, width), BF16),
            pltpu.VMEM((width, 2 * heads_width), BF16),
            pltpu.VMEM((width, heads_width), BF16),
            pltpu.VMEM((4 * heads_width, width // 2), BF16),
            pltpu.VMEM((rows, heads_width), BF16),
            pltpu.VMEM((rows, 4 * heads_width), BF16),
            pltpu.VMEM((rows, 4 * heads_width), BF16),
            kv, kv,
            pltpu.VMEM((rows, width // 4), BF16),
            pltpu.VMEM((frame, width), BF16),
            pltpu.VMEM((frame, heads_width), BF16),
            pltpu.VMEM((frame, 4 * heads_width), BF16),
            pltpu.VMEM((frame, width // 4), BF16),
            pltpu.VMEM((rows, width // 4), BF16),
            pltpu.VMEM((3, level_count, width), F32),
            pltpu.VMEM((2, 8, width), F32),
            pltpu.VMEM((8, width), F32),
            pltpu.SemaphoreType.DMA((15,)),
            pltpu.SemaphoreType.DMA((N_SEM,)),
            pltpu.SemaphoreType.DMA((N_SEM,)),
        ],
        compiler_params=pltpu.CompilerParams(
            collective_id=0, has_side_effects=True, vmem_limit_bytes=60 * 1024 * 1024
        ),
        cost_estimate=pl.CostEstimate(
            flops=4 * rows * width * 1536 * 2, bytes_accessed=40 * 2**20, transcendentals=10**7
        ),
    )(
        queue_latents.reshape(rows, width),
        fresh_noise,
        levels,
        window_start,
        jnp.transpose(modulation, (1, 0, 2)),
        jnp.transpose(w_qkv, (1, 0, 2)),
        qk_gain,
        w_out,
        jnp.transpose(sampler, (1, 0)),
    )
    return result.reshape(frames, frame, width)


def solution(mesh):
    in_specs = (
        P("queue", None, None),
        P(),
        P("queue"),
        P("queue"),
        P(),
        P(None, None, "tensor"),
        P(None, "tensor"),
        P("tensor", None),
        P(),
    )
    out_specs = P("queue", None, None)
    return jax.shard_map(body, mesh=mesh, in_specs=in_specs, out_specs=out_specs, check_vma=False)
```

```python
import functools

import jax
import jax.numpy as jnp
from jax import lax
from jax.experimental import pallas as pl
from jax.experimental.pallas import tpu as pltpu
from jax.sharding import PartitionSpec as P

MESH = pl.DeviceIdType.MESH
BF16 = jnp.bfloat16
F32 = jnp.float32
STEPS = 2
WIN = 3
EPS = 1e-6

SEM = {}


def slots(name, count):
    SEM[name] = sum(n for _, n in SEM.values()), count


slots("halo_up", 12)
slots("halo_down", 12)
slots("attn_core", 15)
slots("attn_y", 15)
slots("attn_fwd", 15)
slots("wout_core", 1)
slots("wout_y", 4)
slots("wout_x", 4)
slots("wout_extra", 4)
slots("gather", 6)
slots("shift", 12)
slots("out_y", 12)
slots("out_core", 12)
slots("out_fwd", 12)
slots("relay", 12)
slots("relayed", 12)
slots("meta", 1)
N_SEM = sum(n for _, n in SEM.values())


def kernel(
    frame, width, heads_width,
    x_in, fresh, levels, window_start, mod_in, w_in, gain, wout_in, sampler,
    out,
    x0, x1, h, wkv, wq, wfull, q, attn0, attn1, kv0, kv1,
    xs, xf, qf, attnf, xsf, relay, mod, slot0, slot1, lsem, ssem, rsem,
):
    rows = 2 * frame
    half = width // 2
    quarter = width // 4
    pairs = heads_width // 128
    qi = lax.axis_index("queue")
    ti = lax.axis_index("tensor")
    n_queue = lax.axis_size("queue")
    core = lax.rem(ti, 2)
    chip = lax.div(ti, 2)
    t_core = chip * 2 + (1 - core)
    t_y = lax.rem(ti + 2, 4)
    t_far = 3 - ti
    up = lax.rem(qi + 1, n_queue)
    down = lax.rem(qi + n_queue - 1, n_queue)
    across = lax.rem(qi + n_queue // 2, n_queue)
    plane = lax.div(qi, 16) * 16
    x_up = plane + lax.rem(qi + 4, 16)
    x_down = plane + lax.rem(qi + 12, 16)
    x_pos = lax.div(lax.rem(qi, 16), 4)
    z_pos = lax.rem(qi, 4)
    first = qi == 0
    final = qi == n_queue - 1
    mirror = plane + 15 - lax.rem(qi, 16)
    middle = qi == n_queue // 2
    not_first = jnp.logical_not(first)
    not_final = jnp.logical_not(final)

    def rcopy(name, index, src, dst, device, lands_as=None):
        slot = SEM[name][0] + index
        lands = SEM[lands_as or name][0] + index
        return pltpu.make_async_remote_copy(
            src_ref=src, dst_ref=dst, send_sem=ssem.at[slot], recv_sem=rsem.at[lands],
            device_id=device, device_id_type=MESH,
        )

    def landed(name, index, ref):
        rcopy(name, index, ref, ref, (qi, t_core)).wait_recv()

    def local(index, src, dst):
        return pltpu.make_async_copy(src, dst, lsem.at[index])

    def at_lane(start, size):
        return pl.ds(pl.multiple_of(start, 128), size)

    def at_row(start, size):
        return pl.ds(pl.multiple_of(start, 16), size)

    load_mod = local(1, mod_in, mod)
    load_mod.start()
    load_x = []
    for c in range(4):
        at = slice(c * frame // 2, (c + 1) * frame // 2)
        load_x.append(local((0, 11, 13, 14)[c], x_in.at[at], x0.at[at]))
    load_w = []
    for p in range(pairs):
        for j in (1, 2):
            load_w.append(
                local(1 + 2 * p + j, w_in.at[j, :, p * 128 : (p + 1) * 128],
                      wkv.at[:, p * 256 + (j - 1) * 128 : p * 256 + j * 128])
            )
    load_w.append(local(8, w_in.at[0], wq))
    for load in load_x[:1] + load_w[: 2 * pairs] + load_x[1:] + load_w[2 * pairs :]:
        load.start()
    my_half = at_lane(core * half, half)
    other_half = at_lane((1 - core) * half, half)
    load_wout = local(9, wout_in.at[:, my_half], wfull.at[at_row(ti * heads_width, heads_width)])

    last = local(10, fresh.at[1], out.at[frame:rows])
    load_f = local(12, fresh.at[0], xf)

    @pl.when(final)
    def _():
        load_f.start()
        last.start()

    load_wout.start()
    barrier = pltpu.get_barrier_semaphore()
    partners = [
        (up, ti), (down, ti), (qi, t_core), (qi, t_y),
        (across, t_y), (across, t_far), (x_up, ti), (x_down, ti), (mirror, ti), (across, ti),
    ]
    for device in partners:
        pl.semaphore_signal(barrier, inc=1, device_id=device, device_id_type=MESH)
    pl.semaphore_wait(barrier, len(partners))

    sends = []

    def send(name, index, src, dst, device):
        copy = rcopy(name, index, src, dst, device)
        copy.start()
        sends.append((None, copy))
        return copy

    def send_if(cond, name, index, src, dst, device, lands_as=None):
        copy = rcopy(name, index, src, dst, device, lands_as)

        @pl.when(cond)
        def _():
            copy.start()

        sends.append((cond, copy))

    piece = heads_width // 4

    def my_piece(k):
        return lax.rem(x_pos + k, 4) * piece

    def wout_rows(t, k):
        return wfull.at[at_row(t * heads_width + my_piece(k), piece)]

    def wout_src(k, columns):
        return wout_in.at[at_row(my_piece(k), piece), columns]

    send("wout_y", 0, wout_src(0, my_half), wout_rows(ti, 0), (across, t_y))
    send("wout_y", 1, wout_src(0, other_half), wout_rows(ti, 0), (across, t_far))
    send("wout_core", 0, wout_in.at[:, other_half],
         wfull.at[at_row(ti * heads_width, heads_width)], (qi, t_core))
    send("wout_y", 2, wout_src(2, my_half), wout_rows(ti, 2), (across, t_y))
    send("wout_y", 3, wout_src(2, other_half), wout_rows(ti, 2), (across, t_far))

    at_bottom = z_pos == 0
    at_top = z_pos == 3
    early_rows = piece // 3

    def wout_cut(t, k, start, count):
        return wfull.at[at_row(t * heads_width + my_piece(k) + start, count)]

    for cond, k, index in ((at_top, 3, 0), (at_bottom, 1, 2)):
        for i, (columns, t) in enumerate(((my_half, t_y), (other_half, t_far))):
            send_if(cond, "wout_extra", index + i,
                    wout_in.at[at_row(my_piece(k), early_rows), columns],
                    wout_cut(ti, k, 0, early_rows), (across, t))

    def forward_wout_late():
        for i, t in enumerate((t_y, t_far)):
            rest = wout_cut(t, 0, early_rows, piece - early_rows)
            send_if(at_top, "wout_x", i, rest, rest, (x_up, ti))
            send_if(at_bottom, "wout_x", 2 + i, rest, rest, (x_down, ti))

    def forward_wout():
        for i, t in enumerate((t_y, t_far)):
            landed("wout_y", i, wout_rows(t, 0))
            mine = wout_rows(t, 0)
            send_if(jnp.logical_not(at_top), "wout_x", i, mine, mine, (x_up, ti))
            send_if(jnp.logical_not(at_bottom), "wout_x", 2 + i, mine, mine, (x_down, ti))

    def finish_piece(cond, t, k, index):
        @pl.when(cond)
        def _():
            landed("wout_extra", index, wout_cut(t, k, 0, early_rows))
            landed("wout_x", index, wout_cut(t, k, early_rows, piece - early_rows))

        @pl.when(jnp.logical_not(cond))
        def _():
            landed("wout_x", index, wout_rows(t, k))

    def finish_wout():
        load_wout.wait()
        landed("wout_core", 0, wfull.at[at_row(t_core * heads_width, heads_width)])
        for i, t in enumerate((t_y, t_far)):
            landed("wout_y", 2 + i, wout_rows(t, 2))
            for cond, k, index in ((at_top, 3, i), (at_bottom, 1, 2 + i)):
                finish_piece(cond, t, k, index)

    row_head = lax.broadcasted_iota(jnp.int32, (128, 128), 0) >> 6
    col_head = lax.broadcasted_iota(jnp.int32, (128, 128), 1) >> 6
    head_mean = jnp.where(row_head == col_head, 1.0 / 64.0, 0.0).astype(BF16)

    def head_norm(values, gain_row):
        high = values.astype(BF16)
        low = (values - high.astype(F32)).astype(BF16)
        mean = jnp.dot(high, head_mean, preferred_element_type=F32)
        mean = mean + jnp.dot(low, head_mean, preferred_element_type=F32)
        centered = values - mean
        var = jnp.dot((centered * centered).astype(BF16), head_mean, preferred_element_type=F32)
        return (centered * lax.rsqrt(var + EPS) * gain_row).astype(BF16)

    for f in range(2):
        slot0[f, 3:4, :] = jnp.full((1, width), sampler[0, levels[f]], F32)
        slot0[f, 4:5, :] = jnp.full((1, width), sampler[1, levels[f]], F32)
        slot0[f, 5:8, :] = jnp.full((3, width), window_start[f].astype(F32), F32)
    load_mod.wait()
    for f in range(2):
        for j in range(3):
            slot0[f, j : j + 1, :] = mod[j, pl.ds(levels[f], 1), :]
    send_if(not_final, "meta", 0, slot0.at[1], slot1, (up, ti))

    @pl.when(first)
    def _():
        slot1[...] = slot0[0]

    def norm_rows(src, param, start, count):
        chunk = 64
        for i in range(count // chunk):
            at = slice(start + i * chunk, start + (i + 1) * chunk)
            mean = jnp.mean(src[at, :].astype(F32), axis=-1, keepdims=True)
            centered = src[at, :].astype(F32) - mean
            var = jnp.mean(centered * centered, axis=-1, keepdims=True)
            normed = (src[at, :].astype(F32) - mean) * lax.rsqrt(var + EPS)
            h[at, :] = (normed * (1.0 + param[1:2, :]) + param[0:1, :]).astype(BF16)

    def store_kv(kv, p, slot, at, acc):
        kv[slot, at, p * 256 : p * 256 + 128] = head_norm(
            acc[:, :128], gain[1:2, p * 128 : (p + 1) * 128]
        )
        kv[slot, at, p * 256 + 128 : (p + 1) * 256] = acc[:, 128:].astype(BF16)

    def store_q(to, acc):
        for p in range(pairs):
            cols = slice(p * 128, (p + 1) * 128)
            to[:, cols] = head_norm(acc[:, cols], gain[0:1, cols]) * jnp.asarray(0.125, BF16)

    part = frame // 2

    def project(src, params, order, kv, send_halo, ready):
        ready(order[0])
        norm_rows(src, params[order[0] // 2], order[0] * part, part)
        if load_w:
            for load in load_w[: 2 * pairs]:
                load.wait()
        for i, c in enumerate(order):
            if i + 1 < len(order):
                after = order[i + 1]
                ready(after)
                norm_rows(src, params[after // 2], after * part, part)
            f = c // 2
            at = slice((c % 2) * part, (c % 2 + 1) * part)
            acc = jnp.dot(
                h[c * part : (c + 1) * part, :], wkv[...], preferred_element_type=F32
            )
            for p in range(pairs):
                store_kv(kv, p, f + 2, at, acc[:, p * 256 : (p + 1) * 256])
            send_halo(i, f, at)
        if load_w:
            load_w[2 * pairs].wait()
            load_w.clear()
        store_q(q, jnp.dot(h[...], wq[...], preferred_element_type=F32))

    q_chunk = 128
    first_head = lax.broadcasted_iota(jnp.int32, (q_chunk, 128), 1) < 64
    zeros = jnp.zeros((q_chunk, 128), BF16)
    ones = jnp.ones((WIN * frame, 128), BF16)

    def attend(kv, p, f, window, flag, queries, attn):
        fixed, second, if_set, if_clear = window
        lanes = slice(p * 256, (p + 1) * 256)
        k_lanes = slice(p * 256, p * 256 + 128)
        v_lanes = slice(p * 256 + 128, (p + 1) * 256)
        chosen = jnp.where(
            flag, kv[if_set, :, lanes].astype(F32), kv[if_clear, :, lanes].astype(F32)
        ).astype(BF16)
        keys = jnp.concatenate(
            [kv[fixed, :, k_lanes], kv[second, :, k_lanes], chosen[:, :128]], axis=0
        )
        values = jnp.concatenate(
            [kv[fixed, :, v_lanes], kv[second, :, v_lanes], chosen[:, 128:]], axis=0
        )
        values = jnp.concatenate([values, ones], axis=1)

        def scores_of(i):
            start = f * frame + i * q_chunk
            rows_q = queries[start : start + q_chunk, p * 128 : (p + 1) * 128]
            both = jnp.concatenate(
                [jnp.where(first_head, rows_q, zeros), jnp.where(first_head, zeros, rows_q)], axis=0
            )
            return lax.dot_general(
                both, keys, (((1,), (1,)), ((), ())), preferred_element_type=F32
            )

        n = frame // q_chunk
        ahead = scores_of(0)
        for i in range(n):
            scores = ahead
            if i + 1 < n:
                ahead = scores_of(i + 1)
            top = jnp.max(scores, axis=-1, keepdims=True)
            expo = jnp.exp(scores - top).astype(BF16)
            total = jnp.dot(expo, values, preferred_element_type=F32)
            picked = jnp.where(
                jnp.concatenate([first_head, first_head], axis=1), total[:q_chunk], total[q_chunk:]
            )
            start = f * frame + i * q_chunk
            attn[start : start + q_chunk, at_lane(ti * heads_width + p * 128, 128)] = (
                picked[:, :128] / picked[:, 128:]
            ).astype(BF16)

    def attn_block(attn, t, p, f):
        return attn.at[f * frame : (f + 1) * frame, at_lane(t * heads_width + p * 128, 128)]

    def attn_slot(step, p, f):
        return step * 6 + p * 2 + f

    def share_attn(step, attn, p, f):
        mine = attn_block(attn, ti, p, f)
        send("attn_y", attn_slot(step, p, f), mine, mine, (qi, t_y))
        send("attn_core", attn_slot(step, p, f), mine, mine, (qi, t_core))

    def forward_attn(step, attn, p, f):
        block = attn_block(attn, t_y, p, f)
        landed("attn_y", attn_slot(step, p, f), block)
        send("attn_fwd", attn_slot(step, p, f), block, block, (qi, t_core))

    def finish_attn(step, attn, f):
        for p in range(pairs):
            landed("attn_core", attn_slot(step, p, f), attn_block(attn, t_core, p, f))
            landed("attn_fwd", attn_slot(step, p, f), attn_block(attn, t_far, p, f))

    def update(values, branch, param, columns):
        values = values.astype(F32)
        noise_pred = values + param[2:3, columns] * branch
        return (param[3:4, columns] * values + param[4:5, columns] * noise_pred).astype(BF16)

    param0 = (slot0.at[0], slot0.at[1])
    param1 = (slot1, slot0.at[0])
    window0 = (
        (2, jnp.where(first, 4, 1), 3, 0),
        (3, jnp.where(final, 1, 4), 5, 2),
    )
    window1 = ((2, 3, 4, 1), (3, 2, 4, 1))

    def starts_from(param, slot):
        start = jnp.concatenate([param[5:6, 0:128]] * 2, axis=1)
        return start >= slot.astype(F32)

    def cut(kv, slots_of, at, p):
        lanes = slice(0, 2 * heads_width) if p is None else slice(p * 256, (p + 1) * 256)
        return kv.at[slots_of, at, lanes]

    def send_halo0(i, f, at):
        full = slice(0, frame)
        jobs = [(0, f, at, None)] if i == 0 else [(i, f, at, 0)]
        if i == 3:
            for p in range(1, pairs):
                jobs += [(2 * p + 2, 0, half_of(1), p), (2 * p + 3, 1, full, p)]
        for index, g, rows_at, p in jobs:
            own = cut(kv0, g + 2, rows_at, p)
            send_if(not_final, "halo_up", index, own, cut(kv0, g, rows_at, p), (up, ti))
            send_if(not_first, "halo_down", index, own, cut(kv0, g + 4, rows_at, p), (down, ti))

    def half_of(c):
        return slice((c % 2) * part, (c % 2 + 1) * part)

    def land_halo0(p):
        def land(name, base):
            if p == 0:
                landed(name, 0, cut(kv0, base, half_of(0), None))
                for c in (1, 2, 3):
                    landed(name, c, cut(kv0, base + c // 2, half_of(c), 0))
            else:
                landed(name, 2 * p + 2, cut(kv0, base, half_of(1), p))
                landed(name, 2 * p + 3, cut(kv0, base + 1, slice(0, frame), p))

        pl.when(not_first)(lambda: land("halo_up", 0))
        pl.when(not_final)(lambda: land("halo_down", 4))

    project(x0, param0, (0, 1, 2, 3), kv0, send_halo0, lambda c: load_x[c].wait())

    @pl.when(final)
    def _():
        load_f.wait()
        norm_rows(xf, slot0.at[1], 0, frame)
        entering = jnp.dot(h[0:frame, :], wkv[...], preferred_element_type=F32)
        for p in range(pairs):
            store_kv(kv1, p, 4, slice(0, frame), entering[:, p * 256 : (p + 1) * 256])
        store_q(qf, jnp.dot(h[0:frame, :], wq[...], preferred_element_type=F32))

    lag = 2
    done = []
    for p in range(pairs):
        if p == 1:
            forward_wout()
        land_halo0(p)
        if p == pairs - 1:
            forward_wout_late()
        for f in range(2):
            attend(kv0, p, f, window0[f], starts_from(param0[f], 2 * qi - 1 + 2 * f), q, attn0)
            share_attn(0, attn0, p, f)
            done.append((p, f))
            if len(done) > lag:
                forward_attn(0, attn0, *done[-1 - lag])
    finish_wout()
    waiting = done[-lag:]
    n_cols = 256

    def x1_rows(c, columns):
        return x1.at[c * part : (c + 1) * part, columns]

    order1 = (0, 2, 1, 3)
    for i, c in enumerate(order1):
        if i < 2:
            forward_attn(0, attn0, *waiting[i])
            finish_attn(0, attn0, i)
        at = slice(c * part, (c + 1) * part)
        branch = jnp.dot(attn0[at, :], wfull[...], preferred_element_type=F32)
        x1[at, my_half] = update(x0[at, my_half], branch, param0[c // 2], my_half)
        send("gather", c, x1_rows(c, my_half), x1_rows(c, my_half), (qi, t_core))
    @pl.when(not_first)
    def _():
        landed("meta", 0, slot1)


    def send_halo1(i, f, at):
        last_one = i >= 2
        for p in range(pairs) if last_one else [None]:
            index = 8 + (0 if p is None else p + 1)
            own = cut(kv1, f + 2, at, p)
            if f == 1:
                send_if(not_final, "halo_up", index, own, cut(kv1, 1, at, p), (up, ti))
            else:
                send_if(not_first, "halo_down", index, own, cut(kv1, 4, at, p), (down, ti))

    def land_halo1(p):
        def land(name, slot):
            if p == 0:
                landed(name, 8, cut(kv1, slot, half_of(0), None))
            landed(name, 9 + p, cut(kv1, slot, half_of(1), p))

        pl.when(not_first)(lambda: land("halo_up", 1))
        pl.when(not_final)(lambda: land("halo_down", 4))

    project(
        x1, param1, order1, kv1, send_halo1,
        lambda c: landed("gather", c, x1_rows(c, other_half)),
    )
    done = []
    for f in range(2):
        for p in range(pairs):
            if f == 0:
                land_halo1(p)
            attend(kv1, p, f, window1[f], starts_from(param1[f], 2 * qi - 1), q, attn1)
            share_attn(1, attn1, p, f)
            done.append((p, f))
            if len(done) > lag:
                forward_attn(1, attn1, *done[-1 - lag])

    chunks = 12
    n_rows = rows // chunks
    my_quarter = core * half + chip * quarter
    y_quarter = core * half + (1 - chip) * quarter

    def out_part(j, start):
        return out.at[at_row(j * n_rows, n_rows), at_lane(start, quarter)]

    def piece_of(ref, j):
        return ref.at[j * n_rows : (j + 1) * n_rows]

    def project_out(attn, values, param, f, to):
        at = slice(f * frame, (f + 1) * frame)

        @pl.loop(0, quarter // n_cols)
        def _(n):
            columns = at_lane(my_quarter + n * n_cols, n_cols)
            inner = at_lane(n * n_cols, n_cols)
            weight = wfull[:, at_lane(chip * quarter + n * n_cols, n_cols)]
            branch = jnp.dot(attn[at, :], weight, preferred_element_type=F32)
            to[at, inner] = update(values[at, columns], branch, param, columns)

    by_last = (3, 4, 5, 8, 9, 10, 11)
    by_first = (2, 7)

    for f in range(2):
        if f == 1:
            for piece in done[-lag:]:
                forward_attn(1, attn1, *piece)
        finish_attn(1, attn1, f)
        project_out(attn1, x1, param1[f], f, xs)
        for j in range(f * chunks // 2, (f + 1) * chunks // 2):
            direct = not_first
            if j in by_last + by_first:
                direct = jnp.logical_and(not_first, jnp.logical_not(middle))
                by = mirror if j in by_last else across
                send_if(middle, "relay", j, piece_of(xs, j), piece_of(relay, j), (by, ti))
            send_if(direct, "shift", j, piece_of(xs, j), out_part(j, my_quarter), (down, ti))

    def relayed(j):
        to = across if j in by_last else mirror
        return rcopy("relayed", j, piece_of(relay, j), out_part(j, my_quarter), (to, ti), "shift")

    def pass_relay(j):
        landed("relay", j, piece_of(relay, j))
        relayed(j).start()

    @pl.when(final)
    def _():
        blocks = []
        for p in range(pairs):
            attend(kv1, p, 0, (2, 3, 4, 4), starts_from(slot0.at[1], 2 * qi), qf, attnf)
            mine = attn_block(attnf, ti, p, 0)
            theirs = attn_block(attnf, t_y, p, 0)
            blocks.append((
                rcopy("attn_y", 12 + p, mine, mine, (qi, t_y)),
                rcopy("attn_core", 12 + p, mine, mine, (qi, t_core)),
                rcopy("attn_fwd", 12 + p, theirs, theirs, (qi, t_core)),
            ))
            blocks[p][0].start()
            blocks[p][1].start()
            if p == pairs - 1:
                for j in by_last[:3]:
                    pass_relay(j)
        for p in range(pairs):
            landed("attn_y", 12 + p, attn_block(attnf, t_y, p, 0))
            blocks[p][2].start()
        for p in range(pairs):
            landed("attn_core", 12 + p, attn_block(attnf, t_core, p, 0))
            landed("attn_fwd", 12 + p, attn_block(attnf, t_far, p, 0))
        project_out(attnf, xf, slot0.at[1], 0, xsf)
        stays = local(0, xsf, out.at[0:frame, at_lane(my_quarter, quarter)])
        stays.start()
        for block in blocks:
            for copy in block:
                copy.wait_send()
        stays.wait()

    def guarded(f, action):
        if f == 0:
            action()
        else:
            pl.when(not_final)(action)

    def spread(j):
        part = out_part(j, my_quarter)
        rcopy("out_y", j, part, part, (qi, t_y)).start()
        rcopy("out_core", j, part, part, (qi, t_core)).start()

    def pass_on(j):
        part = out_part(j, y_quarter)
        landed("out_y", j, part)
        rcopy("out_fwd", j, part, part, (qi, t_core)).start()

    behind = 3

    @pl.when(final)
    def _():
        for j in range(chunks // 2):
            spread(j)
        for j in by_last[3:]:
            pass_relay(j)
        for j in range(chunks // 2):
            pass_on(j)

    @pl.when(not_final)
    def _():
        for j in range(chunks):
            for k in {0: by_first[:1], 4: by_first[1:]}.get(j, ()):
                pl.when(first)(functools.partial(pass_relay, k))
            landed("shift", j, out_part(j, my_quarter))
            spread(j)
            if j >= behind:
                pass_on(j - behind)
        for j in range(chunks - behind, chunks):
            pass_on(j)

    core_quarter = (1 - core) * half + chip * quarter
    far_quarter = (1 - core) * half + (1 - chip) * quarter
    for j in range(chunks):

        def action():
            landed("out_core", j, out_part(j, core_quarter))
            landed("out_fwd", j, out_part(j, far_quarter))
            mine = out_part(j, my_quarter)
            rcopy("out_y", j, mine, mine, (qi, t_y)).wait_send()
            rcopy("out_core", j, mine, mine, (qi, t_core)).wait_send()
            passed = out_part(j, y_quarter)
            rcopy("out_fwd", j, passed, passed, (qi, t_core)).wait_send()

        guarded(j // (chunks // 2), action)

    @pl.when(final)
    def _():
        last.wait()
        for j in by_last:
            relayed(j).wait_send()

    @pl.when(first)
    def _():
        for j in by_first:
            relayed(j).wait_send()

    for cond, copy in sends:
        if cond is None:
            copy.wait_send()
        else:
            pl.when(cond)(copy.wait_send)


def hand_out(n_parts, src, dst, held, in_sem, out_sem):
    rows = src.shape[0] // n_parts
    pieces = [pl.ds(i * rows, rows) for i in range(n_parts)]
    reads = [
        pltpu.make_async_copy(src.at[at], held.at[at], in_sem.at[i]) for i, at in enumerate(pieces)
    ]
    writes = [
        pltpu.make_async_copy(held.at[at], dst.at[at], out_sem.at[i]) for i, at in enumerate(pieces)
    ]
    for read in reads:
        read.start()
    for read, write in zip(reads, writes):
        read.wait()
        write.start()
    for write in writes:
        write.wait()


def body(
    queue_latents, fresh_noise, levels, window_start, modulation, w_qkv, qk_gain, w_out, sampler
):
    frames, frame, width = queue_latents.shape
    rows = frames * frame
    heads_width = w_out.shape[0]
    level_count = modulation.shape[0]
    any_space = pl.BlockSpec(memory_space=pl.ANY)
    smem = pl.BlockSpec(memory_space=pltpu.SMEM)
    vmem = pl.BlockSpec(memory_space=pltpu.VMEM)
    kv = pltpu.VMEM((6, frame, 2 * heads_width), BF16)
    moved = pl.pallas_call(
        functools.partial(kernel, frame, width, heads_width),
        name="diagonal_steps",
        out_shape=jax.ShapeDtypeStruct((rows, width), BF16),
        in_specs=[any_space, any_space, smem, smem, any_space, any_space, vmem, any_space, smem],
        out_specs=any_space,
        scratch_shapes=[
            pltpu.VMEM((rows, width), BF16),
            pltpu.VMEM((rows, width), BF16),
            pltpu.VMEM((rows, width), BF16),
            pltpu.VMEM((width, 2 * heads_width), BF16),
            pltpu.VMEM((width, heads_width), BF16),
            pltpu.VMEM((4 * heads_width, width // 2), BF16),
            pltpu.VMEM((rows, heads_width), BF16),
            pltpu.VMEM((rows, 4 * heads_width), BF16),
            pltpu.VMEM((rows, 4 * heads_width), BF16),
            kv, kv,
            pltpu.VMEM((rows, width // 4), BF16),
            pltpu.VMEM((frame, width), BF16),
            pltpu.VMEM((frame, heads_width), BF16),
            pltpu.VMEM((frame, 4 * heads_width), BF16),
            pltpu.VMEM((frame, width // 4), BF16),
            pltpu.VMEM((rows, width // 4), BF16),
            pltpu.VMEM((3, level_count, width), F32),
            pltpu.VMEM((2, 8, width), F32),
            pltpu.VMEM((8, width), F32),
            pltpu.SemaphoreType.DMA((15,)),
            pltpu.SemaphoreType.DMA((N_SEM,)),
            pltpu.SemaphoreType.DMA((N_SEM,)),
        ],
        compiler_params=pltpu.CompilerParams(
            collective_id=0, has_side_effects=True, vmem_limit_bytes=60 * 1024 * 1024
        ),
        cost_estimate=pl.CostEstimate(
            flops=4 * rows * width * 1536 * 2, bytes_accessed=40 * 2**20, transcendentals=10**7
        ),
    )(
        queue_latents.reshape(rows, width),
        fresh_noise,
        levels,
        window_start,
        jnp.transpose(modulation, (1, 0, 2)),
        jnp.transpose(w_qkv, (1, 0, 2)),
        qk_gain,
        w_out,
        jnp.transpose(sampler, (1, 0)),
    )
    n_parts = 4
    result = pl.pallas_call(
        functools.partial(hand_out, n_parts),
        name="hand_out",
        out_shape=jax.ShapeDtypeStruct((rows, width), BF16),
        in_specs=[any_space],
        out_specs=any_space,
        scratch_shapes=[
            pltpu.VMEM((rows, width), BF16),
            pltpu.SemaphoreType.DMA((n_parts,)),
            pltpu.SemaphoreType.DMA((n_parts,)),
        ],
        compiler_params=pltpu.CompilerParams(vmem_limit_bytes=60 * 1024 * 1024),
        cost_estimate=pl.CostEstimate(
            flops=0, bytes_accessed=4 * rows * width, transcendentals=0
        ),
    )(moved)
    return result.reshape(frames, frame, width)


def solution(mesh):
    in_specs = (
        P("queue", None, None),
        P(),
        P("queue"),
        P("queue"),
        P(),
        P(None, None, "tensor"),
        P(None, "tensor"),
        P("tensor", None),
        P(),
    )
    out_specs = P("queue", None, None)
    return jax.shard_map(body, mesh=mesh, in_specs=in_specs, out_specs=out_specs, check_vma=False)
```

```python
import functools

import jax
import jax.numpy as jnp
from jax import lax
from jax.experimental import pallas as pl
from jax.experimental.pallas import tpu as pltpu
from jax.sharding import PartitionSpec as P

MESH = pl.DeviceIdType.MESH
BF16 = jnp.bfloat16
F32 = jnp.float32
STEPS = 2
WIN = 3
EPS = 1e-6

SEM = {}


def slots(name, count):
    SEM[name] = sum(n for _, n in SEM.values()), count


slots("halo_up", 12)
slots("halo_down", 12)
slots("attn_core", 15)
slots("attn_y", 15)
slots("attn_fwd", 15)
slots("wout_core", 1)
slots("wout_y", 4)
slots("wout_x", 4)
slots("wout_extra", 4)
slots("gather", 6)
slots("shift", 12)
slots("out_y", 12)
slots("out_core", 12)
slots("out_fwd", 12)
slots("relay", 12)
slots("relayed", 12)
slots("meta", 1)
N_SEM = sum(n for _, n in SEM.values())


def kernel(
    frame, width, heads_width,
    x_in, fresh, levels, window_start, mod_in, w_in, gain, wout_in, sampler,
    out,
    x0, x1, h, wkv, wq, wfull, q, attn0, attn1, kv0, kv1,
    xs, xf, qf, attnf, xsf, relay, mod, slot0, slot1, lsem, ssem, rsem,
):
    rows = 2 * frame
    half = width // 2
    quarter = width // 4
    pairs = heads_width // 128
    qi = lax.axis_index("queue")
    ti = lax.axis_index("tensor")
    n_queue = lax.axis_size("queue")
    core = lax.rem(ti, 2)
    chip = lax.div(ti, 2)
    t_core = chip * 2 + (1 - core)
    t_y = lax.rem(ti + 2, 4)
    t_far = 3 - ti
    up = lax.rem(qi + 1, n_queue)
    down = lax.rem(qi + n_queue - 1, n_queue)
    across = lax.rem(qi + n_queue // 2, n_queue)
    plane = lax.div(qi, 16) * 16
    x_up = plane + lax.rem(qi + 4, 16)
    x_down = plane + lax.rem(qi + 12, 16)
    x_pos = lax.div(lax.rem(qi, 16), 4)
    z_pos = lax.rem(qi, 4)
    first = qi == 0
    final = qi == n_queue - 1
    mirror = plane + 15 - lax.rem(qi, 16)
    middle = qi == n_queue // 2
    not_first = jnp.logical_not(first)
    not_final = jnp.logical_not(final)

    def rcopy(name, index, src, dst, device, lands_as=None):
        slot = SEM[name][0] + index
        lands = SEM[lands_as or name][0] + index
        return pltpu.make_async_remote_copy(
            src_ref=src, dst_ref=dst, send_sem=ssem.at[slot], recv_sem=rsem.at[lands],
            device_id=device, device_id_type=MESH,
        )

    def landed(name, index, ref):
        rcopy(name, index, ref, ref, (qi, t_core)).wait_recv()

    def local(index, src, dst):
        return pltpu.make_async_copy(src, dst, lsem.at[index])

    def at_lane(start, size):
        return pl.ds(pl.multiple_of(start, 128), size)

    def at_row(start, size):
        return pl.ds(pl.multiple_of(start, 16), size)

    load_mod = local(1, mod_in, mod)
    load_mod.start()
    load_x = []
    for c in range(4):
        at = slice(c * frame // 2, (c + 1) * frame // 2)
        load_x.append(local((0, 11, 13, 14)[c], x_in.at[at], x0.at[at]))
    load_w = []
    for p in range(pairs):
        for j in (1, 2):
            load_w.append(
                local(1 + 2 * p + j, w_in.at[j, :, p * 128 : (p + 1) * 128],
                      wkv.at[:, p * 256 + (j - 1) * 128 : p * 256 + j * 128])
            )
    load_w.append(local(8, w_in.at[0], wq))
    for load in load_x[:1] + load_w[: 2 * pairs] + load_x[1:] + load_w[2 * pairs :]:
        load.start()
    my_half = at_lane(core * half, half)
    other_half = at_lane((1 - core) * half, half)
    load_wout = local(9, wout_in.at[:, my_half], wfull.at[at_row(ti * heads_width, heads_width)])

    last = local(10, fresh.at[1], out.at[frame:rows])
    load_f = local(12, fresh.at[0], xf)

    @pl.when(final)
    def _():
        load_f.start()
        last.start()

    load_wout.start()
    barrier = pltpu.get_barrier_semaphore()
    partners = [
        (up, ti), (down, ti), (qi, t_core), (qi, t_y),
        (across, t_y), (across, t_far), (x_up, ti), (x_down, ti), (mirror, ti), (across, ti),
    ]
    for device in partners:
        pl.semaphore_signal(barrier, inc=1, device_id=device, device_id_type=MESH)
    pl.semaphore_wait(barrier, len(partners))

    sends = []

    def send(name, index, src, dst, device):
        copy = rcopy(name, index, src, dst, device)
        copy.start()
        sends.append((None, copy))
        return copy

    def send_if(cond, name, index, src, dst, device, lands_as=None):
        copy = rcopy(name, index, src, dst, device, lands_as)

        @pl.when(cond)
        def _():
            copy.start()

        sends.append((cond, copy))

    piece = heads_width // 4

    def my_piece(k):
        return lax.rem(x_pos + k, 4) * piece

    def wout_rows(t, k):
        return wfull.at[at_row(t * heads_width + my_piece(k), piece)]

    def wout_src(k, columns):
        return wout_in.at[at_row(my_piece(k), piece), columns]

    send("wout_y", 0, wout_src(0, my_half), wout_rows(ti, 0), (across, t_y))
    send("wout_y", 1, wout_src(0, other_half), wout_rows(ti, 0), (across, t_far))
    send("wout_core", 0, wout_in.at[:, other_half],
         wfull.at[at_row(ti * heads_width, heads_width)], (qi, t_core))
    send("wout_y", 2, wout_src(2, my_half), wout_rows(ti, 2), (across, t_y))
    send("wout_y", 3, wout_src(2, other_half), wout_rows(ti, 2), (across, t_far))

    at_bottom = z_pos == 0
    at_top = z_pos == 3
    early_rows = piece // 3

    def wout_cut(t, k, start, count):
        return wfull.at[at_row(t * heads_width + my_piece(k) + start, count)]

    for cond, k, index in ((at_top, 3, 0), (at_bottom, 1, 2)):
        for i, (columns, t) in enumerate(((my_half, t_y), (other_half, t_far))):
            send_if(cond, "wout_extra", index + i,
                    wout_in.at[at_row(my_piece(k), early_rows), columns],
                    wout_cut(ti, k, 0, early_rows), (across, t))

    def forward_wout_late():
        for i, t in enumerate((t_y, t_far)):
            rest = wout_cut(t, 0, early_rows, piece - early_rows)
            send_if(at_top, "wout_x", i, rest, rest, (x_up, ti))
            send_if(at_bottom, "wout_x", 2 + i, rest, rest, (x_down, ti))

    def forward_wout():
        for i, t in enumerate((t_y, t_far)):
            landed("wout_y", i, wout_rows(t, 0))
            mine = wout_rows(t, 0)
            send_if(jnp.logical_not(at_top), "wout_x", i, mine, mine, (x_up, ti))
            send_if(jnp.logical_not(at_bottom), "wout_x", 2 + i, mine, mine, (x_down, ti))

    def finish_piece(cond, t, k, index):
        @pl.when(cond)
        def _():
            landed("wout_extra", index, wout_cut(t, k, 0, early_rows))
            landed("wout_x", index, wout_cut(t, k, early_rows, piece - early_rows))

        @pl.when(jnp.logical_not(cond))
        def _():
            landed("wout_x", index, wout_rows(t, k))

    def finish_wout():
        load_wout.wait()
        landed("wout_core", 0, wfull.at[at_row(t_core * heads_width, heads_width)])
        for i, t in enumerate((t_y, t_far)):
            landed("wout_y", 2 + i, wout_rows(t, 2))
            for cond, k, index in ((at_top, 3, i), (at_bottom, 1, 2 + i)):
                finish_piece(cond, t, k, index)

    row_head = lax.broadcasted_iota(jnp.int32, (128, 128), 0) >> 6
    col_head = lax.broadcasted_iota(jnp.int32, (128, 128), 1) >> 6
    head_mean = jnp.where(row_head == col_head, 1.0 / 64.0, 0.0).astype(BF16)

    def head_norm(values, gain_row):
        high = values.astype(BF16)
        low = (values - high.astype(F32)).astype(BF16)
        mean = jnp.dot(high, head_mean, preferred_element_type=F32)
        mean = mean + jnp.dot(low, head_mean, preferred_element_type=F32)
        centered = values - mean
        var = jnp.dot((centered * centered).astype(BF16), head_mean, preferred_element_type=F32)
        return (centered * lax.rsqrt(var + EPS) * gain_row).astype(BF16)

    for f in range(2):
        slot0[f, 3:4, :] = jnp.full((1, width), sampler[0, levels[f]], F32)
        slot0[f, 4:5, :] = jnp.full((1, width), sampler[1, levels[f]], F32)
        slot0[f, 5:8, :] = jnp.full((3, width), window_start[f].astype(F32), F32)
    load_mod.wait()
    for f in range(2):
        for j in range(3):
            slot0[f, j : j + 1, :] = mod[j, pl.ds(levels[f], 1), :]
    send_if(not_final, "meta", 0, slot0.at[1], slot1, (up, ti))

    @pl.when(first)
    def _():
        slot1[...] = slot0[0]

    def norm_rows(src, param, start, count):
        chunk = 64
        for i in range(count // chunk):
            at = slice(start + i * chunk, start + (i + 1) * chunk)
            mean = jnp.mean(src[at, :].astype(F32), axis=-1, keepdims=True)
            centered = src[at, :].astype(F32) - mean
            var = jnp.mean(centered * centered, axis=-1, keepdims=True)
            normed = (src[at, :].astype(F32) - mean) * lax.rsqrt(var + EPS)
            h[at, :] = (normed * (1.0 + param[1:2, :]) + param[0:1, :]).astype(BF16)

    def store_kv(kv, p, slot, at, acc):
        kv[slot, at, p * 256 : p * 256 + 128] = head_norm(
            acc[:, :128], gain[1:2, p * 128 : (p + 1) * 128]
        )
        kv[slot, at, p * 256 + 128 : (p + 1) * 256] = acc[:, 128:].astype(BF16)

    def store_q(to, acc):
        for p in range(pairs):
            cols = slice(p * 128, (p + 1) * 128)
            to[:, cols] = head_norm(acc[:, cols], gain[0:1, cols]) * jnp.asarray(0.125, BF16)

    part = frame // 2

    def project(src, params, order, kv, send_halo, ready):
        ready(order[0])
        norm_rows(src, params[order[0] // 2], order[0] * part, part)
        if load_w:
            for load in load_w[: 2 * pairs]:
                load.wait()
        for i, c in enumerate(order):
            if i + 1 < len(order):
                after = order[i + 1]
                ready(after)
                norm_rows(src, params[after // 2], after * part, part)
            f = c // 2
            at = slice((c % 2) * part, (c % 2 + 1) * part)
            acc = jnp.dot(
                h[c * part : (c + 1) * part, :], wkv[...], preferred_element_type=F32
            )
            for p in range(pairs):
                store_kv(kv, p, f + 2, at, acc[:, p * 256 : (p + 1) * 256])
            send_halo(i, f, at)
        if load_w:
            load_w[2 * pairs].wait()
            load_w.clear()
        store_q(q, jnp.dot(h[...], wq[...], preferred_element_type=F32))

    q_chunk = 128
    first_head = lax.broadcasted_iota(jnp.int32, (q_chunk, 128), 1) < 64
    zeros = jnp.zeros((q_chunk, 128), BF16)
    ones = jnp.ones((WIN * frame, 128), BF16)

    def attend(kv, p, f, window, flag, queries, attn):
        fixed, second, if_set, if_clear = window
        lanes = slice(p * 256, (p + 1) * 256)
        k_lanes = slice(p * 256, p * 256 + 128)
        v_lanes = slice(p * 256 + 128, (p + 1) * 256)
        chosen = jnp.where(
            flag, kv[if_set, :, lanes].astype(F32), kv[if_clear, :, lanes].astype(F32)
        ).astype(BF16)
        keys = jnp.concatenate(
            [kv[fixed, :, k_lanes], kv[second, :, k_lanes], chosen[:, :128]], axis=0
        )
        values = jnp.concatenate(
            [kv[fixed, :, v_lanes], kv[second, :, v_lanes], chosen[:, 128:]], axis=0
        )
        values = jnp.concatenate([values, ones], axis=1)

        def scores_of(i):
            start = f * frame + i * q_chunk
            rows_q = queries[start : start + q_chunk, p * 128 : (p + 1) * 128]
            both = jnp.concatenate(
                [jnp.where(first_head, rows_q, zeros), jnp.where(first_head, zeros, rows_q)], axis=0
            )
            return lax.dot_general(
                both, keys, (((1,), (1,)), ((), ())), preferred_element_type=F32
            )

        n = frame // q_chunk
        ahead = scores_of(0)
        for i in range(n):
            scores = ahead
            if i + 1 < n:
                ahead = scores_of(i + 1)
            top = jnp.max(scores, axis=-1, keepdims=True)
            expo = jnp.exp(scores - top).astype(BF16)
            total = jnp.dot(expo, values, preferred_element_type=F32)
            picked = jnp.where(
                jnp.concatenate([first_head, first_head], axis=1), total[:q_chunk], total[q_chunk:]
            )
            start = f * frame + i * q_chunk
            attn[start : start + q_chunk, at_lane(ti * heads_width + p * 128, 128)] = (
                picked[:, :128] / picked[:, 128:]
            ).astype(BF16)

    def attn_block(attn, t, p, f):
        return attn.at[f * frame : (f + 1) * frame, at_lane(t * heads_width + p * 128, 128)]

    def attn_slot(step, p, f):
        return step * 6 + p * 2 + f

    def share_attn(step, attn, p, f):
        mine = attn_block(attn, ti, p, f)
        send("attn_y", attn_slot(step, p, f), mine, mine, (qi, t_y))
        send("attn_core", attn_slot(step, p, f), mine, mine, (qi, t_core))

    def forward_attn(step, attn, p, f):
        block = attn_block(attn, t_y, p, f)
        landed("attn_y", attn_slot(step, p, f), block)
        send("attn_fwd", attn_slot(step, p, f), block, block, (qi, t_core))

    def finish_attn(step, attn, f):
        for p in range(pairs):
            landed("attn_core", attn_slot(step, p, f), attn_block(attn, t_core, p, f))
            landed("attn_fwd", attn_slot(step, p, f), attn_block(attn, t_far, p, f))

    def update(values, branch, param, columns):
        values = values.astype(F32)
        noise_pred = values + param[2:3, columns] * branch
        return (param[3:4, columns] * values + param[4:5, columns] * noise_pred).astype(BF16)

    param0 = (slot0.at[0], slot0.at[1])
    param1 = (slot1, slot0.at[0])
    window0 = (
        (2, jnp.where(first, 4, 1), 3, 0),
        (3, jnp.where(final, 1, 4), 5, 2),
    )
    window1 = ((2, 3, 4, 1), (3, 2, 4, 1))

    def starts_from(param, slot):
        start = jnp.concatenate([param[5:6, 0:128]] * 2, axis=1)
        return start >= slot.astype(F32)

    def cut(kv, slots_of, at, p):
        lanes = slice(0, 2 * heads_width) if p is None else slice(p * 256, (p + 1) * 256)
        return kv.at[slots_of, at, lanes]

    def send_halo0(i, f, at):
        full = slice(0, frame)
        jobs = [(0, f, at, None)] if i == 0 else [(i, f, at, 0)]
        if i == 3:
            for p in range(1, pairs):
                jobs += [(2 * p + 2, 0, half_of(1), p), (2 * p + 3, 1, full, p)]
        for index, g, rows_at, p in jobs:
            own = cut(kv0, g + 2, rows_at, p)
            send_if(not_final, "halo_up", index, own, cut(kv0, g, rows_at, p), (up, ti))
            send_if(not_first, "halo_down", index, own, cut(kv0, g + 4, rows_at, p), (down, ti))

    def half_of(c):
        return slice((c % 2) * part, (c % 2 + 1) * part)

    def land_halo0(p):
        def land(name, base):
            if p == 0:
                landed(name, 0, cut(kv0, base, half_of(0), None))
                for c in (1, 2, 3):
                    landed(name, c, cut(kv0, base + c // 2, half_of(c), 0))
            else:
                landed(name, 2 * p + 2, cut(kv0, base, half_of(1), p))
                landed(name, 2 * p + 3, cut(kv0, base + 1, slice(0, frame), p))

        pl.when(not_first)(lambda: land("halo_up", 0))
        pl.when(not_final)(lambda: land("halo_down", 4))

    project(x0, param0, (0, 1, 2, 3), kv0, send_halo0, lambda c: load_x[c].wait())

    @pl.when(final)
    def _():
        load_f.wait()
        norm_rows(xf, slot0.at[1], 0, frame)
        entering = jnp.dot(h[0:frame, :], wkv[...], preferred_element_type=F32)
        for p in range(pairs):
            store_kv(kv1, p, 4, slice(0, frame), entering[:, p * 256 : (p + 1) * 256])
        store_q(qf, jnp.dot(h[0:frame, :], wq[...], preferred_element_type=F32))

    lag = 2
    done = []
    for p in range(pairs):
        if p == 1:
            forward_wout()
        land_halo0(p)
        if p == pairs - 1:
            forward_wout_late()
        for f in range(2):
            attend(kv0, p, f, window0[f], starts_from(param0[f], 2 * qi - 1 + 2 * f), q, attn0)
            share_attn(0, attn0, p, f)
            done.append((p, f))
            if len(done) > lag:
                forward_attn(0, attn0, *done[-1 - lag])
    finish_wout()
    waiting = done[-lag:]
    n_cols = 256

    def x1_rows(c, columns):
        return x1.at[c * part : (c + 1) * part, columns]

    order1 = (0, 2, 1, 3)
    for i, c in enumerate(order1):
        if i < 2:
            forward_attn(0, attn0, *waiting[i])
            finish_attn(0, attn0, i)
        at = slice(c * part, (c + 1) * part)
        branch = jnp.dot(attn0[at, :], wfull[...], preferred_element_type=F32)
        x1[at, my_half] = update(x0[at, my_half], branch, param0[c // 2], my_half)
        send("gather", c, x1_rows(c, my_half), x1_rows(c, my_half), (qi, t_core))
    @pl.when(not_first)
    def _():
        landed("meta", 0, slot1)


    def send_halo1(i, f, at):
        last_one = i >= 2
        for p in range(pairs) if last_one else [None]:
            index = 8 + (0 if p is None else p + 1)
            own = cut(kv1, f + 2, at, p)
            if f == 1:
                send_if(not_final, "halo_up", index, own, cut(kv1, 1, at, p), (up, ti))
            else:
                send_if(not_first, "halo_down", index, own, cut(kv1, 4, at, p), (down, ti))

    def land_halo1(p):
        def land(name, slot):
            if p == 0:
                landed(name, 8, cut(kv1, slot, half_of(0), None))
            landed(name, 9 + p, cut(kv1, slot, half_of(1), p))

        pl.when(not_first)(lambda: land("halo_up", 1))
        pl.when(not_final)(lambda: land("halo_down", 4))

    project(
        x1, param1, order1, kv1, send_halo1,
        lambda c: landed("gather", c, x1_rows(c, other_half)),
    )
    def entering_copies(p):
        mine = attn_block(attnf, ti, p, 0)
        theirs = attn_block(attnf, t_y, p, 0)
        return (
            rcopy("attn_y", 12 + p, mine, mine, (qi, t_y)),
            rcopy("attn_core", 12 + p, mine, mine, (qi, t_core)),
            rcopy("attn_fwd", 12 + p, theirs, theirs, (qi, t_core)),
        )

    @pl.when(final)
    def _():
        for p in range(pairs):
            attend(kv1, p, 0, (2, 3, 4, 4), starts_from(slot0.at[1], 2 * qi), qf, attnf)
            for copy in entering_copies(p)[:2]:
                copy.start()

    done = []
    for f in range(2):
        for p in range(pairs):
            if f == 0:
                land_halo1(p)
            attend(kv1, p, f, window1[f], starts_from(param1[f], 2 * qi - 1), q, attn1)
            share_attn(1, attn1, p, f)
            done.append((p, f))
            if len(done) > lag:
                forward_attn(1, attn1, *done[-1 - lag])

    chunks = 12
    n_rows = rows // chunks
    my_quarter = core * half + chip * quarter
    y_quarter = core * half + (1 - chip) * quarter

    def out_part(j, start):
        return out.at[at_row(j * n_rows, n_rows), at_lane(start, quarter)]

    def piece_of(ref, j):
        return ref.at[j * n_rows : (j + 1) * n_rows]

    def project_out(attn, values, param, f, to):
        at = slice(f * frame, (f + 1) * frame)

        @pl.loop(0, quarter // n_cols)
        def _(n):
            columns = at_lane(my_quarter + n * n_cols, n_cols)
            inner = at_lane(n * n_cols, n_cols)
            weight = wfull[:, at_lane(chip * quarter + n * n_cols, n_cols)]
            branch = jnp.dot(attn[at, :], weight, preferred_element_type=F32)
            to[at, inner] = update(values[at, columns], branch, param, columns)

    by_last = (3, 4, 5, 8, 9, 10, 11)
    by_first = (2, 7)

    for f in range(2):
        if f == 1:
            for piece in done[-lag:]:
                forward_attn(1, attn1, *piece)
        finish_attn(1, attn1, f)
        project_out(attn1, x1, param1[f], f, xs)
        for j in range(f * chunks // 2, (f + 1) * chunks // 2):
            direct = not_first
            if j in by_last + by_first:
                direct = jnp.logical_and(not_first, jnp.logical_not(middle))
                by = mirror if j in by_last else across
                send_if(middle, "relay", j, piece_of(xs, j), piece_of(relay, j), (by, ti))
            send_if(direct, "shift", j, piece_of(xs, j), out_part(j, my_quarter), (down, ti))

    def relayed(j):
        to = across if j in by_last else mirror
        return rcopy("relayed", j, piece_of(relay, j), out_part(j, my_quarter), (to, ti), "shift")

    def pass_relay(j):
        landed("relay", j, piece_of(relay, j))
        relayed(j).start()

    @pl.when(final)
    def _():
        for p in range(pairs):
            landed("attn_y", 12 + p, attn_block(attnf, t_y, p, 0))
            entering_copies(p)[2].start()
        for p in range(pairs):
            landed("attn_core", 12 + p, attn_block(attnf, t_core, p, 0))
            landed("attn_fwd", 12 + p, attn_block(attnf, t_far, p, 0))
        project_out(attnf, xf, slot0.at[1], 0, xsf)
        stays = local(0, xsf, out.at[0:frame, at_lane(my_quarter, quarter)])
        stays.start()
        stays.wait()
        for p in range(pairs):
            for copy in entering_copies(p):
                copy.wait_send()

    def guarded(f, action):
        if f == 0:
            action()
        else:
            pl.when(not_final)(action)

    def spread(j):
        part = out_part(j, my_quarter)
        rcopy("out_y", j, part, part, (qi, t_y)).start()
        rcopy("out_core", j, part, part, (qi, t_core)).start()

    def pass_on(j):
        part = out_part(j, y_quarter)
        landed("out_y", j, part)
        rcopy("out_fwd", j, part, part, (qi, t_core)).start()

    behind = 3

    @pl.when(final)
    def _():
        for j in range(chunks // 2):
            spread(j)
        for j in by_last:
            pass_relay(j)
        for j in range(chunks // 2):
            pass_on(j)

    @pl.when(not_final)
    def _():
        for j in range(chunks):
            for k in {0: by_first[:1], 4: by_first[1:]}.get(j, ()):
                pl.when(first)(functools.partial(pass_relay, k))
            landed("shift", j, out_part(j, my_quarter))
            spread(j)
            if j >= behind:
                pass_on(j - behind)
        for j in range(chunks - behind, chunks):
            pass_on(j)

    core_quarter = (1 - core) * half + chip * quarter
    far_quarter = (1 - core) * half + (1 - chip) * quarter
    for j in range(chunks):

        def action():
            landed("out_core", j, out_part(j, core_quarter))
            landed("out_fwd", j, out_part(j, far_quarter))
            mine = out_part(j, my_quarter)
            rcopy("out_y", j, mine, mine, (qi, t_y)).wait_send()
            rcopy("out_core", j, mine, mine, (qi, t_core)).wait_send()
            passed = out_part(j, y_quarter)
            rcopy("out_fwd", j, passed, passed, (qi, t_core)).wait_send()

        guarded(j // (chunks // 2), action)

    @pl.when(final)
    def _():
        last.wait()
        for j in by_last:
            relayed(j).wait_send()

    @pl.when(first)
    def _():
        for j in by_first:
            relayed(j).wait_send()

    for cond, copy in sends:
        if cond is None:
            copy.wait_send()
        else:
            pl.when(cond)(copy.wait_send)


def hand_out(n_parts, src, dst, held, in_sem, out_sem):
    rows = src.shape[0] // n_parts
    pieces = [pl.ds(i * rows, rows) for i in range(n_parts)]
    reads = [
        pltpu.make_async_copy(src.at[at], held.at[at], in_sem.at[i]) for i, at in enumerate(pieces)
    ]
    writes = [
        pltpu.make_async_copy(held.at[at], dst.at[at], out_sem.at[i]) for i, at in enumerate(pieces)
    ]
    for read in reads:
        read.start()
    for read, write in zip(reads, writes):
        read.wait()
        write.start()
    for write in writes:
        write.wait()


def body(
    queue_latents, fresh_noise, levels, window_start, modulation, w_qkv, qk_gain, w_out, sampler
):
    frames, frame, width = queue_latents.shape
    rows = frames * frame
    heads_width = w_out.shape[0]
    level_count = modulation.shape[0]
    any_space = pl.BlockSpec(memory_space=pl.ANY)
    smem = pl.BlockSpec(memory_space=pltpu.SMEM)
    vmem = pl.BlockSpec(memory_space=pltpu.VMEM)
    kv = pltpu.VMEM((6, frame, 2 * heads_width), BF16)
    moved = pl.pallas_call(
        functools.partial(kernel, frame, width, heads_width),
        name="diagonal_steps",
        out_shape=jax.ShapeDtypeStruct((rows, width), BF16),
        in_specs=[any_space, any_space, smem, smem, any_space, any_space, vmem, any_space, smem],
        out_specs=any_space,
        scratch_shapes=[
            pltpu.VMEM((rows, width), BF16),
            pltpu.VMEM((rows, width), BF16),
            pltpu.VMEM((rows, width), BF16),
            pltpu.VMEM((width, 2 * heads_width), BF16),
            pltpu.VMEM((width, heads_width), BF16),
            pltpu.VMEM((4 * heads_width, width // 2), BF16),
            pltpu.VMEM((rows, heads_width), BF16),
            pltpu.VMEM((rows, 4 * heads_width), BF16),
            pltpu.VMEM((rows, 4 * heads_width), BF16),
            kv, kv,
            pltpu.VMEM((rows, width // 4), BF16),
            pltpu.VMEM((frame, width), BF16),
            pltpu.VMEM((frame, heads_width), BF16),
            pltpu.VMEM((frame, 4 * heads_width), BF16),
            pltpu.VMEM((frame, width // 4), BF16),
            pltpu.VMEM((rows, width // 4), BF16),
            pltpu.VMEM((3, level_count, width), F32),
            pltpu.VMEM((2, 8, width), F32),
            pltpu.VMEM((8, width), F32),
            pltpu.SemaphoreType.DMA((15,)),
            pltpu.SemaphoreType.DMA((N_SEM,)),
            pltpu.SemaphoreType.DMA((N_SEM,)),
        ],
        compiler_params=pltpu.CompilerParams(
            collective_id=0, has_side_effects=True, vmem_limit_bytes=60 * 1024 * 1024
        ),
        cost_estimate=pl.CostEstimate(
            flops=4 * rows * width * 1536 * 2, bytes_accessed=40 * 2**20, transcendentals=10**7
        ),
    )(
        queue_latents.reshape(rows, width),
        fresh_noise,
        levels,
        window_start,
        jnp.transpose(modulation, (1, 0, 2)),
        jnp.transpose(w_qkv, (1, 0, 2)),
        qk_gain,
        w_out,
        jnp.transpose(sampler, (1, 0)),
    )
    n_parts = 4
    result = pl.pallas_call(
        functools.partial(hand_out, n_parts),
        name="hand_out",
        out_shape=jax.ShapeDtypeStruct((rows, width), BF16),
        in_specs=[any_space],
        out_specs=any_space,
        scratch_shapes=[
            pltpu.VMEM((rows, width), BF16),
            pltpu.SemaphoreType.DMA((n_parts,)),
            pltpu.SemaphoreType.DMA((n_parts,)),
        ],
        compiler_params=pltpu.CompilerParams(vmem_limit_bytes=60 * 1024 * 1024),
        cost_estimate=pl.CostEstimate(
            flops=0, bytes_accessed=4 * rows * width, transcendentals=0
        ),
    )(moved)
    return result.reshape(frames, frame, width)


def solution(mesh):
    in_specs = (
        P("queue", None, None),
        P(),
        P("queue"),
        P("queue"),
        P(),
        P(None, None, "tensor"),
        P(None, "tensor"),
        P("tensor", None),
        P(),
    )
    out_specs = P("queue", None, None)
    return jax.shard_map(body, mesh=mesh, in_specs=in_specs, out_specs=out_specs, check_vma=False)
```

```python
import functools

import jax
import jax.numpy as jnp
from jax import lax
from jax.experimental import pallas as pl
from jax.experimental.pallas import tpu as pltpu
from jax.sharding import PartitionSpec as P

MESH = pl.DeviceIdType.MESH
BF16 = jnp.bfloat16
F32 = jnp.float32
STEPS = 2
WIN = 3
EPS = 1e-6

SEM = {}


def slots(name, count):
    SEM[name] = sum(n for _, n in SEM.values()), count


slots("halo_up", 12)
slots("halo_down", 12)
slots("attn_core", 15)
slots("attn_y", 15)
slots("attn_fwd", 15)
slots("wout_core", 1)
slots("wout_y", 4)
slots("wout_x", 4)
slots("wout_extra", 4)
slots("gather", 6)
slots("shift", 12)
slots("out_y", 12)
slots("out_core", 12)
slots("out_fwd", 12)
slots("relay", 12)
slots("relayed", 12)
slots("meta", 1)
N_SEM = sum(n for _, n in SEM.values())


def kernel(
    frame, width, heads_width,
    x_in, fresh, levels, window_start, mod_in, w_in, gain, wout_in, sampler,
    out,
    x0, x1, h, wkv, wq, wfull, q, attn0, attn1, kv0, kv1,
    xs, xf, qf, attnf, xsf, relay, mod, slot0, slot1, lsem, ssem, rsem,
):
    rows = 2 * frame
    half = width // 2
    quarter = width // 4
    pairs = heads_width // 128
    qi = lax.axis_index("queue")
    ti = lax.axis_index("tensor")
    n_queue = lax.axis_size("queue")
    core = lax.rem(ti, 2)
    chip = lax.div(ti, 2)
    t_core = chip * 2 + (1 - core)
    t_y = lax.rem(ti + 2, 4)
    t_far = 3 - ti
    up = lax.rem(qi + 1, n_queue)
    down = lax.rem(qi + n_queue - 1, n_queue)
    across = lax.rem(qi + n_queue // 2, n_queue)
    plane = lax.div(qi, 16) * 16
    x_up = plane + lax.rem(qi + 4, 16)
    x_down = plane + lax.rem(qi + 12, 16)
    x_pos = lax.div(lax.rem(qi, 16), 4)
    z_pos = lax.rem(qi, 4)
    first = qi == 0
    final = qi == n_queue - 1
    mirror = plane + 15 - lax.rem(qi, 16)
    middle = qi == n_queue // 2
    not_first = jnp.logical_not(first)
    not_final = jnp.logical_not(final)

    def rcopy(name, index, src, dst, device, lands_as=None):
        slot = SEM[name][0] + index
        lands = SEM[lands_as or name][0] + index
        return pltpu.make_async_remote_copy(
            src_ref=src, dst_ref=dst, send_sem=ssem.at[slot], recv_sem=rsem.at[lands],
            device_id=device, device_id_type=MESH,
        )

    def landed(name, index, ref):
        rcopy(name, index, ref, ref, (qi, t_core)).wait_recv()

    def local(index, src, dst):
        return pltpu.make_async_copy(src, dst, lsem.at[index])

    def at_lane(start, size):
        return pl.ds(pl.multiple_of(start, 128), size)

    def at_row(start, size):
        return pl.ds(pl.multiple_of(start, 16), size)

    load_mod = local(1, mod_in, mod)
    load_mod.start()
    load_x = []
    for c in range(4):
        at = slice(c * frame // 2, (c + 1) * frame // 2)
        load_x.append(local((0, 11, 13, 14)[c], x_in.at[at], x0.at[at]))
    load_w = []
    for p in range(pairs):
        for j in (1, 2):
            load_w.append(
                local(1 + 2 * p + j, w_in.at[j, :, p * 128 : (p + 1) * 128],
                      wkv.at[:, p * 256 + (j - 1) * 128 : p * 256 + j * 128])
            )
    load_w.append(local(8, w_in.at[0], wq))
    for load in load_x[:1] + load_w[: 2 * pairs] + load_x[1:] + load_w[2 * pairs :]:
        load.start()
    my_half = at_lane(core * half, half)
    other_half = at_lane((1 - core) * half, half)
    load_wout = local(9, wout_in.at[:, my_half], wfull.at[at_row(ti * heads_width, heads_width)])

    last = local(10, fresh.at[1], out.at[frame:rows])
    load_f = local(12, fresh.at[0], xf)

    @pl.when(final)
    def _():
        load_f.start()
        last.start()

    load_wout.start()
    barrier = pltpu.get_barrier_semaphore()
    partners = [
        (up, ti), (down, ti), (qi, t_core), (qi, t_y),
        (across, t_y), (across, t_far), (x_up, ti), (x_down, ti), (mirror, ti), (across, ti),
    ]
    for device in partners:
        pl.semaphore_signal(barrier, inc=1, device_id=device, device_id_type=MESH)
    pl.semaphore_wait(barrier, len(partners))

    sends = []

    def send(name, index, src, dst, device):
        copy = rcopy(name, index, src, dst, device)
        copy.start()
        sends.append((None, copy))
        return copy

    def send_if(cond, name, index, src, dst, device, lands_as=None):
        copy = rcopy(name, index, src, dst, device, lands_as)

        @pl.when(cond)
        def _():
            copy.start()

        sends.append((cond, copy))

    piece = heads_width // 4

    def my_piece(k):
        return lax.rem(x_pos + k, 4) * piece

    def wout_rows(t, k):
        return wfull.at[at_row(t * heads_width + my_piece(k), piece)]

    def wout_src(k, columns):
        return wout_in.at[at_row(my_piece(k), piece), columns]

    send("wout_y", 0, wout_src(0, my_half), wout_rows(ti, 0), (across, t_y))
    send("wout_y", 1, wout_src(0, other_half), wout_rows(ti, 0), (across, t_far))
    send("wout_core", 0, wout_in.at[:, other_half],
         wfull.at[at_row(ti * heads_width, heads_width)], (qi, t_core))
    send("wout_y", 2, wout_src(2, my_half), wout_rows(ti, 2), (across, t_y))
    send("wout_y", 3, wout_src(2, other_half), wout_rows(ti, 2), (across, t_far))

    at_bottom = z_pos == 0
    at_top = z_pos == 3
    early_rows = piece // 3

    def wout_cut(t, k, start, count):
        return wfull.at[at_row(t * heads_width + my_piece(k) + start, count)]

    for cond, k, index in ((at_top, 3, 0), (at_bottom, 1, 2)):
        for i, (columns, t) in enumerate(((my_half, t_y), (other_half, t_far))):
            send_if(cond, "wout_extra", index + i,
                    wout_in.at[at_row(my_piece(k), early_rows), columns],
                    wout_cut(ti, k, 0, early_rows), (across, t))

    def forward_wout_late():
        for i, t in enumerate((t_y, t_far)):
            rest = wout_cut(t, 0, early_rows, piece - early_rows)
            send_if(at_top, "wout_x", i, rest, rest, (x_up, ti))
            send_if(at_bottom, "wout_x", 2 + i, rest, rest, (x_down, ti))

    def forward_wout():
        for i, t in enumerate((t_y, t_far)):
            landed("wout_y", i, wout_rows(t, 0))
            mine = wout_rows(t, 0)
            send_if(jnp.logical_not(at_top), "wout_x", i, mine, mine, (x_up, ti))
            send_if(jnp.logical_not(at_bottom), "wout_x", 2 + i, mine, mine, (x_down, ti))

    def finish_piece(cond, t, k, index):
        @pl.when(cond)
        def _():
            landed("wout_extra", index, wout_cut(t, k, 0, early_rows))
            landed("wout_x", index, wout_cut(t, k, early_rows, piece - early_rows))

        @pl.when(jnp.logical_not(cond))
        def _():
            landed("wout_x", index, wout_rows(t, k))

    def finish_wout():
        load_wout.wait()
        landed("wout_core", 0, wfull.at[at_row(t_core * heads_width, heads_width)])
        for i, t in enumerate((t_y, t_far)):
            landed("wout_y", 2 + i, wout_rows(t, 2))
            for cond, k, index in ((at_top, 3, i), (at_bottom, 1, 2 + i)):
                finish_piece(cond, t, k, index)

    row_head = lax.broadcasted_iota(jnp.int32, (128, 128), 0) >> 6
    col_head = lax.broadcasted_iota(jnp.int32, (128, 128), 1) >> 6
    head_mean = jnp.where(row_head == col_head, 1.0 / 64.0, 0.0).astype(BF16)

    def head_norm(values, gain_row):
        high = values.astype(BF16)
        low = (values - high.astype(F32)).astype(BF16)
        mean = jnp.dot(high, head_mean, preferred_element_type=F32)
        mean = mean + jnp.dot(low, head_mean, preferred_element_type=F32)
        centered = values - mean
        var = jnp.dot((centered * centered).astype(BF16), head_mean, preferred_element_type=F32)
        return (centered * lax.rsqrt(var + EPS) * gain_row).astype(BF16)

    for f in range(2):
        slot0[f, 3:4, :] = jnp.full((1, width), sampler[0, levels[f]], F32)
        slot0[f, 4:5, :] = jnp.full((1, width), sampler[1, levels[f]], F32)
        slot0[f, 5:8, :] = jnp.full((3, width), window_start[f].astype(F32), F32)
    load_mod.wait()
    for f in range(2):
        for j in range(3):
            slot0[f, j : j + 1, :] = mod[j, pl.ds(levels[f], 1), :]
    send_if(not_final, "meta", 0, slot0.at[1], slot1, (up, ti))

    @pl.when(first)
    def _():
        slot1[...] = slot0[0]

    def norm_rows(src, param, start, count):
        chunk = 64
        for i in range(count // chunk):
            at = slice(start + i * chunk, start + (i + 1) * chunk)
            mean = jnp.mean(src[at, :].astype(F32), axis=-1, keepdims=True)
            centered = src[at, :].astype(F32) - mean
            var = jnp.mean(centered * centered, axis=-1, keepdims=True)
            normed = (src[at, :].astype(F32) - mean) * lax.rsqrt(var + EPS)
            h[at, :] = (normed * (1.0 + param[1:2, :]) + param[0:1, :]).astype(BF16)

    def store_kv(kv, p, slot, at, acc):
        kv[slot, at, p * 256 : p * 256 + 128] = head_norm(
            acc[:, :128], gain[1:2, p * 128 : (p + 1) * 128]
        )
        kv[slot, at, p * 256 + 128 : (p + 1) * 256] = acc[:, 128:].astype(BF16)

    def store_q(to, acc):
        for p in range(pairs):
            cols = slice(p * 128, (p + 1) * 128)
            to[:, cols] = head_norm(acc[:, cols], gain[0:1, cols]) * jnp.asarray(0.125, BF16)

    part = frame // 2

    def project(src, params, order, kv, send_halo, ready):
        ready(order[0])
        norm_rows(src, params[order[0] // 2], order[0] * part, part)
        if load_w:
            for load in load_w[: 2 * pairs]:
                load.wait()
        for i, c in enumerate(order):
            if i + 1 < len(order):
                after = order[i + 1]
                ready(after)
                norm_rows(src, params[after // 2], after * part, part)
            f = c // 2
            at = slice((c % 2) * part, (c % 2 + 1) * part)
            acc = jnp.dot(
                h[c * part : (c + 1) * part, :], wkv[...], preferred_element_type=F32
            )
            for p in range(pairs):
                store_kv(kv, p, f + 2, at, acc[:, p * 256 : (p + 1) * 256])
            send_halo(i, f, at)
        if load_w:
            load_w[2 * pairs].wait()
            load_w.clear()
        store_q(q, jnp.dot(h[...], wq[...], preferred_element_type=F32))

    q_chunk = 128
    first_head = lax.broadcasted_iota(jnp.int32, (q_chunk, 128), 1) < 64
    zeros = jnp.zeros((q_chunk, 128), BF16)
    ones = jnp.ones((WIN * frame, 128), BF16)

    def attend(kv, p, f, window, flag, queries, attn):
        fixed, second, if_set, if_clear = window
        lanes = slice(p * 256, (p + 1) * 256)
        k_lanes = slice(p * 256, p * 256 + 128)
        v_lanes = slice(p * 256 + 128, (p + 1) * 256)
        chosen = jnp.where(
            flag, kv[if_set, :, lanes].astype(F32), kv[if_clear, :, lanes].astype(F32)
        ).astype(BF16)
        keys = jnp.concatenate(
            [kv[fixed, :, k_lanes], kv[second, :, k_lanes], chosen[:, :128]], axis=0
        )
        values = jnp.concatenate(
            [kv[fixed, :, v_lanes], kv[second, :, v_lanes], chosen[:, 128:]], axis=0
        )
        values = jnp.concatenate([values, ones], axis=1)

        def scores_of(i):
            start = f * frame + i * q_chunk
            rows_q = queries[start : start + q_chunk, p * 128 : (p + 1) * 128]
            both = jnp.concatenate(
                [jnp.where(first_head, rows_q, zeros), jnp.where(first_head, zeros, rows_q)], axis=0
            )
            return lax.dot_general(
                both, keys, (((1,), (1,)), ((), ())), preferred_element_type=F32
            )

        n = frame // q_chunk
        ahead = scores_of(0)
        for i in range(n):
            scores = ahead
            if i + 1 < n:
                ahead = scores_of(i + 1)
            top = jnp.max(scores, axis=-1, keepdims=True)
            expo = jnp.exp(scores - top).astype(BF16)
            total = jnp.dot(expo, values, preferred_element_type=F32)
            picked = jnp.where(
                jnp.concatenate([first_head, first_head], axis=1), total[:q_chunk], total[q_chunk:]
            )
            start = f * frame + i * q_chunk
            attn[start : start + q_chunk, at_lane(ti * heads_width + p * 128, 128)] = (
                picked[:, :128] / picked[:, 128:]
            ).astype(BF16)

    def attn_block(attn, t, p, f):
        return attn.at[f * frame : (f + 1) * frame, at_lane(t * heads_width + p * 128, 128)]

    def attn_slot(step, p, f):
        return step * 6 + p * 2 + f

    def share_attn(step, attn, p, f):
        mine = attn_block(attn, ti, p, f)
        send("attn_y", attn_slot(step, p, f), mine, mine, (qi, t_y))
        send("attn_core", attn_slot(step, p, f), mine, mine, (qi, t_core))

    def forward_attn(step, attn, p, f):
        block = attn_block(attn, t_y, p, f)
        landed("attn_y", attn_slot(step, p, f), block)
        send("attn_fwd", attn_slot(step, p, f), block, block, (qi, t_core))

    def finish_attn(step, attn, f):
        for p in range(pairs):
            landed("attn_core", attn_slot(step, p, f), attn_block(attn, t_core, p, f))
            landed("attn_fwd", attn_slot(step, p, f), attn_block(attn, t_far, p, f))

    def update(values, branch, param, columns):
        values = values.astype(F32)
        noise_pred = values + param[2:3, columns] * branch
        return (param[3:4, columns] * values + param[4:5, columns] * noise_pred).astype(BF16)

    param0 = (slot0.at[0], slot0.at[1])
    param1 = (slot1, slot0.at[0])
    window0 = (
        (2, jnp.where(first, 4, 1), 3, 0),
        (3, jnp.where(final, 1, 4), 5, 2),
    )
    window1 = ((2, 3, 4, 1), (3, 2, 4, 1))

    def starts_from(param, slot):
        start = jnp.concatenate([param[5:6, 0:128]] * 2, axis=1)
        return start >= slot.astype(F32)

    def cut(kv, slots_of, at, p):
        lanes = slice(0, 2 * heads_width) if p is None else slice(p * 256, (p + 1) * 256)
        return kv.at[slots_of, at, lanes]

    def send_halo0(i, f, at):
        full = slice(0, frame)
        jobs = [(0, f, at, None)] if i == 0 else [(i, f, at, 0)]
        if i == 3:
            for p in range(1, pairs):
                jobs += [(2 * p + 2, 0, half_of(1), p), (2 * p + 3, 1, full, p)]
        for index, g, rows_at, p in jobs:
            own = cut(kv0, g + 2, rows_at, p)
            send_if(not_final, "halo_up", index, own, cut(kv0, g, rows_at, p), (up, ti))
            send_if(not_first, "halo_down", index, own, cut(kv0, g + 4, rows_at, p), (down, ti))

    def half_of(c):
        return slice((c % 2) * part, (c % 2 + 1) * part)

    def land_halo0(p):
        def land(name, base):
            if p == 0:
                landed(name, 0, cut(kv0, base, half_of(0), None))
                for c in (1, 2, 3):
                    landed(name, c, cut(kv0, base + c // 2, half_of(c), 0))
            else:
                landed(name, 2 * p + 2, cut(kv0, base, half_of(1), p))
                landed(name, 2 * p + 3, cut(kv0, base + 1, slice(0, frame), p))

        pl.when(not_first)(lambda: land("halo_up", 0))
        pl.when(not_final)(lambda: land("halo_down", 4))

    project(x0, param0, (0, 1, 2, 3), kv0, send_halo0, lambda c: load_x[c].wait())

    @pl.when(final)
    def _():
        load_f.wait()
        norm_rows(xf, slot0.at[1], 0, frame)
        entering = jnp.dot(h[0:frame, :], wkv[...], preferred_element_type=F32)
        for p in range(pairs):
            store_kv(kv1, p, 4, slice(0, frame), entering[:, p * 256 : (p + 1) * 256])
        store_q(qf, jnp.dot(h[0:frame, :], wq[...], preferred_element_type=F32))

    lag = 2
    done = []
    for p in range(pairs):
        if p == 1:
            forward_wout()
        land_halo0(p)
        if p == pairs - 1:
            forward_wout_late()
        for f in range(2):
            attend(kv0, p, f, window0[f], starts_from(param0[f], 2 * qi - 1 + 2 * f), q, attn0)
            share_attn(0, attn0, p, f)
            done.append((p, f))
            if len(done) > lag:
                forward_attn(0, attn0, *done[-1 - lag])
    finish_wout()
    waiting = done[-lag:]
    n_cols = 256

    def x1_rows(c, columns):
        return x1.at[c * part : (c + 1) * part, columns]

    order1 = (0, 2, 1, 3)
    for i, c in enumerate(order1):
        if i < 2:
            forward_attn(0, attn0, *waiting[i])
            finish_attn(0, attn0, i)
        at = slice(c * part, (c + 1) * part)
        branch = jnp.dot(attn0[at, :], wfull[...], preferred_element_type=F32)
        x1[at, my_half] = update(x0[at, my_half], branch, param0[c // 2], my_half)
        send("gather", c, x1_rows(c, my_half), x1_rows(c, my_half), (qi, t_core))
    @pl.when(not_first)
    def _():
        landed("meta", 0, slot1)


    def send_halo1(i, f, at):
        last_one = i >= 2
        for p in range(pairs) if last_one else [None]:
            index = 8 + (0 if p is None else p + 1)
            own = cut(kv1, f + 2, at, p)
            if f == 1:
                send_if(not_final, "halo_up", index, own, cut(kv1, 1, at, p), (up, ti))
            else:
                send_if(not_first, "halo_down", index, own, cut(kv1, 4, at, p), (down, ti))

    def land_halo1(p):
        def land(name, slot):
            if p == 0:
                landed(name, 8, cut(kv1, slot, half_of(0), None))
            landed(name, 9 + p, cut(kv1, slot, half_of(1), p))

        pl.when(not_first)(lambda: land("halo_up", 1))
        pl.when(not_final)(lambda: land("halo_down", 4))

    project(
        x1, param1, order1, kv1, send_halo1,
        lambda c: landed("gather", c, x1_rows(c, other_half)),
    )
    def entering_copies(p):
        mine = attn_block(attnf, ti, p, 0)
        theirs = attn_block(attnf, t_y, p, 0)
        return (
            rcopy("attn_y", 12 + p, mine, mine, (qi, t_y)),
            rcopy("attn_core", 12 + p, mine, mine, (qi, t_core)),
            rcopy("attn_fwd", 12 + p, theirs, theirs, (qi, t_core)),
        )

    @pl.when(final)
    def _():
        for p in range(pairs):
            attend(kv1, p, 0, (2, 3, 4, 4), starts_from(slot0.at[1], 2 * qi), qf, attnf)
            for copy in entering_copies(p)[:2]:
                copy.start()

    done = []
    for f in range(2):
        for p in range(pairs):
            if f == 0:
                land_halo1(p)
            attend(kv1, p, f, window1[f], starts_from(param1[f], 2 * qi - 1), q, attn1)
            share_attn(1, attn1, p, f)
            done.append((p, f))
            if len(done) > lag:
                forward_attn(1, attn1, *done[-1 - lag])

    chunks = 12
    n_rows = rows // chunks
    my_quarter = core * half + chip * quarter
    y_quarter = core * half + (1 - chip) * quarter

    def out_part(j, start):
        return out.at[at_row(j * n_rows, n_rows), at_lane(start, quarter)]

    def piece_of(ref, j):
        return ref.at[j * n_rows : (j + 1) * n_rows]

    def project_out(attn, values, param, f, to):
        at = slice(f * frame, (f + 1) * frame)

        @pl.loop(0, quarter // n_cols)
        def _(n):
            columns = at_lane(my_quarter + n * n_cols, n_cols)
            inner = at_lane(n * n_cols, n_cols)
            weight = wfull[:, at_lane(chip * quarter + n * n_cols, n_cols)]
            branch = jnp.dot(attn[at, :], weight, preferred_element_type=F32)
            to[at, inner] = update(values[at, columns], branch, param, columns)

    by_last = (3, 4, 5, 9, 10, 11)
    by_first = (2, 8)

    for f in range(2):
        if f == 1:
            for piece in done[-lag:]:
                forward_attn(1, attn1, *piece)
        finish_attn(1, attn1, f)
        project_out(attn1, x1, param1[f], f, xs)
        for j in range(f * chunks // 2, (f + 1) * chunks // 2):
            direct = not_first
            if j in by_last + by_first:
                direct = jnp.logical_and(not_first, jnp.logical_not(middle))
                by = mirror if j in by_last else across
                send_if(middle, "relay", j, piece_of(xs, j), piece_of(relay, j), (by, ti))
            send_if(direct, "shift", j, piece_of(xs, j), out_part(j, my_quarter), (down, ti))

    def relayed(j):
        to = across if j in by_last else mirror
        return rcopy("relayed", j, piece_of(relay, j), out_part(j, my_quarter), (to, ti), "shift")

    def pass_relay(j):
        landed("relay", j, piece_of(relay, j))
        relayed(j).start()

    @pl.when(final)
    def _():
        for p in range(pairs):
            landed("attn_y", 12 + p, attn_block(attnf, t_y, p, 0))
            entering_copies(p)[2].start()
        for p in range(pairs):
            landed("attn_core", 12 + p, attn_block(attnf, t_core, p, 0))
            landed("attn_fwd", 12 + p, attn_block(attnf, t_far, p, 0))
        project_out(attnf, xf, slot0.at[1], 0, xsf)
        stays = local(0, xsf, out.at[0:frame, at_lane(my_quarter, quarter)])
        stays.start()
        stays.wait()
        for p in range(pairs):
            for copy in entering_copies(p):
                copy.wait_send()

    def guarded(f, action):
        if f == 0:
            action()
        else:
            pl.when(not_final)(action)

    def spread(j):
        part = out_part(j, my_quarter)
        rcopy("out_y", j, part, part, (qi, t_y)).start()
        rcopy("out_core", j, part, part, (qi, t_core)).start()

    def pass_on(j):
        part = out_part(j, y_quarter)
        landed("out_y", j, part)
        rcopy("out_fwd", j, part, part, (qi, t_core)).start()

    behind = 3

    @pl.when(final)
    def _():
        for j in by_last[:3]:
            pass_relay(j)
        for j in range(chunks // 4):
            spread(j)
        for j in by_last[3:]:
            pass_relay(j)
        for j in range(chunks // 4, chunks // 2):
            spread(j)
        for j in range(chunks // 2):
            pass_on(j)

    @pl.when(not_final)
    def _():
        for j in range(chunks):
            for k in {0: by_first[:1], 4: by_first[1:]}.get(j, ()):
                pl.when(first)(functools.partial(pass_relay, k))
            landed("shift", j, out_part(j, my_quarter))
            spread(j)
            if j >= behind:
                pass_on(j - behind)
        for j in range(chunks - behind, chunks):
            pass_on(j)

    core_quarter = (1 - core) * half + chip * quarter
    far_quarter = (1 - core) * half + (1 - chip) * quarter
    for j in range(chunks):

        def action():
            landed("out_core", j, out_part(j, core_quarter))
            landed("out_fwd", j, out_part(j, far_quarter))
            mine = out_part(j, my_quarter)
            rcopy("out_y", j, mine, mine, (qi, t_y)).wait_send()
            rcopy("out_core", j, mine, mine, (qi, t_core)).wait_send()
            passed = out_part(j, y_quarter)
            rcopy("out_fwd", j, passed, passed, (qi, t_core)).wait_send()

        guarded(j // (chunks // 2), action)

    @pl.when(final)
    def _():
        last.wait()
        for j in by_last:
            relayed(j).wait_send()

    @pl.when(first)
    def _():
        for j in by_first:
            relayed(j).wait_send()

    for cond, copy in sends:
        if cond is None:
            copy.wait_send()
        else:
            pl.when(cond)(copy.wait_send)


def hand_out(n_parts, src, dst, held, in_sem, out_sem):
    rows = src.shape[0] // n_parts
    pieces = [pl.ds(i * rows, rows) for i in range(n_parts)]
    reads = [
        pltpu.make_async_copy(src.at[at], held.at[at], in_sem.at[i]) for i, at in enumerate(pieces)
    ]
    writes = [
        pltpu.make_async_copy(held.at[at], dst.at[at], out_sem.at[i]) for i, at in enumerate(pieces)
    ]
    for read in reads:
        read.start()
    for read, write in zip(reads, writes):
        read.wait()
        write.start()
    for write in writes:
        write.wait()


def body(
    queue_latents, fresh_noise, levels, window_start, modulation, w_qkv, qk_gain, w_out, sampler
):
    frames, frame, width = queue_latents.shape
    rows = frames * frame
    heads_width = w_out.shape[0]
    level_count = modulation.shape[0]
    any_space = pl.BlockSpec(memory_space=pl.ANY)
    smem = pl.BlockSpec(memory_space=pltpu.SMEM)
    vmem = pl.BlockSpec(memory_space=pltpu.VMEM)
    kv = pltpu.VMEM((6, frame, 2 * heads_width), BF16)
    moved = pl.pallas_call(
        functools.partial(kernel, frame, width, heads_width),
        name="diagonal_steps",
        out_shape=jax.ShapeDtypeStruct((rows, width), BF16),
        in_specs=[any_space, any_space, smem, smem, any_space, any_space, vmem, any_space, smem],
        out_specs=any_space,
        scratch_shapes=[
            pltpu.VMEM((rows, width), BF16),
            pltpu.VMEM((rows, width), BF16),
            pltpu.VMEM((rows, width), BF16),
            pltpu.VMEM((width, 2 * heads_width), BF16),
            pltpu.VMEM((width, heads_width), BF16),
            pltpu.VMEM((4 * heads_width, width // 2), BF16),
            pltpu.VMEM((rows, heads_width), BF16),
            pltpu.VMEM((rows, 4 * heads_width), BF16),
            pltpu.VMEM((rows, 4 * heads_width), BF16),
            kv, kv,
            pltpu.VMEM((rows, width // 4), BF16),
            pltpu.VMEM((frame, width), BF16),
            pltpu.VMEM((frame, heads_width), BF16),
            pltpu.VMEM((frame, 4 * heads_width), BF16),
            pltpu.VMEM((frame, width // 4), BF16),
            pltpu.VMEM((rows, width // 4), BF16),
            pltpu.VMEM((3, level_count, width), F32),
            pltpu.VMEM((2, 8, width), F32),
            pltpu.VMEM((8, width), F32),
            pltpu.SemaphoreType.DMA((15,)),
            pltpu.SemaphoreType.DMA((N_SEM,)),
            pltpu.SemaphoreType.DMA((N_SEM,)),
        ],
        compiler_params=pltpu.CompilerParams(
            collective_id=0, has_side_effects=True, vmem_limit_bytes=60 * 1024 * 1024
        ),
        cost_estimate=pl.CostEstimate(
            flops=4 * rows * width * 1536 * 2, bytes_accessed=40 * 2**20, transcendentals=10**7
        ),
    )(
        queue_latents.reshape(rows, width),
        fresh_noise,
        levels,
        window_start,
        jnp.transpose(modulation, (1, 0, 2)),
        jnp.transpose(w_qkv, (1, 0, 2)),
        qk_gain,
        w_out,
        jnp.transpose(sampler, (1, 0)),
    )
    n_parts = 4
    result = pl.pallas_call(
        functools.partial(hand_out, n_parts),
        name="hand_out",
        out_shape=jax.ShapeDtypeStruct((rows, width), BF16),
        in_specs=[any_space],
        out_specs=any_space,
        scratch_shapes=[
            pltpu.VMEM((rows, width), BF16),
            pltpu.SemaphoreType.DMA((n_parts,)),
            pltpu.SemaphoreType.DMA((n_parts,)),
        ],
        compiler_params=pltpu.CompilerParams(vmem_limit_bytes=60 * 1024 * 1024),
        cost_estimate=pl.CostEstimate(
            flops=0, bytes_accessed=4 * rows * width, transcendentals=0
        ),
    )(moved)
    return result.reshape(frames, frame, width)


def solution(mesh):
    in_specs = (
        P("queue", None, None),
        P(),
        P("queue"),
        P("queue"),
        P(),
        P(None, None, "tensor"),
        P(None, "tensor"),
        P("tensor", None),
        P(),
    )
    out_specs = P("queue", None, None)
    return jax.shard_map(body, mesh=mesh, in_specs=in_specs, out_specs=out_specs, check_vma=False)
```
